32 devices in a mesh: seq: 16 (over z, y, x), head: 2 (over core).
Axes of the slice: x: 2, y: 2, z: 4, core: 2. Of those that a mesh axis runs over, the one named last changes fastest.
Arguments:
- tokens: bfloat16 [16384, 768], P('seq'), may hold values from -6 to 6
- out_grad: bfloat16 [16384, 768], P('seq'), may hold values from -6 to 6
- doc_lengths: int32 [15], replicated, may hold values from 1 to 2048, as said below
- cluster_perm: int32 [16384], P('seq'), may hold values from 0 to 2047, as said below
- query_weight: bfloat16 [768, 768], P(None, 'head'), may hold values from -0.21875 to 0.21875
- query_bias: float32 [768], P('head'), may hold values from -3 to 3
- key_weight: bfloat16 [768, 768], P(None, 'head'), may hold values from -0.21875 to 0.21875
- value_weight: bfloat16 [768, 768], P(None, 'head'), may hold values from -0.21875 to 0.21875
- value_bias: float32 [768], P('head'), may hold values from -3 to 3
- output_weight: bfloat16 [768, 768], P('head'), may hold values from -0.875 to 0.875
- output_bias: float32 [768], replicated, may hold values from -3 to 3
- first_gain: float32 [768], replicated, may hold values from 0.1 to 1.9
- first_shift: float32 [768], replicated, may hold values from -3 to 3
- up_weight: bfloat16 [768, 3072], P(None, 'head'), may hold values from -0.21875 to 0.21875
- up_bias: float32 [3072], P('head'), may hold values from -3 to 3
- down_weight: bfloat16 [3072, 768], P('head'), may hold values from -0.109375 to 0.109375
- down_bias: float32 [768], replicated, may hold values from -3 to 3
- second_gain: float32 [768], replicated, may hold values from 0.1 to 1.9
- second_shift: float32 [768], replicated, may hold values from -3 to 3
Outputs:
- layer_out: float32 [16384, 768], P('seq')
- input_grad: float32 [16384, 768], P('seq')
- query_weight_grad: float32 [768, 768], P('seq', 'head')
- query_bias_grad: float32 [768], P('head')
- key_weight_grad: float32 [768, 768], P('seq', 'head')
- value_weight_grad: float32 [768, 768], P('seq', 'head')
- value_bias_grad: float32 [768], P('head')
- output_weight_grad: float32 [768, 768], P('head', 'seq')
- output_bias_grad: float32 [768], P('seq')
- first_gain_grad: float32 [768], P('seq')
- first_shift_grad: float32 [768], P('seq')
- up_weight_grad: float32 [768, 3072], P('seq', 'head')
- up_bias_grad: float32 [3072], P('head')
- down_weight_grad: float32 [3072, 768], P('head', 'seq')
- down_bias_grad: float32 [768], P('seq')
- second_gain_grad: float32 [768], P('seq')
- second_shift_grad: float32 [768], P('seq')
The draws below stay inside these ranges and needn't reach their ends.
Inputs may be any that keep to these rules, and one draw needn't show every extreme that they name: `doc_lengths`: document i occupies its length rounded up to a multiple of 128 positions; the documents lie end to end from position 0 and fill all 16384 positions; positions past a length in its last cluster are padding. `cluster_perm`: within each document of padded length P, the values at its positions are a permutation of 0 to P - 1.
All inputs are finite; a program needn't handle non-finite values.
Results may differ from the reference program's by a relative error of at most 0.014.
The reference program's roundings to bfloat16 on the way count: a program that leaves them out, or rounds other values in their place, can miss the bound.
Values may be sent and summed in bfloat16 or wider, within the bound.
A program may use at most 128 MiB of HBM per device.

```python
import math
from functools import partial
import jax
import jax.numpy as jnp
from jax import lax

D = 768
HEADS = 12
HEAD_DIM = 64
FF = 3072
CLUSTER = 128
TOKENS = 16384
BLOCKS = 128
MAXB = 16
NDOC = 15


def doc_layout(key):
    front_blocks = BLOCKS - MAXB - 1
    pair_count = front_blocks // (MAXB + 1)
    remainder = front_blocks - pair_count * (MAXB + 1)
    front_docs = 2 * pair_count + 1
    per_device = MAXB // 2
    key_leading = jax.random.fold_in(key, 101)
    key_padding = jax.random.fold_in(key, 102)
    key_order = jax.random.fold_in(key, 103)
    leading = jax.random.randint(key_leading, (pair_count,), 1, MAXB + 1).astype(jnp.int32)
    leading = leading.at[0].set(1)
    second = (MAXB + 1 - leading).astype(jnp.int32)
    front = jnp.concatenate([leading, second, jnp.full((1,), remainder, jnp.int32)])
    padding = jax.random.randint(key_padding, (NDOC,), 0, CLUSTER).astype(jnp.int32)
    padding = padding.at[pair_count].set(0)
    doc_order = jax.random.permutation(key_order, front_docs)
    tail = jnp.array([per_device + 2, per_device - 1], jnp.int32)
    blocks = jnp.concatenate([front[doc_order], tail])
    padding = jnp.concatenate([padding[:front_docs][doc_order], padding[front_docs:]])
    return (blocks, padding)


def draw_doc_lengths(key, part):
    blocks, padding = doc_layout(key)
    return (blocks * CLUSTER - padding).astype(jnp.int32)


def draw_cluster_perm(key, part):
    blocks, padding = doc_layout(key)
    key = jax.random.fold_in(key, 2)
    padded = (blocks * CLUSTER).astype(jnp.int32)
    doc_ids = jnp.repeat(jnp.arange(NDOC, dtype=jnp.int32), padded, total_repeat_length=TOKENS)
    starts = (jnp.cumsum(padded) - padded).astype(jnp.int32)
    ranking = jax.random.permutation(key, TOKENS).astype(jnp.int32)
    doc_order = jnp.argsort(doc_ids * TOKENS + ranking, stable=True).astype(jnp.int32)
    return (doc_order - starts[doc_ids]).astype(jnp.int32)


def spiked(values, rng, source, target, parts, factor):
    owner, partner = [(jnp.arange(values.shape[axis_at]) // (values.shape[axis_at] // parts)).reshape([-1 if axis == axis_at else 1 for axis in range(values.ndim)]) for axis_at in (source, target)]
    chosen = jax.random.permutation(rng, parts)[partner]
    strong = (owner == chosen) | (owner == (partner + parts // 2) % parts)
    return jnp.where(strong, factor * values, values)


def steps_of(stream_key, dims, split, smallest, high):
    level = 1.0
    for axis_at, blocks in split:
        heights = jax.random.uniform(jax.random.fold_in(jax.random.fold_in(stream_key, 6), axis_at), (blocks,), jnp.float32, smallest / len(split), high / len(split))
        level = level * jnp.repeat(jnp.exp(heights), dims[axis_at] // blocks).reshape((-1,) + (1,) * (len(dims) - 1 - axis_at))
    return level


def normal_values(own_key, shape, spread, reach, pieces=(), kind=jnp.bfloat16):
    loudness = steps_of(own_key, shape, pieces, -0.22, 0.18) if pieces else 1.0
    entries = jax.random.normal(own_key, shape, jnp.float32) * spread * loudness
    return jnp.minimum(jnp.maximum(entries, -reach), reach).astype(kind)


def gaussian_with(own_key, extent, spread, limit, split, heavy, kind=jnp.bfloat16):
    drawn = spread * jax.random.normal(own_key, extent, jnp.float32)
    if split:
        drawn = drawn * steps_of(own_key, extent, split, -0.22, 0.18)
    return jnp.clip(spiked(drawn, jax.random.fold_in(own_key, 3), *heavy), -limit, limit).astype(kind)


def setup_inputs(seed: int = 0) -> dict:
    arg_keys = jax.random.split(jax.random.key(seed), 20)
    tokens = gaussian_with(arg_keys[0], (TOKENS, D), 1.0, 6.0, ((0, 16),), (0, 1, 16, 2.0))
    out_grad = gaussian_with(arg_keys[1], (TOKENS, D), 1.0, 6.0, ((0, 16),), (0, 1, 16, 2.0))
    doc_lengths = draw_doc_lengths(jax.random.fold_in(arg_keys[19], 71), 0)
    cluster_perm = draw_cluster_perm(jax.random.fold_in(arg_keys[19], 71), 0)
    query_weight = normal_values(arg_keys[4], (D, D), D ** -0.5, 0.21875, ((1, 2),))
    query_bias = normal_values(arg_keys[5], (D,), 0.5, 3.0, ((0, 2),), jnp.float32)
    key_weight = normal_values(arg_keys[6], (D, D), D ** -0.5, 0.21875, ((1, 2),))
    value_weight = normal_values(arg_keys[7], (D, D), D ** -0.5, 0.21875, ((1, 2),))
    value_bias = normal_values(arg_keys[8], (D,), 0.5, 3.0, ((0, 2),), jnp.float32)
    output_weight = normal_values(arg_keys[9], (D, D), (D // 16) ** -0.5, 0.875, ((0, 2),))
    output_bias = normal_values(arg_keys[10], (D,), 0.5, 3.0, (), jnp.float32)
    first_gain = jnp.clip(1.0 + 0.18 * jax.random.normal(arg_keys[11], (D,), jnp.float32), 0.1, 1.9)
    first_shift = normal_values(arg_keys[12], (D,), 0.5, 3.0, (), jnp.float32)
    up_weight = normal_values(arg_keys[13], (D, FF), D ** -0.5, 0.21875, ((1, 2),))
    up_bias = normal_values(arg_keys[14], (FF,), 0.5, 3.0, ((0, 2),), jnp.float32)
    down_weight = normal_values(arg_keys[15], (FF, D), FF ** -0.5, 0.109375, ((0, 2),))
    down_bias = normal_values(arg_keys[16], (D,), 0.5, 3.0, (), jnp.float32)
    second_gain = jnp.clip(1.0 + 0.18 * jax.random.normal(arg_keys[17], (D,), jnp.float32), 0.1, 1.9)
    second_shift = normal_values(arg_keys[18], (D,), 0.5, 3.0, (), jnp.float32)
    return dict(tokens=tokens, out_grad=out_grad, doc_lengths=doc_lengths, cluster_perm=cluster_perm, query_weight=query_weight, query_bias=query_bias, key_weight=key_weight, value_weight=value_weight, value_bias=value_bias, output_weight=output_weight, output_bias=output_bias, first_gain=first_gain, first_shift=first_shift, up_weight=up_weight, up_bias=up_bias, down_weight=down_weight, down_bias=down_bias, second_gain=second_gain, second_shift=second_shift)


norm_eps = 1e-12
masked_score = -1e+30

@jax.custom_vjp
def low(v):
    return lax.optimization_barrier(v.astype(jnp.bfloat16)).astype(jnp.float32)

@jax.custom_vjp
def low_back(v):
    return v

def low_keep(v):
    return (low(v), None)

def low_pass(kept, grad):
    return (grad,)

def back_keep(v):
    return (v, None)

def back_low(kept, grad):
    return (low(grad),)
low.defvjp(low_keep, low_pass)
low_back.defvjp(back_keep, back_low)

def rounded_both(values):
    return low(low_back(values))

def product(left, right):
    return jnp.dot(left, right, precision=lax.Precision.HIGHEST)

def norm_rows(values, gain, shift):
    row_mean = lax.optimization_barrier(jnp.mean(values, axis=-1, keepdims=True))
    centered = values - row_mean
    variance = lax.optimization_barrier(jnp.mean(centered * centered, axis=-1, keepdims=True))
    return centered * lax.rsqrt(variance + norm_eps) * gain + shift

def slot_sources(doc_lengths, cluster_perm):
    padded = (doc_lengths + CLUSTER - 1) // CLUSTER * CLUSTER
    starts = (jnp.cumsum(padded) - padded).astype(jnp.int32)
    positions = jnp.arange(TOKENS, dtype=jnp.int32)
    doc_of = (lax.optimization_barrier(jnp.sum((starts[None, :] <= positions[:, None]).astype(jnp.int32), axis=1)) - 1).astype(jnp.int32)
    source = (starts[doc_of] + cluster_perm).astype(jnp.int32)
    key_valid = cluster_perm < doc_lengths[doc_of]
    return (source, key_valid)

def cluster_attend(members):
    query_blk, key_blk, value_blk, valid_blk = members
    groups = query_blk.shape[0]
    head_shape = (groups, CLUSTER, HEADS, HEAD_DIM)
    scores = jnp.einsum('gqhd,gkhd->ghqk', query_blk.reshape(head_shape), key_blk.reshape(head_shape), precision=lax.Precision.HIGHEST) * HEAD_DIM ** (-0.5)
    scores = low_back(scores)
    scores = jnp.where(valid_blk[:, None, None, :], scores, masked_score)
    row_max = lax.optimization_barrier(jnp.max(scores, axis=-1, keepdims=True))
    raw_weight = jnp.exp(scores - row_max)
    attn_prob = raw_weight / lax.optimization_barrier(jnp.sum(raw_weight, axis=-1, keepdims=True))
    context = jnp.einsum('ghqk,gkhd->gqhd', low(attn_prob), value_blk.reshape(head_shape), precision=lax.Precision.HIGHEST)
    return context.reshape(groups, CLUSTER, HEADS * HEAD_DIM)

def forward(source, key_valid, tokens, query_weight, query_bias, key_weight, value_weight, value_bias, output_weight, output_bias, first_gain, first_shift, up_weight, up_bias, down_weight, down_bias, second_gain, second_shift):
    query_rows = rounded_both(product(tokens, query_weight) + query_bias)
    key_rows = rounded_both(product(tokens, key_weight))
    value_rows = rounded_both(product(tokens, value_weight) + value_bias)
    per_group = math.gcd(BLOCKS, 32)
    group_count = BLOCKS // per_group

    def gather_slots(rows):
        return rows[source].reshape(group_count, per_group, CLUSTER, D)
    valid_slots = key_valid.reshape(group_count, per_group, CLUSTER)
    context = lax.map(jax.checkpoint(cluster_attend), (gather_slots(query_rows), gather_slots(key_rows), gather_slots(value_rows), valid_slots))
    context = rounded_both(context.reshape(TOKENS, D))
    context_home = jnp.zeros_like(context).at[source].set(context)
    attn_out = low_back(product(context_home, output_weight))
    hidden = tokens + attn_out + output_bias
    per_rows = math.gcd(TOKENS, 4096)

    def post_attention(hidden_blk):
        first_norm = norm_rows(hidden_blk, first_gain, first_shift)
        pre_act = low_back(product(low(first_norm), up_weight) + up_bias)
        activation = low(jax.nn.gelu(pre_act, approximate=False))
        ffn_out = low_back(product(activation, down_weight))
        return norm_rows(first_norm + ffn_out + down_bias, second_gain, second_shift)
    layer_out = lax.map(jax.checkpoint(post_attention), hidden.reshape(TOKENS // per_rows, per_rows, D))
    return layer_out.reshape(TOKENS, D)

def reference(tokens, out_grad, doc_lengths, cluster_perm, query_weight, query_bias, key_weight, value_weight, value_bias, output_weight, output_bias, first_gain, first_shift, up_weight, up_bias, down_weight, down_bias, second_gain, second_shift):
    source, key_valid = slot_sources(doc_lengths, cluster_perm)
    floats = tuple((array_in.astype(jnp.float32) for array_in in (tokens, query_weight, query_bias, key_weight, value_weight, value_bias, output_weight, output_bias, first_gain, first_shift, up_weight, up_bias, down_weight, down_bias, second_gain, second_shift)))
    layer_out, pullback = jax.vjp(partial(forward, source, key_valid), *floats)
    gradients = pullback(out_grad.astype(jnp.float32))
    return (layer_out, gradients[0], gradients[1], gradients[2], gradients[3], gradients[4], gradients[5], gradients[6], gradients[7], gradients[8], gradients[9], gradients[10], gradients[11], gradients[12], gradients[13], gradients[14], gradients[15])
```

```python
import functools

import jax
import jax.numpy as jnp
from jax import lax
from jax.experimental import pallas as pl
from jax.experimental.pallas import tpu as pltpu
from jax.sharding import PartitionSpec as P

MESH = pl.DeviceIdType.MESH
HEAD_DIM = 64
CLUSTER = 128
OFFSETS = (0, 1, -1, 2, -2)
SLOT = {offset: slot for slot, offset in enumerate(OFFSETS)}
MEBI = 1 << 20

norm_eps = 1e-12
masked_score = -1e30
root_half = 0.7071067811865476
inv_root_tau = 0.3989422804014327
score_scale = HEAD_DIM ** (-0.5)

F32 = jnp.float32
BF16 = jnp.bfloat16


def doc_lookup(doc_lengths, positions):
    padded = (doc_lengths + CLUSTER - 1) // CLUSTER * CLUSTER
    starts = jnp.cumsum(padded) - padded
    doc_of = jnp.sum((starts[None, :] <= positions[:, None]).astype(jnp.int32), axis=1) - 1
    picked = jnp.arange(starts.shape[0], dtype=jnp.int32)[None, :] == doc_of[:, None]
    slot_start = jnp.sum(jnp.where(picked, starts[None, :], 0), axis=1)
    slot_length = jnp.sum(jnp.where(picked, doc_lengths[None, :], 0), axis=1)
    return (slot_start, slot_length)


def remote(src, dst, send, recv, device):
    return pltpu.make_async_remote_copy(
        src_ref=src, dst_ref=dst, send_sem=send, recv_sem=recv, device_id=device, device_id_type=MESH
    )


def greet(devices):
    barrier = pltpu.get_barrier_semaphore()
    count = 0
    for device, valid in devices:
        def hello(device=device):
            pl.semaphore_signal(barrier, inc=1, device_id=device, device_id_type=MESH)

        if valid is None:
            hello()
            count = count + 1
        else:
            pl.when(valid)(hello)
            count = count + valid.astype(jnp.int32)
    pl.semaphore_wait(barrier, count)


def near(seq, core, blocks):
    out = {}
    for offset in OFFSETS[1:]:
        there = seq + offset
        out[offset] = ((there, core), (there >= 0) & (there < blocks))
    return out


def inner(left, right):
    return lax.dot_general(left, right, (((1,), (0,)), ((), ())), preferred_element_type=F32)


def outer(left, right):
    return lax.dot_general(left, right, (((1,), (1,)), ((), ())), preferred_element_type=F32)


def under(left, right):
    return lax.dot_general(left, right, (((0,), (0,)), ((), ())), preferred_element_type=F32)


def entry_kernel(
    blocks,
    tokens,
    out_grad,
    rel,
    source,
    wq,
    wk,
    wv,
    wo,
    wu,
    wd,
    bq,
    bv,
    bu,
    slot_tokens,
    slot_grad,
    sources,
    wqkv_full,
    wo_full,
    wu_full,
    wd_full,
    bqkv_full,
    bu_full,
    window,
    total,
    picked,
    source_win,
    wsend,
    wrecv,
    wlocal,
    send,
    recv,
    local,
    ssend,
    srecv,
    psend,
    precv,
    plocal,
):
    seq, core = lax.axis_index("seq"), lax.axis_index("head")
    rows, width = window.shape[2], window.shape[3]
    half = rows // 2
    partner = (seq, 1 - core)
    others = near(seq, core, blocks)
    greet([(partner, None)] + [others[offset] for offset in OFFSETS[1:]])

    mine = pl.ds(pl.multiple_of(core * width, width), width)
    arrays = (tokens, out_grad)
    locals_ = []
    for which, array in enumerate(arrays):
        for offset in OFFSETS[1:]:
            device, valid = others[offset]
            slot = SLOT[-offset]
            copy = remote(
                array.at[:, mine], window.at[which, slot], send.at[which, slot], recv.at[which, slot], device
            )
            pl.when(valid)(copy.start)
            if which == 0:
                tiny = remote(source, source_win.at[slot], ssend.at[slot], srecv.at[slot], device)
                pl.when(valid)(tiny.start)
        own = pltpu.make_async_copy(array.at[:, mine], window.at[which, 0], local.at[which])
        own.start()
        locals_.append(own)

    wide, deep = wq.shape[1], wd.shape[0]
    model = wq.shape[0]
    at_core = pl.multiple_of(core * wide, wide)
    at_deep = pl.multiple_of(core * deep, deep)
    pieces = []
    for i, array in enumerate((wq, wk, wv)):
        at = pl.multiple_of(i * model + core * wide, wide)
        pieces.append((array, wqkv_full.at[:, pl.ds(at, wide)]))
    pieces.append((wo, wo_full.at[pl.ds(at_core, wide), :]))
    pieces.append((wu, wu_full.at[:, pl.ds(at_deep, deep)]))
    pieces.append((wd, wd_full.at[pl.ds(at_deep, deep), :]))
    pieces.append((bq, bqkv_full.at[:, pl.ds(at_core, wide)]))
    pieces.append((bv, bqkv_full.at[:, pl.ds(pl.multiple_of(2 * model + core * wide, wide), wide)]))
    pieces.append((bu, bu_full.at[:, pl.ds(at_deep, deep)]))
    moves = []
    for i, (array, place) in enumerate(pieces):
        there = remote(array, place, wsend.at[i], wrecv.at[i], partner)
        here = pltpu.make_async_copy(array, place, wlocal.at[i])
        there.start()
        here.start()
        moves.append((there, here))

    source_win[0] = source[...]
    for offset in OFFSETS[1:]:

        def blank(slot=SLOT[offset]):
            source_win[slot] = jnp.full(source.shape, -1, jnp.int32)

        pl.when(jnp.logical_not(others[offset][1]))(blank)
    tile = 256
    outs = (slot_tokens, slot_grad)
    finals = []
    for which in range(2):
        locals_[which].wait()
        for offset in OFFSETS:
            slot = SLOT[offset]

            def add(which=which, offset=offset, slot=slot):
                if offset != 0:
                    device, _ = others[offset]
                    remote(
                        arrays[which].at[:, mine],
                        window.at[which, slot],
                        send.at[which, slot],
                        recv.at[which, slot],
                        device,
                    ).wait_recv()

                @pl.loop(0, rows // tile)
                def _(step):
                    at = pl.ds(pl.multiple_of(step * tile, tile), tile)
                    wanted = rel[at, :] - offset * rows
                    lanes = lax.broadcasted_iota(jnp.int32, (tile, rows), 1)
                    chosen = jnp.where(lanes == wanted, 1.0, 0.0).astype(BF16)
                    part = inner(chosen, window[which, slot])
                    if offset == 0:
                        total[at, :] = part
                    else:
                        total[at, :] += part

            if offset == 0:
                add()
            else:
                pl.when(others[offset][1])(add)
        picked[which] = total[...].astype(BF16)
        keep = pl.ds(pl.multiple_of(core * half, half), half)
        give = pl.ds(pl.multiple_of((1 - core) * half, half), half)
        there = remote(
            picked.at[which, give], outs[which].at[:, mine], psend.at[which], precv.at[which], partner
        )
        here = pltpu.make_async_copy(picked.at[which, keep], outs[which].at[:, mine], plocal.at[which])
        there.start()
        here.start()
        finals.append((there, here))

    for offset in OFFSETS[1:]:
        device, valid = others[offset]

        def finish(offset=offset, device=device):
            for which in range(2):
                slot = SLOT[-offset]
                remote(
                    arrays[which].at[:, mine],
                    window.at[which, slot],
                    send.at[which, slot],
                    recv.at[which, slot],
                    device,
                ).wait_send()
            slot = SLOT[-offset]
            remote(source, source_win.at[slot], ssend.at[slot], srecv.at[slot], device).wait_send()
            slot = SLOT[offset]
            remote(source, source_win.at[slot], ssend.at[slot], srecv.at[slot], device).wait_recv()

        pl.when(valid)(finish)
    sources[...] = source_win[...]
    for there, here in moves + finals:
        there.wait()
        here.wait()


def entry(mesh, tokens, out_grad, rel, source, wq, wk, wv, wo, wu, wd, bq, bv, bu):
    rows, model = tokens.shape
    width = model // 2
    hidden = 2 * wu.shape[1]
    hbm = pl.BlockSpec(memory_space=pl.ANY)
    vmem = pl.BlockSpec(memory_space=pltpu.VMEM)
    slots = len(OFFSETS)
    dma = pltpu.SemaphoreType.DMA
    return pl.pallas_call(
        functools.partial(entry_kernel, mesh.shape["seq"]),
        out_shape=(
            jax.ShapeDtypeStruct((rows // 2, model), BF16),
            jax.ShapeDtypeStruct((rows // 2, model), BF16),
            jax.ShapeDtypeStruct((slots, 1, rows), jnp.int32),
            jax.ShapeDtypeStruct((model, 3 * model), BF16),
            jax.ShapeDtypeStruct((model, model), BF16),
            jax.ShapeDtypeStruct((model, hidden), BF16),
            jax.ShapeDtypeStruct((hidden, model), BF16),
            jax.ShapeDtypeStruct((1, 3 * model), F32),
            jax.ShapeDtypeStruct((1, hidden), F32),
        ),
        in_specs=[hbm, hbm, vmem, vmem] + [hbm] * 9,
        out_specs=(hbm, hbm, vmem) + (hbm,) * 6,
        scratch_shapes=[
            pltpu.VMEM((2, slots, rows, width), BF16),
            pltpu.VMEM((rows, width), F32),
            pltpu.VMEM((2, rows, width), BF16),
            pltpu.VMEM((slots, 1, rows), jnp.int32),
            dma((9,)),
            dma((9,)),
            dma((9,)),
            dma((2, slots)),
            dma((2, slots)),
            dma((2,)),
            dma((slots,)),
            dma((slots,)),
            dma((2,)),
            dma((2,)),
            dma((2,)),
        ],
        compiler_params=pltpu.CompilerParams(
            collective_id=0, has_side_effects=True, vmem_limit_bytes=40 * MEBI
        ),
    )(tokens, out_grad, rel, source, wq, wk, wv, wo, wu, wd, bq, bv, bu)


def fold_rows(values):
    return jnp.sum(values.reshape(values.shape[0] // 8, 8, values.shape[1]), axis=0)


def layer_kernel(
    chunk,
    x,
    og,
    valid,
    wqkv,
    wo,
    wu,
    wd,
    bqkv,
    bo,
    g1,
    s1,
    bu,
    bd,
    g2,
    s2,
    out_low,
    in_low,
    grads,
    sums,
    qkv,
    ctx,
    prob,
    hat1,
    inv1,
    low1,
    act,
    slope,
    pre_low,
    work,
    flipped,
    dqkv,
    cgrad,
    low2,
    gtile,
    accs,
    gsem,
):
    rows, model = x.shape
    hidden = wu.shape[1]
    clusters = rows // CLUSTER
    pairs = model // 128
    tile = 256
    band = 64

    def at(step, size):
        return pl.ds(pl.multiple_of(step * size, size), size)

    lanes = lax.broadcasted_iota(jnp.int32, (CLUSTER, 128), 1)
    first_f = jnp.where(lanes < HEAD_DIM, 1.0, 0.0)
    first = first_f.astype(BF16)
    second = (1.0 - first_f).astype(BF16)

    def stacked(pair):
        return jnp.concatenate([pair * first, pair * second], axis=0)

    def beside(tall):
        return jnp.concatenate([tall[:CLUSTER], tall[CLUSTER:]], axis=1)

    @pl.loop(0, 3 * model // tile)
    def _(step):
        cols = at(step, tile)
        qkv[:, cols] = (inner(x[...], wqkv[:, cols]) + bqkv[:, cols]).astype(BF16)

    @pl.loop(0, clusters * pairs)
    def _(step):
        cluster, pair = step // pairs, step % pairs
        r = at(cluster, CLUSTER)
        q = qkv[r, at(pair, 128)]
        k = qkv[r, pl.ds(pl.multiple_of(model + pair * 128, 128), 128)]
        v = qkv[r, pl.ds(pl.multiple_of(2 * model + pair * 128, 128), 128)]
        scores = outer(stacked(q), k) * score_scale
        scores = jnp.where(valid[cluster] > 0.5, scores, masked_score)
        top = jnp.max(scores, axis=-1, keepdims=True)
        weight = jnp.exp(scores - top)
        p = weight / jnp.sum(weight, axis=-1, keepdims=True)
        prob[step] = p
        ctx[r, at(pair, 128)] = inner(beside(p.astype(BF16)), stacked(v)).astype(BF16)

    @pl.loop(0, model // tile)
    def _(step):
        cols = at(step, tile)
        hat1[:, cols] = inner(ctx[...], wo[:, cols]) + x[:, cols].astype(F32) + bo[:, cols]

    @pl.loop(0, rows // band)
    def _(step):
        r = at(step, band)
        h = hat1[r, :]
        centered = h - jnp.mean(h, axis=-1, keepdims=True)
        inv = lax.rsqrt(jnp.mean(centered * centered, axis=-1, keepdims=True) + norm_eps)
        hat = centered * inv
        hat1[r, :] = hat
        inv1[r, :] = inv
        low1[r, :] = (hat * g1[...] + s1[...]).astype(BF16)

    @pl.loop(0, hidden // tile)
    def _(step):
        cols = at(step, tile)
        pre = inner(low1[...], wu[:, cols]) + bu[:, cols]
        cdf = 0.5 * (1.0 + lax.erf(pre * root_half))
        act[:, cols] = (pre * cdf).astype(BF16)
        slope[:, cols] = cdf + pre * jnp.exp(-0.5 * pre * pre) * inv_root_tau

    @pl.loop(0, model // tile)
    def _(step):
        cols = at(step, tile)
        norm = hat1[:, cols] * g1[:, cols] + s1[:, cols]
        work[:, cols] = inner(act[...], wd[:, cols]) + norm + bd[:, cols]

    accs[...] = jnp.zeros_like(accs)

    @pl.loop(0, rows // band)
    def _(step):
        r = at(step, band)
        h = work[r, :]
        centered = h - jnp.mean(h, axis=-1, keepdims=True)
        inv = lax.rsqrt(jnp.mean(centered * centered, axis=-1, keepdims=True) + norm_eps)
        hat = centered * inv
        out_low[r, :] = (hat * g2[...] + s2[...]).astype(BF16)
        grad = og[r, :].astype(F32)
        accs[4] += fold_rows(grad * hat)
        accs[5] += fold_rows(grad)
        scaled = grad * g2[...]
        back = inv * (
            scaled
            - jnp.mean(scaled, axis=-1, keepdims=True)
            - hat * jnp.mean(scaled * hat, axis=-1, keepdims=True)
        )
        accs[3] += fold_rows(back)
        work[r, :] = back
        low2[r, :] = back.astype(BF16)

    def flip(source):
        @pl.loop(0, model // 128)
        def _(step):
            flipped[at(step, 128), :] = source[:, at(step, 128)].T

    half_rows = model // 2
    chunks = half_rows // chunk

    def product_tiles(right, width, places, count):
        def moves(index, slot):
            m, n = index // count, index % count
            for piece, (part, start, size) in enumerate(places(n)):
                yield pltpu.make_async_copy(
                    gtile.at[slot, :, :, pl.ds(piece * size, size)] if size != width
                    else gtile.at[slot, :, :, pl.ds(0, width)],
                    grads.at[part, pl.ds(m * chunks, chunks), :, pl.ds(start, size)],
                    gsem.at[slot, piece],
                )

        total = 2 * count

        @pl.loop(0, total)
        def _(index):
            slot = index % 2
            m, n = index // count, index % count

            @pl.when(index >= 2)
            def _():
                for move in moves(index - 2, slot):
                    move.wait()

            value = inner(flipped[at(m, half_rows), :], right[:, at(n, width)])
            gtile[slot, :, :, pl.ds(0, width)] = value.reshape(chunks, chunk, width).astype(BF16)
            for move in moves(index, slot):
                move.start()

        for index in range(max(total - 2, 0), total):
            for move in moves(index, index % 2):
                move.wait()

    part_q = model // 2
    part_h = hidden // 2
    wide = 512

    def square(which):
        def places(n):
            return [(0, which * part_q, part_q), (1, which * part_q, part_q)]

        return places

    def long(base):
        per_part = part_h // wide

        def places(n):
            part, inside = n // per_part, n % per_part
            return [(part, pl.multiple_of(base + inside * wide, 128), wide)]

        return places

    flip(low2)
    product_tiles(act, wide, long(4 * part_q + part_h), hidden // wide)

    @pl.loop(0, hidden // tile)
    def _(step):
        cols = at(step, tile)
        back = outer(low2[...], wd[cols, :]) * slope[:, cols]
        back = back.astype(BF16)
        pre_low[:, cols] = back
        sums[:, pl.ds(pl.multiple_of(2 * model + step * tile, tile), tile)] = jnp.sum(
            back.astype(F32), axis=0, keepdims=True
        )

    flip(low1)
    product_tiles(pre_low, wide, long(4 * part_q), hidden // wide)

    @pl.loop(0, model // tile)
    def _(step):
        cols = at(step, tile)
        work[:, cols] += outer(pre_low[...], wu[cols, :])

    @pl.loop(0, rows // band)
    def _(step):
        r = at(step, band)
        grad = work[r, :]
        hat = hat1[r, :]
        accs[1] += fold_rows(grad * hat)
        accs[2] += fold_rows(grad)
        scaled = grad * g1[...]
        back = inv1[r, :] * (
            scaled
            - jnp.mean(scaled, axis=-1, keepdims=True)
            - hat * jnp.mean(scaled * hat, axis=-1, keepdims=True)
        )
        accs[0] += fold_rows(back)
        work[r, :] = back
        low2[r, :] = back.astype(BF16)

    flip(low2)
    product_tiles(ctx, model, square(3), 1)

    @pl.loop(0, model // tile)
    def _(step):
        cols = at(step, tile)
        cgrad[:, cols] = outer(low2[...], wo[cols, :]).astype(BF16)

    @pl.loop(0, clusters * pairs)
    def _(step):
        cluster, pair = step // pairs, step % pairs
        r = at(cluster, CLUSTER)
        at_q = at(pair, 128)
        at_k = pl.ds(pl.multiple_of(model + pair * 128, 128), 128)
        at_v = pl.ds(pl.multiple_of(2 * model + pair * 128, 128), 128)
        q, k, v = qkv[r, at_q], qkv[r, at_k], qkv[r, at_v]
        p = prob[step]
        dctx = stacked(cgrad[r, at_q])
        dprob = outer(dctx, v)
        dscore = (p * (dprob - jnp.sum(p * dprob, axis=-1, keepdims=True))).astype(BF16)
        dqkv[r, at_q] = (inner(beside(dscore), stacked(k)) * score_scale).astype(BF16)
        dqkv[r, at_k] = (under(dscore, stacked(q)) * score_scale).astype(BF16)
        dqkv[r, at_v] = under(p.astype(BF16), dctx).astype(BF16)

    flip(x)
    for which in range(3):
        product_tiles(dqkv.at[:, pl.ds(which * model, model)], model, square(which), 1)

    for which in range(2):
        @pl.loop(0, model // tile)
        def _(step, which=which):
            value = dqkv[:, pl.ds(pl.multiple_of(2 * which * model + step * tile, tile), tile)]
            sums[:, pl.ds(pl.multiple_of(which * model + step * tile, tile), tile)] = jnp.sum(
                value.astype(F32), axis=0, keepdims=True
            )

    @pl.loop(0, model // tile)
    def _(step):
        cols = at(step, tile)
        in_low[:, cols] = (work[:, cols] + outer(dqkv[...], wqkv[cols, :])).astype(BF16)

    for i in range(6):
        sums[:, pl.ds(2 * model + hidden + i * model, model)] = jnp.sum(accs[i], axis=0, keepdims=True)


def layer(chunk, x, og, valid, wqkv, wo, wu, wd, bqkv, bo, g1, s1, bu, bd, g2, s2):
    rows, model = x.shape
    hidden = wu.shape[1]
    hbm = pl.BlockSpec(memory_space=pl.ANY)
    vmem = pl.BlockSpec(memory_space=pltpu.VMEM)
    part = 2 * model + hidden
    steps = rows // CLUSTER * (model // 128)
    total = 8 * model + hidden
    return pl.pallas_call(
        functools.partial(layer_kernel, chunk),
        out_shape=(
            jax.ShapeDtypeStruct((rows, model), BF16),
            jax.ShapeDtypeStruct((rows, model), BF16),
            jax.ShapeDtypeStruct((2, model // chunk, chunk, part), BF16),
            jax.ShapeDtypeStruct((1, total), F32),
        ),
        in_specs=[vmem] * 15,
        out_specs=(vmem, vmem, hbm, vmem),
        scratch_shapes=[
            pltpu.VMEM((rows, 3 * model), BF16),
            pltpu.VMEM((rows, model), BF16),
            pltpu.VMEM((steps, 2 * CLUSTER, CLUSTER), F32),
            pltpu.VMEM((rows, model), F32),
            pltpu.VMEM((rows, 1), F32),
            pltpu.VMEM((rows, model), BF16),
            pltpu.VMEM((rows, hidden), BF16),
            pltpu.VMEM((rows, hidden), F32),
            pltpu.VMEM((rows, hidden), BF16),
            pltpu.VMEM((rows, model), F32),
            pltpu.VMEM((model, rows), BF16),
            pltpu.VMEM((rows, 3 * model), BF16),
            pltpu.VMEM((rows, model), BF16),
            pltpu.VMEM((rows, model), BF16),
            pltpu.VMEM((2, model // 2 // chunk, chunk, model), BF16),
            pltpu.VMEM((6, 8, model), F32),
            pltpu.SemaphoreType.DMA((2, 2)),
        ],
        compiler_params=pltpu.CompilerParams(vmem_limit_bytes=60 * MEBI),
    )(x, og, valid, wqkv, wo, wu, wd, bqkv, bo, g1, s1, bu, bd, g2, s2)


def exit_kernel(blocks, reduce, *refs):
    if reduce:
        (out_low, in_low, sources, grads, sums, out_home, in_home, grad_sum, sums_sum, *scratch) = refs
        (window, home, wsend, wrecv, csend, crecv, clocal, hsend, hrecv, hlocal, *scratch) = scratch
        (mine_g, from_core, got, gsend, grecv, glocal, rsend, rrecv, vrecv, vsend, vsem) = scratch
    else:
        (out_low, in_low, sources, out_home, in_home, *scratch) = refs
        (window, home, wsend, wrecv, csend, crecv, clocal, hsend, hrecv, hlocal) = scratch
    seq, core = lax.axis_index("seq"), lax.axis_index("head")
    rows, width = window.shape[2], window.shape[3]
    half = rows // 2
    partner = (seq, 1 - core)
    others = near(seq, core, blocks)
    bits = max(blocks.bit_length() - 1, 0)
    greetings = [(partner, None)] + [others[offset] for offset in OFFSETS[1:]]

    def across(bit):
        mask = 1 << bit
        return (seq + mask - 2 * mask * ((seq // mask) % 2), core)

    if reduce:
        greetings += [(across(bit), None) for bit in range(2, bits)]
    greet(greetings)

    mine = pl.ds(pl.multiple_of(core * width, width), width)
    theirs = pl.ds(pl.multiple_of((1 - core) * width, width), width)
    keep = pl.ds(pl.multiple_of(core * half, half), half)
    arrays = (out_low, in_low)
    firsts = []
    for which, array in enumerate(arrays):
        there = remote(
            array.at[:, theirs], window.at[which, 0, keep], csend.at[which], crecv.at[which], partner
        )
        here = pltpu.make_async_copy(array.at[:, mine], window.at[which, 0, keep], clocal.at[which])
        there.start()
        here.start()
        firsts.append((there, here))

    if reduce:
        parts = 2
        span = mine_g.shape[3] // parts
        core_moves = []
        for part in range(parts):
            cols = pl.ds(part * span, span)
            there = remote(
                grads.at[1 - core, :, :, cols], from_core.at[:, :, cols], gsend.at[part], grecv.at[part], partner
            )
            here = pltpu.make_async_copy(grads.at[core, :, :, cols], mine_g.at[0, :, :, cols], glocal.at[part])
            there.start()
            here.start()
            core_moves.append((there, here))

    def spread(which):
        for offset in OFFSETS[1:]:
            device, valid = others[offset]
            slot = SLOT[-offset]
            pl.when(valid)(
                remote(
                    window.at[which, 0], window.at[which, slot], wsend.at[which, slot], wrecv.at[which, slot], device
                ).start
            )

    for which in range(2):
        there, here = firsts[which]
        there.wait()
        here.wait()
        spread(which)

    def reduce_start(part, level):
        cols = pl.ds(part * span, span)
        order = orders[part]
        bit = order[level]
        own = (seq // (1 << bit)) % 2
        left = sorted(set(range(bits)) - set(order[:level]))
        low = 1 << left.index(bit)
        high = (1 << len(left)) // (2 * low)
        outs = []
        for top in range(high):
            src = mine_g.at[level % 2, pl.ds(pl.multiple_of((top * 2 + 1 - own) * low, low), low), :, cols]
            dst = got.at[pl.ds(base[level] + top * low, low), :, cols]
            outs.append(remote(src, dst, rsend.at[part, level, top], rrecv.at[part, level, top], across(bit)))
        return outs, own, low, high, cols

    def reduce_finish(part, level, state):
        outs, own, low, high, cols = state
        for copy in outs:
            copy.wait()
        for top in range(high):
            @pl.loop(0, low)
            def _(inside):
                held = mine_g[level % 2, (top * 2 + own) * low + inside, :, cols].astype(F32)
                other = got[base[level] + top * low + inside, :, cols].astype(F32)
                value = held + other
                if level == bits - 1:
                    grad_sum[:, cols] = value
                else:
                    mine_g[(level + 1) % 2, top * low + inside, :, cols] = value.astype(BF16)

    def pick(which):
        tile = 256
        for offset in OFFSETS:
            slot = SLOT[offset]

            def add(offset=offset, slot=slot):
                if offset != 0:
                    device, _ = others[offset]
                    remote(
                        window.at[which, 0],
                        window.at[which, slot],
                        wsend.at[which, slot],
                        wrecv.at[which, slot],
                        device,
                    ).wait_recv()

                @pl.loop(0, rows // tile)
                def _(step):
                    at = pl.ds(pl.multiple_of(step * tile, tile), tile)
                    places = lax.broadcasted_iota(jnp.int32, (tile, rows), 0) + (step * tile + seq * rows)
                    chosen = jnp.where(sources[slot] == places, 1.0, 0.0).astype(BF16)
                    part = inner(chosen, window[which, slot]).astype(BF16)
                    if offset == 0:
                        home[which, at, :] = part
                    else:
                        home[which, at, :] += part

            if offset == 0:
                add()
            else:
                pl.when(others[offset][1])(add)
        target = (out_home, in_home)[which]
        there = remote(home.at[which], target.at[:, mine], hsend.at[which], hrecv.at[which], partner)
        here = pltpu.make_async_copy(home.at[which], target.at[:, mine], hlocal.at[which])
        there.start()
        here.start()
        return there, here

    lasts = []
    if not reduce:
        lasts = [pick(0), pick(1)]
    else:
        orders = ([0, 1] + list(range(bits - 1, 1, -1)), [1, 0] + list(range(bits - 1, 1, -1)))
        base, count = [], 0
        for level in range(bits):
            base.append(count)
            count += blocks >> (level + 1)

        def sum_level(level):
            device = partner if level == 0 else across(level - 1)
            return remote(vsend.at[level], vrecv.at[level], vsem.at[0, level], vsem.at[1, level], device)

        def sum_start(level):
            if level == 0:
                vsend[0] = sums[...]
            sum_level(level).start()

        def sum_finish(level):
            sum_level(level).wait()
            value = vsend[level] + vrecv[level]
            if level == bits:
                sums_sum[...] = value
            else:
                vsend[level + 1] = value

        sum_start(0)
        states = [None] * parts
        for part in range(parts):
            there, here = core_moves[part]
            there.wait()
            here.wait()
            cols = pl.ds(part * span, span)

            @pl.loop(0, blocks)
            def _(inside):
                value = mine_g[0, inside, :, cols].astype(F32) + from_core[inside, :, cols].astype(F32)
                mine_g[0, inside, :, cols] = value.astype(BF16)

            states[part] = reduce_start(part, 0)
            for copy in states[part][0]:
                copy.start()
        sum_finish(0)
        sum_start(1)
        lasts.append(pick(0))
        for level in range(bits):
            for part in range(parts):
                reduce_finish(part, level, states[part])
                if level + 1 < bits:
                    states[part] = reduce_start(part, level + 1)
                    for copy in states[part][0]:
                        copy.start()
            sum_finish(level + 1)
            if level + 1 < bits:
                sum_start(level + 2)
            if level == 1:
                lasts.append(pick(1))
        if bits < 2:
            lasts.append(pick(1))

    for offset in OFFSETS[1:]:
        device, valid = others[offset]
        slot = SLOT[-offset]

        def finish(device=device, slot=slot):
            for which in range(2):
                remote(
                    window.at[which, 0], window.at[which, slot], wsend.at[which, slot], wrecv.at[which, slot], device
                ).wait_send()

        pl.when(valid)(finish)
    for there, here in lasts:
        there.wait()
        here.wait()


def leave(mesh, reduce, out_low, in_low, sources, grads, sums):
    half, model = out_low.shape
    rows, width = 2 * half, model // 2
    blocks = mesh.shape["seq"]
    slots = len(OFFSETS)
    hbm = pl.BlockSpec(memory_space=pl.ANY)
    vmem = pl.BlockSpec(memory_space=pltpu.VMEM)
    dma = pltpu.SemaphoreType.DMA
    out_shape = [jax.ShapeDtypeStruct((rows, model), BF16)] * 2
    out_specs = [hbm, hbm]
    in_specs = [hbm, hbm, vmem]
    args = [out_low, in_low, sources]
    scratch = [
        pltpu.VMEM((2, slots, rows, width), BF16),
        pltpu.VMEM((2, rows, width), BF16),
        dma((2, slots)),
        dma((2, slots)),
        dma((2,)),
        dma((2,)),
        dma((2,)),
        dma((2,)),
        dma((2,)),
        dma((2,)),
    ]
    if reduce:
        _, chunks, chunk, span = grads.shape
        bits = blocks.bit_length() - 1
        args += [grads, sums]
        in_specs += [hbm, vmem]
        out_shape += [jax.ShapeDtypeStruct((chunk, span), F32), jax.ShapeDtypeStruct(sums.shape, F32)]
        out_specs += [vmem, vmem]
        scratch += [
            pltpu.VMEM((2, blocks, chunk, span), BF16),
            pltpu.VMEM((blocks, chunk, span), BF16),
            pltpu.VMEM((blocks, chunk, span), BF16),
            dma((2,)),
            dma((2,)),
            dma((2,)),
            dma((2, bits, blocks // 2)),
            dma((2, bits, blocks // 2)),
            pltpu.VMEM((bits + 1,) + sums.shape, F32),
            pltpu.VMEM((bits + 1,) + sums.shape, F32),
            dma((2, bits + 1)),
        ]
    return pl.pallas_call(
        functools.partial(exit_kernel, blocks, reduce),
        out_shape=tuple(out_shape),
        in_specs=in_specs,
        out_specs=tuple(out_specs),
        scratch_shapes=scratch,
        compiler_params=pltpu.CompilerParams(
            collective_id=1, has_side_effects=True, vmem_limit_bytes=60 * MEBI
        ),
    )(*args)


def body(
    mesh,
    tokens,
    out_grad,
    doc_lengths,
    cluster_perm,
    query_weight,
    query_bias,
    key_weight,
    value_weight,
    value_bias,
    output_weight,
    output_bias,
    first_gain,
    first_shift,
    up_weight,
    up_bias,
    down_weight,
    down_bias,
    second_gain,
    second_shift,
):
    rows, model = tokens.shape
    half = rows // 2
    hidden = 2 * up_weight.shape[1]
    blocks = mesh.shape["seq"]
    seq, core = lax.axis_index("seq"), lax.axis_index("head")
    positions = seq * rows + jnp.arange(rows, dtype=jnp.int32)
    slot_start, slot_length = doc_lookup(doc_lengths, positions)
    source = slot_start + cluster_perm
    valid = (cluster_perm < slot_length).astype(F32).reshape(2, half // CLUSTER, 1, CLUSTER)
    valid = lax.dynamic_index_in_dim(valid, core, 0, keepdims=False)

    def row(v):
        return v.reshape(1, -1)

    x, og, sources, wqkv, wo, wu, wd, bqkv, bu = entry(
        mesh,
        tokens,
        out_grad,
        (source - seq * rows).reshape(rows, 1),
        row(source),
        query_weight,
        key_weight,
        value_weight,
        output_weight,
        up_weight,
        down_weight,
        row(query_bias),
        row(value_bias),
        row(up_bias),
    )
    no_key = (jnp.arange(3 * model) // model != 1)[None, :]
    bqkv = jnp.where(no_key, bqkv, 0.0)
    chunk = model // blocks
    reduce = chunk % 16 == 0 and blocks >= 4 and blocks & (blocks - 1) == 0
    out_low, in_low, grads, sums = layer(
        chunk if reduce else 48,
        x,
        og,
        valid,
        wqkv,
        wo,
        wu,
        wd,
        bqkv,
        row(output_bias),
        row(first_gain),
        row(first_shift),
        bu,
        row(down_bias),
        row(second_gain),
        row(second_shift),
    )
    if reduce:
        out_home, in_home, grad_sum, sums = leave(mesh, True, out_low, in_low, sources, grads, sums)
    else:
        out_home, in_home = leave(mesh, False, out_low, in_low, sources, None, None)
        sums = lax.psum(sums, ("seq", "head"))
        grads = grads.reshape(2, model, -1)
        grads = lax.psum_scatter(grads.astype(F32), "head", scatter_dimension=0, tiled=True)[0]
        grad_sum = lax.psum_scatter(grads, "seq", scatter_dimension=0, tiled=True)
    part_q, part_h = model // 2, hidden // 2
    cuts = [part_q * i for i in range(5)] + [4 * part_q + part_h, 4 * part_q + 2 * part_h]
    dwq, dwk, dwv, dwo, dwu, dwd = (grad_sum[:, a:b] for a, b in zip(cuts[:-1], cuts[1:]))
    sums = sums[0]

    def mine(start, size):
        return lax.dynamic_slice(sums, (start + core * size,), (size,))

    def block(index):
        return lax.dynamic_slice(sums, (2 * model + hidden + index * model + seq * chunk,), (chunk,))

    return (
        out_home.astype(F32),
        in_home.astype(F32),
        dwq,
        mine(0, part_q),
        dwk,
        dwv,
        mine(model, part_q),
        dwo.T,
        block(0),
        block(1),
        block(2),
        dwu,
        mine(2 * model, part_h),
        dwd.T,
        block(3),
        block(4),
        block(5),
    )


def solution(mesh):
    placed = (
        P("seq", None),
        P("seq", None),
        P(),
        P("seq"),
        P(None, "head"),
        P("head"),
        P(None, "head"),
        P(None, "head"),
        P("head"),
        P("head", None),
        P(),
        P(),
        P(),
        P(None, "head"),
        P("head"),
        P("head", None),
        P(),
        P(),
        P(),
    )
    return jax.shard_map(
        functools.partial(body, mesh),
        mesh=mesh,
        in_specs=placed,
        out_specs=(
            P("seq", None),
            P("seq", None),
            P("seq", "head"),
            P("head"),
            P("seq", "head"),
            P("seq", "head"),
            P("head"),
            P("head", "seq"),
            P("seq"),
            P("seq"),
            P("seq"),
            P("seq", "head"),
            P("head"),
            P("head", "seq"),
            P("seq"),
            P("seq"),
            P("seq"),
        ),
        check_vma=False,
    )
```

```python
import functools

import jax
import jax.numpy as jnp
from jax import lax
from jax.experimental import pallas as pl
from jax.experimental.pallas import tpu as pltpu
from jax.sharding import PartitionSpec as P

MESH = pl.DeviceIdType.MESH
HEAD_DIM = 64
CLUSTER = 128
OFFSETS = (0, 1, -1, 2, -2)
SLOT = {offset: slot for slot, offset in enumerate(OFFSETS)}
MEBI = 1 << 20

norm_eps = 1e-12
masked_score = -1e30
root_half = 0.7071067811865476
inv_root_tau = 0.3989422804014327
score_scale = HEAD_DIM ** (-0.5)

F32 = jnp.float32
BF16 = jnp.bfloat16


def doc_lookup(doc_lengths, positions):
    padded = (doc_lengths + CLUSTER - 1) // CLUSTER * CLUSTER
    starts = jnp.cumsum(padded) - padded
    doc_of = jnp.sum((starts[None, :] <= positions[:, None]).astype(jnp.int32), axis=1) - 1
    picked = jnp.arange(starts.shape[0], dtype=jnp.int32)[None, :] == doc_of[:, None]
    slot_start = jnp.sum(jnp.where(picked, starts[None, :], 0), axis=1)
    slot_length = jnp.sum(jnp.where(picked, doc_lengths[None, :], 0), axis=1)
    return (slot_start, slot_length)


def remote(src, dst, send, recv, device):
    return pltpu.make_async_remote_copy(
        src_ref=src, dst_ref=dst, send_sem=send, recv_sem=recv, device_id=device, device_id_type=MESH
    )


def greet(devices):
    barrier = pltpu.get_barrier_semaphore()
    count = 0
    for device, valid in devices:
        def hello(device=device):
            pl.semaphore_signal(barrier, inc=1, device_id=device, device_id_type=MESH)

        if valid is None:
            hello()
            count = count + 1
        else:
            pl.when(valid)(hello)
            count = count + valid.astype(jnp.int32)
    pl.semaphore_wait(barrier, count)


def near(seq, core, blocks):
    out = {}
    for offset in OFFSETS[1:]:
        there = seq + offset
        out[offset] = ((there, core), (there >= 0) & (there < blocks))
    return out


def inner(left, right):
    return lax.dot_general(left, right, (((1,), (0,)), ((), ())), preferred_element_type=F32)


def outer(left, right):
    return lax.dot_general(left, right, (((1,), (1,)), ((), ())), preferred_element_type=F32)


def under(left, right):
    return lax.dot_general(left, right, (((0,), (0,)), ((), ())), preferred_element_type=F32)


def entry_kernel(
    blocks,
    tokens,
    out_grad,
    rel,
    source,
    wq,
    wk,
    wv,
    wo,
    wu,
    wd,
    bq,
    bv,
    bu,
    slot_tokens,
    slot_grad,
    sources,
    wqkv_full,
    wo_full,
    wu_full,
    wd_full,
    bqkv_full,
    bu_full,
    window,
    total,
    picked,
    source_win,
    wsend,
    wrecv,
    wlocal,
    send,
    recv,
    local,
    ssend,
    srecv,
    psend,
    precv,
    plocal,
):
    seq, core = lax.axis_index("seq"), lax.axis_index("head")
    rows, width = window.shape[2], window.shape[3]
    half = rows // 2
    partner = (seq, 1 - core)
    others = near(seq, core, blocks)
    greet([(partner, None)] + [others[offset] for offset in OFFSETS[1:]])

    mine = pl.ds(pl.multiple_of(core * width, width), width)
    arrays = (tokens, out_grad)
    locals_ = []
    for which, array in enumerate(arrays):
        for offset in OFFSETS[1:]:
            device, valid = others[offset]
            slot = SLOT[-offset]
            copy = remote(
                array.at[:, mine], window.at[which, slot], send.at[which, slot], recv.at[which, slot], device
            )
            pl.when(valid)(copy.start)
            if which == 0:
                tiny = remote(source, source_win.at[slot], ssend.at[slot], srecv.at[slot], device)
                pl.when(valid)(tiny.start)
        own = pltpu.make_async_copy(array.at[:, mine], window.at[which, 0], local.at[which])
        own.start()
        locals_.append(own)

    wide, deep = wq.shape[1], wd.shape[0]
    model = wq.shape[0]
    at_core = pl.multiple_of(core * wide, wide)
    at_deep = pl.multiple_of(core * deep, deep)
    pieces = []
    for i, array in enumerate((wq, wk, wv)):
        at = pl.multiple_of(i * model + core * wide, wide)
        pieces.append((array, wqkv_full.at[:, pl.ds(at, wide)]))
    pieces.append((wo, wo_full.at[pl.ds(at_core, wide), :]))
    pieces.append((wu, wu_full.at[:, pl.ds(at_deep, deep)]))
    pieces.append((wd, wd_full.at[pl.ds(at_deep, deep), :]))
    pieces.append((bq, bqkv_full.at[:, pl.ds(at_core, wide)]))
    pieces.append((bv, bqkv_full.at[:, pl.ds(pl.multiple_of(2 * model + core * wide, wide), wide)]))
    pieces.append((bu, bu_full.at[:, pl.ds(at_deep, deep)]))
    moves = []
    for i, (array, place) in enumerate(pieces):
        there = remote(array, place, wsend.at[i], wrecv.at[i], partner)
        here = pltpu.make_async_copy(array, place, wlocal.at[i])
        there.start()
        here.start()
        moves.append((there, here))

    source_win[0] = source[...]
    for offset in OFFSETS[1:]:

        def blank(slot=SLOT[offset]):
            source_win[slot] = jnp.full(source.shape, -1, jnp.int32)

        pl.when(jnp.logical_not(others[offset][1]))(blank)
    tile = 256
    outs = (slot_tokens, slot_grad)
    finals = []
    for which in range(2):
        locals_[which].wait()
        for offset in OFFSETS:
            slot = SLOT[offset]

            def add(which=which, offset=offset, slot=slot):
                if offset != 0:
                    device, _ = others[offset]
                    remote(
                        arrays[which].at[:, mine],
                        window.at[which, slot],
                        send.at[which, slot],
                        recv.at[which, slot],
                        device,
                    ).wait_recv()

                @pl.loop(0, rows // tile)
                def _(step):
                    at = pl.ds(pl.multiple_of(step * tile, tile), tile)
                    wanted = rel[at, :] - offset * rows
                    lanes = lax.broadcasted_iota(jnp.int32, (tile, rows), 1)
                    chosen = jnp.where(lanes == wanted, 1.0, 0.0).astype(BF16)
                    part = inner(chosen, window[which, slot])
                    if offset == 0:
                        total[at, :] = part
                    else:
                        total[at, :] += part

            if offset == 0:
                add()
            else:
                pl.when(others[offset][1])(add)
        picked[which] = total[...].astype(BF16)
        keep = pl.ds(pl.multiple_of(core * half, half), half)
        give = pl.ds(pl.multiple_of((1 - core) * half, half), half)
        there = remote(
            picked.at[which, give], outs[which].at[:, mine], psend.at[which], precv.at[which], partner
        )
        here = pltpu.make_async_copy(picked.at[which, keep], outs[which].at[:, mine], plocal.at[which])
        there.start()
        here.start()
        finals.append((there, here))

    for offset in OFFSETS[1:]:
        device, valid = others[offset]

        def finish(offset=offset, device=device):
            for which in range(2):
                slot = SLOT[-offset]
                remote(
                    arrays[which].at[:, mine],
                    window.at[which, slot],
                    send.at[which, slot],
                    recv.at[which, slot],
                    device,
                ).wait_send()
            slot = SLOT[-offset]
            remote(source, source_win.at[slot], ssend.at[slot], srecv.at[slot], device).wait_send()
            slot = SLOT[offset]
            remote(source, source_win.at[slot], ssend.at[slot], srecv.at[slot], device).wait_recv()

        pl.when(valid)(finish)
    sources[...] = source_win[...]
    for there, here in moves + finals:
        there.wait()
        here.wait()


def entry(mesh, tokens, out_grad, rel, source, wq, wk, wv, wo, wu, wd, bq, bv, bu):
    rows, model = tokens.shape
    width = model // 2
    hidden = 2 * wu.shape[1]
    hbm = pl.BlockSpec(memory_space=pl.ANY)
    vmem = pl.BlockSpec(memory_space=pltpu.VMEM)
    slots = len(OFFSETS)
    dma = pltpu.SemaphoreType.DMA
    return pl.pallas_call(
        functools.partial(entry_kernel, mesh.shape["seq"]),
        out_shape=(
            jax.ShapeDtypeStruct((rows // 2, model), BF16),
            jax.ShapeDtypeStruct((rows // 2, model), BF16),
            jax.ShapeDtypeStruct((slots, 1, rows), jnp.int32),
            jax.ShapeDtypeStruct((model, 3 * model), BF16),
            jax.ShapeDtypeStruct((model, model), BF16),
            jax.ShapeDtypeStruct((model, hidden), BF16),
            jax.ShapeDtypeStruct((hidden, model), BF16),
            jax.ShapeDtypeStruct((1, 3 * model), F32),
            jax.ShapeDtypeStruct((1, hidden), F32),
        ),
        in_specs=[hbm, hbm, vmem, vmem] + [hbm] * 9,
        out_specs=(hbm, hbm, vmem) + (hbm,) * 6,
        scratch_shapes=[
            pltpu.VMEM((2, slots, rows, width), BF16),
            pltpu.VMEM((rows, width), F32),
            pltpu.VMEM((2, rows, width), BF16),
            pltpu.VMEM((slots, 1, rows), jnp.int32),
            dma((9,)),
            dma((9,)),
            dma((9,)),
            dma((2, slots)),
            dma((2, slots)),
            dma((2,)),
            dma((slots,)),
            dma((slots,)),
            dma((2,)),
            dma((2,)),
            dma((2,)),
        ],
        compiler_params=pltpu.CompilerParams(
            collective_id=0, has_side_effects=True, vmem_limit_bytes=40 * MEBI
        ),
    )(tokens, out_grad, rel, source, wq, wk, wv, wo, wu, wd, bq, bv, bu)


def fold_rows(values):
    return jnp.sum(values.reshape(values.shape[0] // 8, 8, values.shape[1]), axis=0)


def layer_kernel(
    chunk,
    x,
    og,
    valid,
    wqkv,
    wo,
    wu,
    wd,
    bqkv,
    bo,
    g1,
    s1,
    bu,
    bd,
    g2,
    s2,
    out_low,
    in_low,
    grads,
    sums,
    qkv,
    ctx,
    prob,
    hat1,
    inv1,
    low1,
    act,
    slope,
    pre_low,
    work,
    flipped,
    dqkv,
    cgrad,
    low2,
    gtile,
    accs,
    gsem,
):
    rows, model = x.shape
    hidden = wu.shape[1]
    clusters = rows // CLUSTER
    pairs = model // 128
    tile = 256
    band = 64

    def at(step, size):
        return pl.ds(pl.multiple_of(step * size, size), size)

    lanes = lax.broadcasted_iota(jnp.int32, (CLUSTER, 128), 1)
    first_f = jnp.where(lanes < HEAD_DIM, 1.0, 0.0)
    first = first_f.astype(BF16)
    second = (1.0 - first_f).astype(BF16)

    def stacked(pair):
        return jnp.concatenate([pair * first, pair * second], axis=0)

    def beside(tall):
        return jnp.concatenate([tall[:CLUSTER], tall[CLUSTER:]], axis=1)

    @pl.loop(0, 3 * model // tile)
    def _(step):
        cols = at(step, tile)
        qkv[:, cols] = (inner(x[...], wqkv[:, cols]) + bqkv[:, cols]).astype(BF16)

    @pl.loop(0, clusters * pairs)
    def _(step):
        cluster, pair = step // pairs, step % pairs
        r = at(cluster, CLUSTER)
        q = qkv[r, at(pair, 128)]
        k = qkv[r, pl.ds(pl.multiple_of(model + pair * 128, 128), 128)]
        v = qkv[r, pl.ds(pl.multiple_of(2 * model + pair * 128, 128), 128)]
        scores = outer(stacked(q), k) * score_scale
        scores = jnp.where(valid[cluster] > 0.5, scores, masked_score)
        top = jnp.max(scores, axis=-1, keepdims=True)
        weight = jnp.exp(scores - top)
        p = weight / jnp.sum(weight, axis=-1, keepdims=True)
        prob[step] = p
        ctx[r, at(pair, 128)] = inner(beside(p.astype(BF16)), stacked(v)).astype(BF16)

    @pl.loop(0, model // tile)
    def _(step):
        cols = at(step, tile)
        hat1[:, cols] = inner(ctx[...], wo[:, cols]) + x[:, cols].astype(F32) + bo[:, cols]

    @pl.loop(0, rows // band)
    def _(step):
        r = at(step, band)
        h = hat1[r, :]
        centered = h - jnp.mean(h, axis=-1, keepdims=True)
        inv = lax.rsqrt(jnp.mean(centered * centered, axis=-1, keepdims=True) + norm_eps)
        hat = centered * inv
        hat1[r, :] = hat
        inv1[r, :] = inv
        low1[r, :] = (hat * g1[...] + s1[...]).astype(BF16)

    @pl.loop(0, hidden // tile)
    def _(step):
        cols = at(step, tile)
        pre = inner(low1[...], wu[:, cols]) + bu[:, cols]
        cdf = 0.5 * (1.0 + lax.erf(pre * root_half))
        act[:, cols] = (pre * cdf).astype(BF16)
        slope[:, cols] = cdf + pre * jnp.exp(-0.5 * pre * pre) * inv_root_tau

    @pl.loop(0, model // tile)
    def _(step):
        cols = at(step, tile)
        norm = hat1[:, cols] * g1[:, cols] + s1[:, cols]
        work[:, cols] = inner(act[...], wd[:, cols]) + norm + bd[:, cols]

    accs[...] = jnp.zeros_like(accs)

    @pl.loop(0, rows // band)
    def _(step):
        r = at(step, band)
        h = work[r, :]
        centered = h - jnp.mean(h, axis=-1, keepdims=True)
        inv = lax.rsqrt(jnp.mean(centered * centered, axis=-1, keepdims=True) + norm_eps)
        hat = centered * inv
        out_low[r, :] = (hat * g2[...] + s2[...]).astype(BF16)
        grad = og[r, :].astype(F32)
        accs[4] += fold_rows(grad * hat)
        accs[5] += fold_rows(grad)
        scaled = grad * g2[...]
        back = inv * (
            scaled
            - jnp.mean(scaled, axis=-1, keepdims=True)
            - hat * jnp.mean(scaled * hat, axis=-1, keepdims=True)
        )
        accs[3] += fold_rows(back)
        work[r, :] = back
        low2[r, :] = back.astype(BF16)

    def flip(source):
        @pl.loop(0, model // 128)
        def _(step):
            flipped[at(step, 128), :] = source[:, at(step, 128)].T

    half_rows = model // 2
    chunks = half_rows // chunk

    def product_tiles(right, width, places, count):
        def moves(index, slot):
            m, n = index // count, index % count
            for piece, (part, start, size) in enumerate(places(n)):
                yield pltpu.make_async_copy(
                    gtile.at[slot, :, :, pl.ds(piece * size, size)] if size != width
                    else gtile.at[slot, :, :, pl.ds(0, width)],
                    grads.at[part, pl.ds(m * chunks, chunks), :, pl.ds(start, size)],
                    gsem.at[slot, piece],
                )

        total = 2 * count

        @pl.loop(0, total)
        def _(index):
            slot = index % 2
            m, n = index // count, index % count

            @pl.when(index >= 2)
            def _():
                for move in moves(index - 2, slot):
                    move.wait()

            value = inner(flipped[at(m, half_rows), :], right[:, at(n, width)])
            gtile[slot, :, :, pl.ds(0, width)] = value.reshape(chunks, chunk, width).astype(BF16)
            for move in moves(index, slot):
                move.start()

        for index in range(max(total - 2, 0), total):
            for move in moves(index, index % 2):
                move.wait()

    part_q = model // 2
    part_h = hidden // 2
    wide = 512

    def square(which):
        def places(n):
            return [(0, which * part_q, part_q), (1, which * part_q, part_q)]

        return places

    def long(base):
        per_part = part_h // wide

        def places(n):
            part, inside = n // per_part, n % per_part
            return [(part, pl.multiple_of(base + inside * wide, 128), wide)]

        return places

    flip(low2)
    product_tiles(act, wide, long(4 * part_q + part_h), hidden // wide)

    @pl.loop(0, hidden // tile)
    def _(step):
        cols = at(step, tile)
        back = outer(low2[...], wd[cols, :]) * slope[:, cols]
        back = back.astype(BF16)
        pre_low[:, cols] = back
        sums[:, pl.ds(pl.multiple_of(2 * model + step * tile, tile), tile)] = jnp.sum(
            back.astype(F32), axis=0, keepdims=True
        )

    flip(low1)
    product_tiles(pre_low, wide, long(4 * part_q), hidden // wide)

    @pl.loop(0, model // tile)
    def _(step):
        cols = at(step, tile)
        work[:, cols] += outer(pre_low[...], wu[cols, :])

    @pl.loop(0, rows // band)
    def _(step):
        r = at(step, band)
        grad = work[r, :]
        hat = hat1[r, :]
        accs[1] += fold_rows(grad * hat)
        accs[2] += fold_rows(grad)
        scaled = grad * g1[...]
        back = inv1[r, :] * (
            scaled
            - jnp.mean(scaled, axis=-1, keepdims=True)
            - hat * jnp.mean(scaled * hat, axis=-1, keepdims=True)
        )
        accs[0] += fold_rows(back)
        work[r, :] = back
        low2[r, :] = back.astype(BF16)

    flip(low2)
    product_tiles(ctx, model, square(3), 1)

    @pl.loop(0, model // tile)
    def _(step):
        cols = at(step, tile)
        cgrad[:, cols] = outer(low2[...], wo[cols, :]).astype(BF16)

    @pl.loop(0, clusters * pairs)
    def _(step):
        cluster, pair = step // pairs, step % pairs
        r = at(cluster, CLUSTER)
        at_q = at(pair, 128)
        at_k = pl.ds(pl.multiple_of(model + pair * 128, 128), 128)
        at_v = pl.ds(pl.multiple_of(2 * model + pair * 128, 128), 128)
        q, k, v = qkv[r, at_q], qkv[r, at_k], qkv[r, at_v]
        p = prob[step]
        dctx = stacked(cgrad[r, at_q])
        dprob = outer(dctx, v)
        dscore = (p * (dprob - jnp.sum(p * dprob, axis=-1, keepdims=True))).astype(BF16)
        dqkv[r, at_q] = (inner(beside(dscore), stacked(k)) * score_scale).astype(BF16)
        dqkv[r, at_k] = (under(dscore, stacked(q)) * score_scale).astype(BF16)
        dqkv[r, at_v] = under(p.astype(BF16), dctx).astype(BF16)

    flip(x)
    for which in range(3):
        product_tiles(dqkv.at[:, pl.ds(which * model, model)], model, square(which), 1)

    for which in range(2):
        @pl.loop(0, model // tile)
        def _(step, which=which):
            value = dqkv[:, pl.ds(pl.multiple_of(2 * which * model + step * tile, tile), tile)]
            sums[:, pl.ds(pl.multiple_of(which * model + step * tile, tile), tile)] = jnp.sum(
                value.astype(F32), axis=0, keepdims=True
            )

    @pl.loop(0, model // tile)
    def _(step):
        cols = at(step, tile)
        in_low[:, cols] = (work[:, cols] + outer(dqkv[...], wqkv[cols, :])).astype(BF16)

    for i in range(6):
        sums[:, pl.ds(2 * model + hidden + i * model, model)] = jnp.sum(accs[i], axis=0, keepdims=True)


def layer(chunk, x, og, valid, wqkv, wo, wu, wd, bqkv, bo, g1, s1, bu, bd, g2, s2):
    rows, model = x.shape
    hidden = wu.shape[1]
    hbm = pl.BlockSpec(memory_space=pl.ANY)
    vmem = pl.BlockSpec(memory_space=pltpu.VMEM)
    part = 2 * model + hidden
    steps = rows // CLUSTER * (model // 128)
    total = 8 * model + hidden
    return pl.pallas_call(
        functools.partial(layer_kernel, chunk),
        out_shape=(
            jax.ShapeDtypeStruct((rows, model), BF16),
            jax.ShapeDtypeStruct((rows, model), BF16),
            jax.ShapeDtypeStruct((2, model // chunk, chunk, part), BF16),
            jax.ShapeDtypeStruct((1, total), F32),
        ),
        in_specs=[vmem] * 15,
        out_specs=(vmem, vmem, hbm, vmem),
        scratch_shapes=[
            pltpu.VMEM((rows, 3 * model), BF16),
            pltpu.VMEM((rows, model), BF16),
            pltpu.VMEM((steps, 2 * CLUSTER, CLUSTER), F32),
            pltpu.VMEM((rows, model), F32),
            pltpu.VMEM((rows, 1), F32),
            pltpu.VMEM((rows, model), BF16),
            pltpu.VMEM((rows, hidden), BF16),
            pltpu.VMEM((rows, hidden), F32),
            pltpu.VMEM((rows, hidden), BF16),
            pltpu.VMEM((rows, model), F32),
            pltpu.VMEM((model, rows), BF16),
            pltpu.VMEM((rows, 3 * model), BF16),
            pltpu.VMEM((rows, model), BF16),
            pltpu.VMEM((rows, model), BF16),
            pltpu.VMEM((2, model // 2 // chunk, chunk, model), BF16),
            pltpu.VMEM((6, 8, model), F32),
            pltpu.SemaphoreType.DMA((2, 2)),
        ],
        compiler_params=pltpu.CompilerParams(vmem_limit_bytes=60 * MEBI),
    )(x, og, valid, wqkv, wo, wu, wd, bqkv, bo, g1, s1, bu, bd, g2, s2)


def exit_kernel(blocks, reduce, *refs):
    if reduce:
        (out_low, in_low, sources, grads, sums, out_home, in_home, grad_sum, sums_sum, *scratch) = refs
        (window, home, wsend, wrecv, csend, crecv, clocal, hsend, hrecv, hlocal, *scratch) = scratch
        (mine_g, from_core, got, gsend, grecv, glocal, rsend, rrecv, vrecv, vsend, vsem) = scratch
    else:
        (out_low, in_low, sources, out_home, in_home, *scratch) = refs
        (window, home, wsend, wrecv, csend, crecv, clocal, hsend, hrecv, hlocal) = scratch
    seq, core = lax.axis_index("seq"), lax.axis_index("head")
    rows, width = window.shape[2], window.shape[3]
    half = rows // 2
    partner = (seq, 1 - core)
    others = near(seq, core, blocks)
    bits = max(blocks.bit_length() - 1, 0)
    greetings = [(partner, None)] + [others[offset] for offset in OFFSETS[1:]]

    def across(bit):
        mask = 1 << bit
        return (seq + mask - 2 * mask * ((seq // mask) % 2), core)

    if reduce:
        greetings += [(across(bit), None) for bit in range(2, bits)]
    greet(greetings)

    mine = pl.ds(pl.multiple_of(core * width, width), width)
    theirs = pl.ds(pl.multiple_of((1 - core) * width, width), width)
    keep = pl.ds(pl.multiple_of(core * half, half), half)
    arrays = (out_low, in_low)
    firsts = []
    for which, array in enumerate(arrays):
        there = remote(
            array.at[:, theirs], window.at[which, 0, keep], csend.at[which], crecv.at[which], partner
        )
        here = pltpu.make_async_copy(array.at[:, mine], window.at[which, 0, keep], clocal.at[which])
        there.start()
        here.start()
        firsts.append((there, here))

    if reduce:
        parts = 2
        span = mine_g.shape[3] // parts
        core_moves = []
        for part in range(parts):
            cols = pl.ds(part * span, span)
            there = remote(
                grads.at[1 - core, :, :, cols], from_core.at[:, :, cols], gsend.at[part], grecv.at[part], partner
            )
            here = pltpu.make_async_copy(grads.at[core, :, :, cols], mine_g.at[0, :, :, cols], glocal.at[part])
            there.start()
            here.start()
            core_moves.append((there, here))

    def spread(which):
        for offset in OFFSETS[1:]:
            device, valid = others[offset]
            slot = SLOT[-offset]
            pl.when(valid)(
                remote(
                    window.at[which, 0], window.at[which, slot], wsend.at[which, slot], wrecv.at[which, slot], device
                ).start
            )

    for which in range(2):
        there, here = firsts[which]
        there.wait()
        here.wait()
        spread(which)

    def reduce_start(part, level):
        cols = pl.ds(part * span, span)
        order = orders[part]
        bit = order[level]
        own = (seq // (1 << bit)) % 2
        left = sorted(set(range(bits)) - set(order[:level]))
        low = 1 << left.index(bit)
        high = (1 << len(left)) // (2 * low)
        outs = []
        for top in range(high):
            src = mine_g.at[level % 2, pl.ds(pl.multiple_of((top * 2 + 1 - own) * low, low), low), :, cols]
            dst = got.at[pl.ds(base[level] + top * low, low), :, cols]
            outs.append(remote(src, dst, rsend.at[part, level, top], rrecv.at[part, level, top], across(bit)))
        return outs, own, low, high, cols

    def reduce_finish(part, level, state):
        outs, own, low, high, cols = state
        for copy in outs:
            copy.wait()
        for top in range(high):
            @pl.loop(0, low)
            def _(inside):
                held = mine_g[level % 2, (top * 2 + own) * low + inside, :, cols].astype(F32)
                other = got[base[level] + top * low + inside, :, cols].astype(F32)
                value = held + other
                if level == bits - 1:
                    grad_sum[:, cols] = value
                else:
                    mine_g[(level + 1) % 2, top * low + inside, :, cols] = value.astype(BF16)

    def pick(which):
        tile = 256
        for offset in OFFSETS:
            slot = SLOT[offset]

            def add(offset=offset, slot=slot):
                if offset != 0:
                    device, _ = others[offset]
                    remote(
                        window.at[which, 0],
                        window.at[which, slot],
                        wsend.at[which, slot],
                        wrecv.at[which, slot],
                        device,
                    ).wait_recv()

                @pl.loop(0, rows // tile)
                def _(step):
                    at = pl.ds(pl.multiple_of(step * tile, tile), tile)
                    places = lax.broadcasted_iota(jnp.int32, (tile, rows), 0) + (step * tile + seq * rows)
                    chosen = jnp.where(sources[slot] == places, 1.0, 0.0).astype(BF16)
                    part = inner(chosen, window[which, slot]).astype(BF16)
                    if offset == 0:
                        home[which, at, :] = part
                    else:
                        home[which, at, :] += part

            if offset == 0:
                add()
            else:
                pl.when(others[offset][1])(add)
        target = (out_home, in_home)[which]
        there = remote(home.at[which], target.at[:, mine], hsend.at[which], hrecv.at[which], partner)
        here = pltpu.make_async_copy(home.at[which], target.at[:, mine], hlocal.at[which])
        there.start()
        here.start()
        return there, here

    lasts = []
    if not reduce:
        lasts = [pick(0), pick(1)]
    else:
        orders = ([0, 1] + list(range(bits - 1, 1, -1)), [1, 0] + list(range(bits - 1, 1, -1)))
        base, count = [], 0
        for level in range(bits):
            base.append(count)
            count += blocks >> (level + 1)

        def sum_level(level):
            device = partner if level == 0 else across(level - 1)
            return remote(vsend.at[level], vrecv.at[level], vsem.at[0, level], vsem.at[1, level], device)

        def sum_start(level):
            if level == 0:
                vsend[0] = sums[...]
            sum_level(level).start()

        def sum_finish(level):
            sum_level(level).wait()
            value = vsend[level] + vrecv[level]
            if level == bits:
                sums_sum[...] = value
            else:
                vsend[level + 1] = value

        sum_start(0)
        states = [None] * parts
        for part in range(parts):
            there, here = core_moves[part]
            there.wait()
            here.wait()
            cols = pl.ds(part * span, span)

            @pl.loop(0, blocks)
            def _(inside):
                value = mine_g[0, inside, :, cols].astype(F32) + from_core[inside, :, cols].astype(F32)
                mine_g[0, inside, :, cols] = value.astype(BF16)

            states[part] = reduce_start(part, 0)
            for copy in states[part][0]:
                copy.start()
        sum_finish(0)
        sum_start(1)
        lasts.append(pick(0))
        for level in range(bits):
            for part in range(parts):
                reduce_finish(part, level, states[part])
                if level + 1 < bits:
                    states[part] = reduce_start(part, level + 1)
                    for copy in states[part][0]:
                        copy.start()
            sum_finish(level + 1)
            if level + 1 < bits:
                sum_start(level + 2)
            if level == 1:
                lasts.append(pick(1))
        if bits < 2:
            lasts.append(pick(1))

    for offset in OFFSETS[1:]:
        device, valid = others[offset]
        slot = SLOT[-offset]

        def finish(device=device, slot=slot):
            for which in range(2):
                remote(
                    window.at[which, 0], window.at[which, slot], wsend.at[which, slot], wrecv.at[which, slot], device
                ).wait_send()

        pl.when(valid)(finish)
    for there, here in lasts:
        there.wait()
        here.wait()


def leave(mesh, reduce, out_low, in_low, sources, grads, sums):
    half, model = out_low.shape
    rows, width = 2 * half, model // 2
    blocks = mesh.shape["seq"]
    slots = len(OFFSETS)
    hbm = pl.BlockSpec(memory_space=pl.ANY)
    vmem = pl.BlockSpec(memory_space=pltpu.VMEM)
    dma = pltpu.SemaphoreType.DMA
    out_shape = [jax.ShapeDtypeStruct((rows, model), BF16)] * 2
    out_specs = [hbm, hbm]
    in_specs = [hbm, hbm, vmem]
    args = [out_low, in_low, sources]
    scratch = [
        pltpu.VMEM((2, slots, rows, width), BF16),
        pltpu.VMEM((2, rows, width), BF16),
        dma((2, slots)),
        dma((2, slots)),
        dma((2,)),
        dma((2,)),
        dma((2,)),
        dma((2,)),
        dma((2,)),
        dma((2,)),
    ]
    if reduce:
        _, chunks, chunk, span = grads.shape
        bits = blocks.bit_length() - 1
        args += [grads, sums]
        in_specs += [hbm, vmem]
        out_shape += [jax.ShapeDtypeStruct((chunk, span), F32), jax.ShapeDtypeStruct(sums.shape, F32)]
        out_specs += [vmem, vmem]
        scratch += [
            pltpu.VMEM((2, blocks, chunk, span), BF16),
            pltpu.VMEM((blocks, chunk, span), BF16),
            pltpu.VMEM((blocks, chunk, span), BF16),
            dma((2,)),
            dma((2,)),
            dma((2,)),
            dma((2, bits, blocks // 2)),
            dma((2, bits, blocks // 2)),
            pltpu.VMEM((bits + 1,) + sums.shape, F32),
            pltpu.VMEM((bits + 1,) + sums.shape, F32),
            dma((2, bits + 1)),
        ]
    return pl.pallas_call(
        functools.partial(exit_kernel, blocks, reduce),
        out_shape=tuple(out_shape),
        in_specs=in_specs,
        out_specs=tuple(out_specs),
        scratch_shapes=scratch,
        compiler_params=pltpu.CompilerParams(
            collective_id=1, has_side_effects=True, vmem_limit_bytes=60 * MEBI
        ),
    )(*args)


FROM_X, FROM_Y, FROM_Z, FROM_LAST, RELAY = range(5)
OWN = -1
EXCHANGES = 4
CHUNKS = 2
GROUPS = 3
PARTS = 2
BITS = 4


def whole_kernel(
    blocks,
    tokens,
    out_grad,
    rel,
    source,
    valid,
    wq,
    wk,
    wv,
    wo_half,
    wu_half,
    wd_half,
    bq,
    bv,
    bu_half,
    bo,
    g1,
    s1,
    bd,
    g2,
    s2,
    out_home,
    in_home,
    grad_sum,
    sums_sum,
    win,
    wqkv,
    wo,
    wu,
    wd,
    bqkv,
    bu,
    stage,
    picked,
    block,
    sources,
    x,
    og,
    qkv,
    ctx,
    prob,
    hat1,
    inv1,
    low1,
    act,
    slope,
    work,
    flipped,
    flipped_x,
    low2,
    in_low,
    accs,
    mine_g,
    from_core,
    give,
    got0,
    got1,
    got2,
    got3,
    vsend,
    vrecv,
    wsend,
    wrecv,
    wlocal,
    xsend,
    xrecv,
    ssend,
    srecv,
    ssem,
    psend,
    precv,
    plocal,
    hsend,
    hrecv,
    hlocal,
    gsend,
    grecv,
    rsend,
    rrecv,
    vsem,
    credit,
):
    seq, core = lax.axis_index("seq"), lax.axis_index("head")
    px, py = seq % 2, (seq // 2) % 2
    rows, width = tokens.shape[0], picked.shape[2]
    half, model = x.shape
    hidden = wu.shape[1]
    clusters = half // CLUSTER
    pairs = model // 128
    part_rows = rows // CHUNKS
    tile = 256
    band = 64

    partner = (seq, 1 - core)
    x_next = seq + 1 - 2 * px
    y_next = seq + 2 - 4 * py
    z_to = seq + 4 - 8 * py
    z_from = seq - 4 + 8 * py
    to_ok = (z_to >= 0) & (z_to < blocks)
    from_ok = (z_from >= 0) & (z_from < blocks)
    level_chip = px == py
    off_chip = px != py
    last_next = x_next + core * (y_next - x_next)
    relay_send = (core == 1) & off_chip & from_ok
    relay_recv = (core == 1) & off_chip & to_ok
    later_ok = off_chip & (((core == 0) & from_ok) | ((core == 1) & to_ok))
    last_ok = off_chip | from_ok
    offsets = {
        OWN: 0,
        FROM_X: 1 - 2 * px,
        FROM_Y: 2 - 4 * py,
        FROM_Z: 4 * py - 2,
        FROM_LAST: 2 * px - 1,
    }
    arrived = {OWN: None, FROM_X: None, FROM_Y: None, FROM_Z: from_ok, FROM_LAST: last_ok}
    others = near(seq, core, blocks)

    def across(bit):
        mask = 1 << bit
        return (seq + mask - 2 * mask * ((seq // mask) % 2), core)

    greetings = [(partner, None), ((x_next, core), None), ((y_next, core), None)]
    greetings += [((z_to, core), to_ok), ((z_from, core), from_ok)]
    greetings += [others[offset] for offset in OFFSETS[1:]]
    greetings += [(across(bit), None) for bit in range(BITS)]
    greet(greetings)

    def at(step, size):
        return pl.ds(pl.multiple_of(step * size, size), size)

    def when(condition, action):
        if condition is None:
            action()
        else:
            pl.when(condition)(action)

    mine = at(core, width)
    theirs = at(1 - core, width)
    keep = at(core, half)
    other_rows = at(1 - core, half)

    def piece(chunk):
        return pl.ds(chunk * part_rows, part_rows)

    def own_rows(e, chunk):
        if e < 2:
            return (tokens, out_grad)[e].at[piece(chunk), mine]
        return block.at[e - 2, piece(chunk)]

    def hop(e, kind, chunk, src, there):
        return remote(
            src,
            win.at[e, kind, piece(chunk)],
            xsend.at[e, kind, chunk],
            xrecv.at[e, kind, chunk],
            (there, core),
        )

    def held(e, kind, chunk):
        return win.at[e, kind, piece(chunk)]

    def hop_x(e, chunk):
        return hop(e, FROM_X, chunk, own_rows(e, chunk), x_next)

    def hop_y(e, chunk):
        return hop(e, FROM_Y, chunk, own_rows(e, chunk), y_next)

    def hop_z(e, chunk):
        return hop(e, FROM_Z, chunk, held(e, FROM_Y, chunk), z_to)

    def hop_relay(e, chunk):
        return hop(e, RELAY, chunk, held(e, FROM_X, chunk), z_from)

    def hop_last_early(e, chunk):
        return hop(e, FROM_LAST, chunk, held(e, 1 - core, chunk), last_next)

    def hop_last_late(e, chunk):
        return hop(e, FROM_LAST, chunk, held(e, 2 + 2 * core, chunk), last_next)

    def send_own(e):
        for chunk in range(CHUNKS):
            hop_y(e, chunk).start()
            hop_x(e, chunk).start()

    def first_hop(e, chunk):
        hop_y(e, chunk).wait_recv()
        pl.when(to_ok)(hop_z(e, chunk).start)
        hop_x(e, chunk).wait_recv()
        pl.when(level_chip)(hop_last_early(e, chunk).start)
        pl.when(relay_send)(hop_relay(e, chunk).start)

    def second_hop(e, chunk):
        pl.when(from_ok)(hop_z(e, chunk).wait_recv)
        pl.when(relay_recv)(hop_relay(e, chunk).wait_recv)
        pl.when(later_ok)(hop_last_late(e, chunk).start)

    def last_hop(e, chunk):
        pl.when(last_ok)(hop_last_early(e, chunk).wait_recv)

    def all_sent(e):
        for chunk in range(CHUNKS):
            hop_x(e, chunk).wait_send()
            hop_y(e, chunk).wait_send()
            pl.when(to_ok)(hop_z(e, chunk).wait_send)
            pl.when(relay_send)(hop_relay(e, chunk).wait_send)
            pl.when(level_chip)(hop_last_early(e, chunk).wait_send)
            pl.when(later_ok)(hop_last_late(e, chunk).wait_send)

    def pick(e, units, fresh=False):
        which = e % 2
        moves = {}
        for index, (kind, chunk) in enumerate(units):
            if kind == OWN and e >= 2:
                continue
            src = own_rows(e, chunk) if kind == OWN else held(e, kind, chunk)
            moves[index] = pltpu.make_async_copy(src, stage.at[index], ssem.at[index])
            when(arrived[kind], moves[index].start)
        for index, (kind, chunk) in enumerate(units):

            def add(index=index, kind=kind, chunk=chunk):
                if index in moves:
                    moves[index].wait()
                offset = offsets[kind]

                @pl.loop(0, rows // tile)
                def _(step):
                    r = at(step, tile)
                    if e < 2:
                        wanted = rel[r, :] - (offset * rows + chunk * part_rows)
                        places = lax.broadcasted_iota(jnp.int32, (tile, part_rows), 1)
                        hit = places == wanted
                    else:
                        wanted = sources[offset + 2, :, pl.ds(chunk * part_rows, part_rows)]
                        places = lax.broadcasted_iota(jnp.int32, (tile, part_rows), 0)
                        hit = places == wanted - (step * tile + seq * rows)
                    chosen = jnp.where(hit, 1.0, 0.0).astype(BF16)
                    block_rows = stage[index] if index in moves else block[e - 2, piece(chunk), :]
                    value = inner(chosen, block_rows).astype(BF16)
                    if fresh and index == 0:
                        picked[which, r, :] = value
                    else:
                        picked[which, r, :] += value

            when(arrived[kind], add)

    def deliver(e):
        target = (x, og)[e]
        there = remote(picked.at[e, other_rows], target.at[:, mine], psend.at[e], precv.at[e], partner)
        here = pltpu.make_async_copy(picked.at[e, keep], target.at[:, mine], plocal.at[e])
        return there, here

    def collect(e):
        array = (og, in_low)[e - 2]
        there = remote(array.at[:, theirs], block.at[e - 2, keep], psend.at[e], precv.at[e], partner)
        here = pltpu.make_async_copy(array.at[:, mine], block.at[e - 2, keep], plocal.at[e])
        return there, here

    def bring_home(e):
        target = (out_home, in_home)[e - 2]
        there = remote(picked.at[e - 2], target.at[:, mine], hsend.at[e - 2], hrecv.at[e - 2], partner)
        here = pltpu.make_async_copy(picked.at[e - 2], target.at[:, mine], hlocal.at[e - 2])
        return there, here

    def begin(pair):
        for copy in pair:
            copy.start()

    def end(pair):
        for copy in pair:
            copy.wait()

    orders = ((0, 1, 3, 2), (1, 0, 3, 2))
    gots = (got0, got1, got2, got3)
    span = mine_g.shape[-1]
    part_span = span // PARTS

    def part_cols(part):
        return pl.ds(part * part_span, part_span)

    def own_bit(bit):
        return (seq // (1 << bit)) % 2

    def halving(group, part, level):
        order = orders[part]
        index = []
        for bit in (3, 2, 1, 0):
            if bit in order[:level]:
                index.append(own_bit(bit))
            elif bit == order[level]:
                index.append(1 - own_bit(bit))
            else:
                index.append(slice(None))
        src = mine_g.at[(group, *index, slice(None), part_cols(part))]
        dst = gots[level].at[group, part]
        return remote(
            src, dst, rsend.at[group, part, level], rrecv.at[group, part, level], across(order[level])
        )

    def halving_end(group, part, level):
        halving(group, part, level).wait()
        order = orders[part]
        left = [bit for bit in (3, 2, 1, 0) if bit not in order[: level + 1]]
        cols = part_cols(part)

        @pl.loop(0, 1 << len(left))
        def _(step):
            digits = {bit: (step // (1 << (len(left) - 1 - i))) % 2 for i, bit in enumerate(left)}
            place = [digits[bit] if bit in digits else own_bit(bit) for bit in (3, 2, 1, 0)]
            value = mine_g[(group, *place, slice(None), cols)].astype(F32)
            other = gots[level][(group, part, *[digits[bit] for bit in left])]
            value = value + other.astype(F32)
            if level == BITS - 1:
                grad_sum[:, pl.ds(group * span + part * part_span, part_span)] = value
            else:
                mine_g[(group, *place, slice(None), cols)] = value.astype(BF16)

    def advance(group, level):
        for part in range(PARTS):
            halving_end(group, part, level)
            if level + 1 < BITS:
                halving(group, part, level + 1).start()

    def core_move(group, part):
        cols = part_cols(part)
        return remote(
            give.at[:, :, :, :, :, cols],
            from_core.at[group % 2, :, :, :, :, :, cols],
            gsend.at[group, part],
            grecv.at[group, part],
            partner,
        )

    chunk_rows = give.shape[4]
    m_rows = model // 2

    def group_products(group, columns):
        if group == 2:
            pl.semaphore_wait(credit, 1)
        for side in (0, 1):
            for part in range(PARTS):
                if side == 0 and group > 0:
                    core_move(group - 1, part).wait_send()
                if side == 1:
                    core_move(group, part).wait_recv()
                place = 0
                for left, right, start, size in columns(part, (1 - core, core)[side]):
                    cols = pl.ds(part * part_span + place, size)
                    place += size

                    @pl.loop(0, 2)
                    def _(m, left=left, right=right, start=start, size=size, cols=cols):
                        value = inner(left[at(m, m_rows), :], right[:, pl.ds(start, size)])
                        value = value.reshape(2, 2, 2, chunk_rows, size)
                        if side == 0:
                            give[m, :, :, :, :, cols] = value.astype(BF16)
                        else:
                            value = value + from_core[group % 2, m, :, :, :, :, cols].astype(F32)
                            mine_g[group, m, :, :, :, :, cols] = value.astype(BF16)

                if side == 0:
                    core_move(group, part).start()
                else:
                    halving(group, part, 0).start()
        if group == 0:
            pl.semaphore_signal(credit, inc=1, device_id=partner, device_id_type=MESH)

    part_out = 2 * model + hidden

    def sum_move(level):
        device = partner if level == 0 else across(level - 1)
        return remote(vsend.at[level], vrecv.at[level], vsem.at[0, level], vsem.at[1, level], device)

    def sum_next(level):
        sum_move(level).wait()
        value = vsend[level] + vrecv[level]
        if level == BITS:
            sums_sum[...] = value
        else:
            vsend[level + 1] = value
            sum_move(level + 1).start()

    send_own(0)
    sources[2] = source[...]
    tinies = []
    for offset in OFFSETS[1:]:
        device, there_ok = others[offset]
        out = remote(source, sources.at[2 - offset], ssend.at[2 - offset], srecv.at[2 - offset], device)
        back = remote(source, sources.at[2 + offset], ssend.at[2 + offset], srecv.at[2 + offset], device)
        pl.when(there_ok)(out.start)
        tinies.append((there_ok, out, back))

    wide, deep = wq.shape[1], wd_half.shape[0]
    pieces = []
    for i, array in enumerate((wq, wk, wv)):
        pieces.append((array, wqkv.at[:, pl.ds(pl.multiple_of(i * model + core * wide, wide), wide)]))
    pieces.append((wo_half, wo.at[at(core, wide), :]))
    pieces.append((wu_half, wu.at[:, at(core, deep)]))
    pieces.append((wd_half, wd.at[at(core, deep), :]))
    pieces.append((bq, bqkv.at[:, at(core, wide)]))
    pieces.append((bv, bqkv.at[:, pl.ds(pl.multiple_of(2 * model + core * wide, wide), wide)]))
    pieces.append((bu_half, bu.at[:, at(core, deep)]))
    weights = []
    for i, (array, place) in enumerate(pieces):
        there = remote(array, place, wsend.at[i], wrecv.at[i], partner)
        here = pltpu.make_async_copy(array, place, wlocal.at[i])
        begin((there, here))
        weights.append((there, here))
    bqkv[:, pl.ds(model, model)] = jnp.zeros((1, model), F32)

    pick(0, [(OWN, 0), (OWN, 1)], fresh=True)
    pick(1, [(OWN, 0), (OWN, 1)], fresh=True)
    first_hop(0, 0)
    pick(0, [(FROM_X, 0), (FROM_Y, 0)])
    first_hop(0, 1)
    second_hop(0, 0)
    pick(0, [(FROM_X, 1), (FROM_Y, 1), (FROM_Z, 0)])
    second_hop(0, 1)
    send_own(1)
    last_hop(0, 0)
    pick(0, [(FROM_Z, 1), (FROM_LAST, 0)])
    last_hop(0, 1)
    pick(0, [(FROM_LAST, 1)])
    begin(deliver(0))
    for pair in weights:
        end(pair)
    end(deliver(0))

    lanes = lax.broadcasted_iota(jnp.int32, (CLUSTER, 128), 1)
    first_f = jnp.where(lanes < HEAD_DIM, 1.0, 0.0)
    first = first_f.astype(BF16)
    second = (1.0 - first_f).astype(BF16)

    def stacked(pair):
        return jnp.concatenate([pair * first, pair * second], axis=0)

    def beside(tall):
        return jnp.concatenate([tall[:CLUSTER], tall[CLUSTER:]], axis=1)

    @pl.loop(0, 3 * model // tile)
    def _(step):
        cols = at(step, tile)
        qkv[:, cols] = (inner(x[...], wqkv[:, cols]) + bqkv[:, cols]).astype(BF16)

    first_hop(1, 0)

    @pl.loop(0, clusters)
    def _(cluster):
        r = at(cluster, CLUSTER)
        for pair in range(pairs):
            q = qkv[r, pl.ds(pair * 128, 128)]
            k = qkv[r, pl.ds(model + pair * 128, 128)]
            v = qkv[r, pl.ds(2 * model + pair * 128, 128)]
            scores = outer(stacked(q), k) * score_scale
            scores = jnp.where(valid[cluster] > 0.5, scores, masked_score)
            top = jnp.max(scores, axis=-1, keepdims=True)
            weight = jnp.exp(scores - top)
            p = weight * (1.0 / jnp.sum(weight, axis=-1, keepdims=True))
            prob[cluster * pairs + pair] = p
            ctx[r, pl.ds(pair * 128, 128)] = inner(beside(p.astype(BF16)), stacked(v)).astype(BF16)

    first_hop(1, 1)

    @pl.loop(0, model // tile)
    def _(step):
        cols = at(step, tile)
        hat1[:, cols] = inner(ctx[...], wo[:, cols]) + x[:, cols].astype(F32) + bo[:, cols]

    @pl.loop(0, half // band)
    def _(step):
        r = at(step, band)
        h = hat1[r, :]
        centered = h - jnp.mean(h, axis=-1, keepdims=True)
        inv = lax.rsqrt(jnp.mean(centered * centered, axis=-1, keepdims=True) + norm_eps)
        hat = centered * inv
        hat1[r, :] = hat
        inv1[r, :] = inv
        low1[r, :] = (hat * g1[...] + s1[...]).astype(BF16)

    second_hop(1, 0)

    @pl.loop(0, hidden // tile)
    def _(step):
        cols = at(step, tile)
        pre = inner(low1[...], wu[:, cols]) + bu[:, cols]
        cdf = 0.5 * (1.0 + lax.erf(pre * root_half))
        act[:, cols] = (pre * cdf).astype(BF16)
        slope[:, cols] = cdf + pre * jnp.exp(-0.5 * pre * pre) * inv_root_tau

    second_hop(1, 1)

    @pl.loop(0, model // tile)
    def _(step):
        cols = at(step, tile)
        norm = hat1[:, cols] * g1[:, cols] + s1[:, cols]
        work[:, cols] = inner(act[...], wd[:, cols]) + norm + bd[:, cols]

    pick(1, [(FROM_X, 0), (FROM_Y, 0), (FROM_X, 1), (FROM_Y, 1)])
    last_hop(1, 0)
    last_hop(1, 1)
    pick(1, [(FROM_Z, 0), (FROM_Z, 1), (FROM_LAST, 0), (FROM_LAST, 1)])
    begin(deliver(1))
    end(deliver(1))

    accs[...] = jnp.zeros_like(accs)

    @pl.loop(0, half // band)
    def _(step):
        r = at(step, band)
        h = work[r, :]
        centered = h - jnp.mean(h, axis=-1, keepdims=True)
        inv = lax.rsqrt(jnp.mean(centered * centered, axis=-1, keepdims=True) + norm_eps)
        hat = centered * inv
        grad = og[r, :].astype(F32)
        og[r, :] = (hat * g2[...] + s2[...]).astype(BF16)
        accs[4] += fold_rows(grad * hat)
        accs[5] += fold_rows(grad)
        scaled = grad * g2[...]
        back = inv * (
            scaled
            - jnp.mean(scaled, axis=-1, keepdims=True)
            - hat * jnp.mean(scaled * hat, axis=-1, keepdims=True)
        )
        accs[3] += fold_rows(back)
        work[r, :] = back
        low2[r, :] = back.astype(BF16)

    begin(collect(2))

    def flip(source_rows, target=flipped):
        @pl.loop(0, model // 128)
        def _(step):
            target[at(step, 128), :] = source_rows[:, at(step, 128)].T

    def long_columns(part, side):
        start = pl.multiple_of(side * span + part * part_span, part_span)
        return [(flipped, act, start, part_span)]

    flip(low2)
    end(collect(2))
    send_own(2)
    group_products(0, long_columns)

    @pl.loop(0, hidden // tile)
    def _(step):
        cols = at(step, tile)
        back = outer(low2[...], wd[cols, :]) * slope[:, cols]
        back = back.astype(BF16)
        act[:, cols] = back
        vsend[0, :, pl.ds(pl.multiple_of(2 * model + step * tile, tile), tile)] = jnp.sum(
            back.astype(F32), axis=0, keepdims=True
        )

    first_hop(2, 0)
    flip(low1)
    group_products(1, long_columns)
    first_hop(2, 1)

    @pl.loop(0, model // tile)
    def _(step):
        cols = at(step, tile)
        work[:, cols] += outer(act[...], wu[cols, :])

    @pl.loop(0, half // band)
    def _(step):
        r = at(step, band)
        grad = work[r, :]
        hat = hat1[r, :]
        accs[1] += fold_rows(grad * hat)
        accs[2] += fold_rows(grad)
        scaled = grad * g1[...]
        back = inv1[r, :] * (
            scaled
            - jnp.mean(scaled, axis=-1, keepdims=True)
            - hat * jnp.mean(scaled * hat, axis=-1, keepdims=True)
        )
        accs[0] += fold_rows(back)
        work[r, :] = back
        low2[r, :] = back.astype(BF16)

    second_hop(2, 0)

    @pl.loop(0, model // tile)
    def _(step):
        cols = at(step, tile)
        low1[:, cols] = outer(low2[...], wo[cols, :]).astype(BF16)

    advance(0, 0)
    second_hop(2, 1)

    @pl.loop(0, clusters)
    def _(cluster):
        r = at(cluster, CLUSTER)
        for pair in range(pairs):
            at_q = pl.ds(pair * 128, 128)
            at_k = pl.ds(model + pair * 128, 128)
            at_v = pl.ds(2 * model + pair * 128, 128)
            q, k, v = qkv[r, at_q], qkv[r, at_k], qkv[r, at_v]
            p = prob[cluster * pairs + pair]
            dctx = stacked(low1[r, at_q])
            dprob = outer(dctx, v)
            dscore = (p * (dprob - jnp.sum(p * dprob, axis=-1, keepdims=True))).astype(BF16)
            act[r, at_q] = (inner(beside(dscore), stacked(k)) * score_scale).astype(BF16)
            act[r, at_k] = (under(dscore, stacked(q)) * score_scale).astype(BF16)
            act[r, at_v] = under(p.astype(BF16), dctx).astype(BF16)

    dqkv = act.at[:, pl.ds(0, 3 * model)]

    @pl.loop(0, model // tile)
    def _(step):
        cols = at(step, tile)
        in_low[:, cols] = (work[:, cols] + outer(dqkv[...], wqkv[cols, :])).astype(BF16)

    begin(collect(3))
    advance(0, 1)
    advance(1, 0)
    end(collect(3))
    send_own(3)

    for which in range(2):
        @pl.loop(0, model // tile)
        def _(step, which=which):
            value = act[:, pl.ds(pl.multiple_of(2 * which * model + step * tile, tile), tile)]
            vsend[0, :, pl.ds(pl.multiple_of(which * model + step * tile, tile), tile)] = jnp.sum(
                value.astype(F32), axis=0, keepdims=True
            )

    for i in range(6):
        vsend[0, :, pl.ds(part_out + i * model, model)] = jnp.sum(accs[i], axis=0, keepdims=True)
    sum_move(0).start()

    flip(low2)
    flip(x, flipped_x)

    def square_columns(part, side):
        start = pl.multiple_of(side * width, width)
        if part == 0:
            return [(flipped, ctx, start, width), (flipped_x, act, start, width)]
        return [
            (flipped_x, act, pl.multiple_of(model + side * width, width), width),
            (flipped_x, act, pl.multiple_of(2 * model + side * width, width), width),
        ]

    group_products(2, square_columns)
    first_hop(3, 0)
    advance(0, 2)
    advance(1, 1)
    first_hop(3, 1)
    second_hop(3, 0)
    sum_next(0)
    for there_ok, out, back in tinies:

        def finish(out=out, back=back):
            out.wait_send()
            back.wait_recv()

        pl.when(there_ok)(finish)
    last_hop(2, 0)
    last_hop(2, 1)
    pick(2, [(OWN, 0), (OWN, 1)], fresh=True)
    pick(2, [(FROM_X, 0), (FROM_Y, 0), (FROM_X, 1), (FROM_Y, 1)])
    second_hop(3, 1)
    sum_next(1)
    advance(2, 0)
    pick(2, [(FROM_Z, 0), (FROM_Z, 1), (FROM_LAST, 0), (FROM_LAST, 1)])
    begin(bring_home(2))
    advance(0, 3)
    advance(1, 2)
    sum_next(2)
    pick(3, [(OWN, 0), (OWN, 1)], fresh=True)
    pick(3, [(FROM_X, 0), (FROM_Y, 0), (FROM_X, 1), (FROM_Y, 1)])
    advance(2, 1)
    advance(1, 3)
    sum_next(3)
    last_hop(3, 0)
    pick(3, [(FROM_Z, 0), (FROM_Z, 1), (FROM_LAST, 0)])
    last_hop(3, 1)
    pick(3, [(FROM_LAST, 1)])
    begin(bring_home(3))
    advance(2, 2)
    sum_next(4)
    advance(2, 3)
    for part in range(PARTS):
        core_move(2, part).wait_send()
    for e in range(EXCHANGES):
        all_sent(e)
    end(bring_home(2))
    end(bring_home(3))


def whole(mesh, *args):
    tokens, wu_half = args[0], args[9]
    rows, model = tokens.shape
    half, width = rows // 2, model // 2
    hidden = 2 * wu_half.shape[1]
    blocks = mesh.shape["seq"]
    hbm = pl.BlockSpec(memory_space=pl.ANY)
    vmem = pl.BlockSpec(memory_space=pltpu.VMEM)
    dma = pltpu.SemaphoreType.DMA
    chunk = model // blocks
    span = 4 * width
    part_span = span // PARTS
    steps = half // CLUSTER * (model // 128)
    total = 8 * model + hidden
    cube = (2, 2, 2, 2)
    return pl.pallas_call(
        functools.partial(whole_kernel, blocks),
        out_shape=(
            jax.ShapeDtypeStruct((rows, model), BF16),
            jax.ShapeDtypeStruct((rows, model), BF16),
            jax.ShapeDtypeStruct((chunk, GROUPS * span), F32),
            jax.ShapeDtypeStruct((1, total), F32),
            jax.ShapeDtypeStruct((EXCHANGES, 5, rows, width), BF16),
        ),
        in_specs=[hbm, hbm, vmem, vmem, vmem] + [hbm] * 9 + [vmem] * 6,
        out_specs=(hbm, hbm, vmem, vmem, hbm),
        scratch_shapes=[
            pltpu.VMEM((model, 3 * model), BF16),
            pltpu.VMEM((model, model), BF16),
            pltpu.VMEM((model, hidden), BF16),
            pltpu.VMEM((hidden, model), BF16),
            pltpu.VMEM((1, 3 * model), F32),
            pltpu.VMEM((1, hidden), F32),
            pltpu.VMEM((4, rows // CHUNKS, width), BF16),
            pltpu.VMEM((2, rows, width), BF16),
            pltpu.VMEM((2, rows, width), BF16),
            pltpu.VMEM((5, 1, rows), jnp.int32),
            pltpu.VMEM((half, model), BF16),
            pltpu.VMEM((half, model), BF16),
            pltpu.VMEM((half, 3 * model), BF16),
            pltpu.VMEM((half, model), BF16),
            pltpu.VMEM((steps, 2 * CLUSTER, CLUSTER), F32),
            pltpu.VMEM((half, model), F32),
            pltpu.VMEM((half, 1), F32),
            pltpu.VMEM((half, model), BF16),
            pltpu.VMEM((half, hidden), BF16),
            pltpu.VMEM((half, hidden), F32),
            pltpu.VMEM((half, model), F32),
            pltpu.VMEM((model, half), BF16),
            pltpu.VMEM((model, half), BF16),
            pltpu.VMEM((half, model), BF16),
            pltpu.VMEM((half, model), BF16),
            pltpu.VMEM((6, 8, model), F32),
            pltpu.VMEM((GROUPS,) + cube + (chunk, span), BF16),
            pltpu.VMEM((2,) + cube + (chunk, span), BF16),
            pltpu.VMEM(cube + (chunk, span), BF16),
            pltpu.VMEM((GROUPS, PARTS, 2, 2, 2, chunk, part_span), BF16),
            pltpu.VMEM((GROUPS, PARTS, 2, 2, chunk, part_span), BF16),
            pltpu.VMEM((GROUPS, PARTS, 2, chunk, part_span), BF16),
            pltpu.VMEM((GROUPS, PARTS, chunk, part_span), BF16),
            pltpu.VMEM((BITS + 1, 1, total), F32),
            pltpu.VMEM((BITS + 1, 1, total), F32),
            dma((9,)),
            dma((9,)),
            dma((9,)),
            dma((EXCHANGES, 5, CHUNKS)),
            dma((EXCHANGES, 5, CHUNKS)),
            dma((5,)),
            dma((5,)),
            dma((4,)),
            dma((EXCHANGES,)),
            dma((EXCHANGES,)),
            dma((EXCHANGES,)),
            dma((2,)),
            dma((2,)),
            dma((2,)),
            dma((GROUPS, PARTS)),
            dma((GROUPS, PARTS)),
            dma((GROUPS, PARTS, BITS)),
            dma((GROUPS, PARTS, BITS)),
            dma((2, BITS + 1)),
            pltpu.SemaphoreType.REGULAR,
        ],
        compiler_params=pltpu.CompilerParams(
            collective_id=2, has_side_effects=True, vmem_limit_bytes=64 * MEBI
        ),
    )(*args)[:4]


def body(
    mesh,
    tokens,
    out_grad,
    doc_lengths,
    cluster_perm,
    query_weight,
    query_bias,
    key_weight,
    value_weight,
    value_bias,
    output_weight,
    output_bias,
    first_gain,
    first_shift,
    up_weight,
    up_bias,
    down_weight,
    down_bias,
    second_gain,
    second_shift,
):
    rows, model = tokens.shape
    half = rows // 2
    hidden = 2 * up_weight.shape[1]
    blocks = mesh.shape["seq"]
    seq, core = lax.axis_index("seq"), lax.axis_index("head")
    positions = seq * rows + jnp.arange(rows, dtype=jnp.int32)
    slot_start, slot_length = doc_lookup(doc_lengths, positions)
    source = slot_start + cluster_perm
    valid = (cluster_perm < slot_length).astype(F32).reshape(2, half // CLUSTER, 1, CLUSTER)
    valid = lax.dynamic_index_in_dim(valid, core, 0, keepdims=False)

    def row(v):
        return v.reshape(1, -1)

    rel = (source - seq * rows).reshape(rows, 1)
    chunk = model // blocks
    part_q, part_h = model // 2, hidden // 2
    order = ("q", "k", "v", "o", "up", "down")
    if blocks == 1 << BITS and chunk % 16 == 0 and hidden == 4 * model:
        order = ("down", "up", "o", "q", "k", "v")
        out_home, in_home, grad_sum, sums = whole(
            mesh,
            tokens,
            out_grad,
            rel,
            row(source),
            valid,
            query_weight,
            key_weight,
            value_weight,
            output_weight,
            up_weight,
            down_weight,
            row(query_bias),
            row(value_bias),
            row(up_bias),
            row(output_bias),
            row(first_gain),
            row(first_shift),
            row(down_bias),
            row(second_gain),
            row(second_shift),
        )
    else:
        x, og, sources, wqkv, wo, wu, wd, bqkv, bu = entry(
            mesh,
            tokens,
            out_grad,
            rel,
            row(source),
            query_weight,
            key_weight,
            value_weight,
            output_weight,
            up_weight,
            down_weight,
            row(query_bias),
            row(value_bias),
            row(up_bias),
        )
        no_key = (jnp.arange(3 * model) // model != 1)[None, :]
        bqkv = jnp.where(no_key, bqkv, 0.0)
        reduce = chunk % 16 == 0 and blocks >= 4 and blocks & (blocks - 1) == 0
        out_low, in_low, grads, sums = layer(
            chunk if reduce else 48,
            x,
            og,
            valid,
            wqkv,
            wo,
            wu,
            wd,
            bqkv,
            row(output_bias),
            row(first_gain),
            row(first_shift),
            bu,
            row(down_bias),
            row(second_gain),
            row(second_shift),
        )
        if reduce:
            out_home, in_home, grad_sum, sums = leave(mesh, True, out_low, in_low, sources, grads, sums)
        else:
            out_home, in_home = leave(mesh, False, out_low, in_low, sources, None, None)
            sums = lax.psum(sums, ("seq", "head"))
            grads = grads.reshape(2, model, -1)
            grads = lax.psum_scatter(grads.astype(F32), "head", scatter_dimension=0, tiled=True)[0]
            grad_sum = lax.psum_scatter(grads, "seq", scatter_dimension=0, tiled=True)
    grad_of, place = {}, 0
    for name in order:
        size = part_h if name in ("up", "down") else part_q
        grad_of[name] = grad_sum[:, place : place + size]
        place += size
    sums = sums[0]

    def mine(start, size):
        return lax.dynamic_slice(sums, (start + core * size,), (size,))

    def block(index):
        return lax.dynamic_slice(sums, (2 * model + hidden + index * model + seq * chunk,), (chunk,))

    return (
        out_home.astype(F32),
        in_home.astype(F32),
        grad_of["q"],
        mine(0, part_q),
        grad_of["k"],
        grad_of["v"],
        mine(model, part_q),
        grad_of["o"].T,
        block(0),
        block(1),
        block(2),
        grad_of["up"],
        mine(2 * model, part_h),
        grad_of["down"].T,
        block(3),
        block(4),
        block(5),
    )


def solution(mesh):
    placed = (
        P("seq", None),
        P("seq", None),
        P(),
        P("seq"),
        P(None, "head"),
        P("head"),
        P(None, "head"),
        P(None, "head"),
        P("head"),
        P("head", None),
        P(),
        P(),
        P(),
        P(None, "head"),
        P("head"),
        P("head", None),
        P(),
        P(),
        P(),
    )
    return jax.shard_map(
        functools.partial(body, mesh),
        mesh=mesh,
        in_specs=placed,
        out_specs=(
            P("seq", None),
            P("seq", None),
            P("seq", "head"),
            P("head"),
            P("seq", "head"),
            P("seq", "head"),
            P("head"),
            P("head", "seq"),
            P("seq"),
            P("seq"),
            P("seq"),
            P("seq", "head"),
            P("head"),
            P("head", "seq"),
            P("seq"),
            P("seq"),
            P("seq"),
        ),
        check_vma=False,
    )
```

```python
import functools

import jax
import jax.numpy as jnp
from jax import lax
from jax.experimental import pallas as pl
from jax.experimental.pallas import tpu as pltpu
from jax.sharding import PartitionSpec as P

MESH = pl.DeviceIdType.MESH
HEAD_DIM = 64
CLUSTER = 128
OFFSETS = (0, 1, -1, 2, -2)
SLOT = {offset: slot for slot, offset in enumerate(OFFSETS)}
MEBI = 1 << 20

norm_eps = 1e-12
masked_score = -1e30
root_half = 0.7071067811865476
inv_root_tau = 0.3989422804014327
score_scale = HEAD_DIM ** (-0.5)

F32 = jnp.float32
BF16 = jnp.bfloat16


def doc_lookup(doc_lengths, positions):
    padded = (doc_lengths + CLUSTER - 1) // CLUSTER * CLUSTER
    starts = jnp.cumsum(padded) - padded
    doc_of = jnp.sum((starts[None, :] <= positions[:, None]).astype(jnp.int32), axis=1) - 1
    picked = jnp.arange(starts.shape[0], dtype=jnp.int32)[None, :] == doc_of[:, None]
    slot_start = jnp.sum(jnp.where(picked, starts[None, :], 0), axis=1)
    slot_length = jnp.sum(jnp.where(picked, doc_lengths[None, :], 0), axis=1)
    return (slot_start, slot_length)


def remote(src, dst, send, recv, device):
    return pltpu.make_async_remote_copy(
        src_ref=src, dst_ref=dst, send_sem=send, recv_sem=recv, device_id=device, device_id_type=MESH
    )


def greet(devices):
    pl.semaphore_wait(pltpu.get_barrier_semaphore(), greet_start(devices))


def greet_start(devices):
    barrier = pltpu.get_barrier_semaphore()
    count = 0
    for device, valid in devices:
        def hello(device=device):
            pl.semaphore_signal(barrier, inc=1, device_id=device, device_id_type=MESH)

        if valid is None:
            hello()
            count = count + 1
        else:
            pl.when(valid)(hello)
            count = count + valid.astype(jnp.int32)
    return count


def near(seq, core, blocks):
    out = {}
    for offset in OFFSETS[1:]:
        there = seq + offset
        out[offset] = ((there, core), (there >= 0) & (there < blocks))
    return out


def inner(left, right):
    return lax.dot_general(left, right, (((1,), (0,)), ((), ())), preferred_element_type=F32)


def outer(left, right):
    return lax.dot_general(left, right, (((1,), (1,)), ((), ())), preferred_element_type=F32)


def under(left, right):
    return lax.dot_general(left, right, (((0,), (0,)), ((), ())), preferred_element_type=F32)


def entry_kernel(
    blocks,
    tokens,
    out_grad,
    rel,
    source,
    wq,
    wk,
    wv,
    wo,
    wu,
    wd,
    bq,
    bv,
    bu,
    slot_tokens,
    slot_grad,
    sources,
    wqkv_full,
    wo_full,
    wu_full,
    wd_full,
    bqkv_full,
    bu_full,
    window,
    total,
    picked,
    source_win,
    wsend,
    wrecv,
    wlocal,
    send,
    recv,
    local,
    ssend,
    srecv,
    psend,
    precv,
    plocal,
):
    seq, core = lax.axis_index("seq"), lax.axis_index("head")
    rows, width = window.shape[2], window.shape[3]
    half = rows // 2
    partner = (seq, 1 - core)
    others = near(seq, core, blocks)
    greet([(partner, None)] + [others[offset] for offset in OFFSETS[1:]])

    mine = pl.ds(pl.multiple_of(core * width, width), width)
    arrays = (tokens, out_grad)
    locals_ = []
    for which, array in enumerate(arrays):
        for offset in OFFSETS[1:]:
            device, valid = others[offset]
            slot = SLOT[-offset]
            copy = remote(
                array.at[:, mine], window.at[which, slot], send.at[which, slot], recv.at[which, slot], device
            )
            pl.when(valid)(copy.start)
            if which == 0:
                tiny = remote(source, source_win.at[slot], ssend.at[slot], srecv.at[slot], device)
                pl.when(valid)(tiny.start)
        own = pltpu.make_async_copy(array.at[:, mine], window.at[which, 0], local.at[which])
        own.start()
        locals_.append(own)

    wide, deep = wq.shape[1], wd.shape[0]
    model = wq.shape[0]
    at_core = pl.multiple_of(core * wide, wide)
    at_deep = pl.multiple_of(core * deep, deep)
    pieces = []
    for i, array in enumerate((wq, wk, wv)):
        at = pl.multiple_of(i * model + core * wide, wide)
        pieces.append((array, wqkv_full.at[:, pl.ds(at, wide)]))
    pieces.append((wo, wo_full.at[pl.ds(at_core, wide), :]))
    pieces.append((wu, wu_full.at[:, pl.ds(at_deep, deep)]))
    pieces.append((wd, wd_full.at[pl.ds(at_deep, deep), :]))
    pieces.append((bq, bqkv_full.at[:, pl.ds(at_core, wide)]))
    pieces.append((bv, bqkv_full.at[:, pl.ds(pl.multiple_of(2 * model + core * wide, wide), wide)]))
    pieces.append((bu, bu_full.at[:, pl.ds(at_deep, deep)]))
    moves = []
    for i, (array, place) in enumerate(pieces):
        there = remote(array, place, wsend.at[i], wrecv.at[i], partner)
        here = pltpu.make_async_copy(array, place, wlocal.at[i])
        there.start()
        here.start()
        moves.append((there, here))

    source_win[0] = source[...]
    for offset in OFFSETS[1:]:

        def blank(slot=SLOT[offset]):
            source_win[slot] = jnp.full(source.shape, -1, jnp.int32)

        pl.when(jnp.logical_not(others[offset][1]))(blank)
    tile = 256
    outs = (slot_tokens, slot_grad)
    finals = []
    for which in range(2):
        locals_[which].wait()
        for offset in OFFSETS:
            slot = SLOT[offset]

            def add(which=which, offset=offset, slot=slot):
                if offset != 0:
                    device, _ = others[offset]
                    remote(
                        arrays[which].at[:, mine],
                        window.at[which, slot],
                        send.at[which, slot],
                        recv.at[which, slot],
                        device,
                    ).wait_recv()

                @pl.loop(0, rows // tile)
                def _(step):
                    at = pl.ds(pl.multiple_of(step * tile, tile), tile)
                    wanted = rel[at, :] - offset * rows
                    lanes = lax.broadcasted_iota(jnp.int32, (tile, rows), 1)
                    chosen = jnp.where(lanes == wanted, 1.0, 0.0).astype(BF16)
                    part = inner(chosen, window[which, slot])
                    if offset == 0:
                        total[at, :] = part
                    else:
                        total[at, :] += part

            if offset == 0:
                add()
            else:
                pl.when(others[offset][1])(add)
        picked[which] = total[...].astype(BF16)
        keep = pl.ds(pl.multiple_of(core * half, half), half)
        give = pl.ds(pl.multiple_of((1 - core) * half, half), half)
        there = remote(
            picked.at[which, give], outs[which].at[:, mine], psend.at[which], precv.at[which], partner
        )
        here = pltpu.make_async_copy(picked.at[which, keep], outs[which].at[:, mine], plocal.at[which])
        there.start()
        here.start()
        finals.append((there, here))

    for offset in OFFSETS[1:]:
        device, valid = others[offset]

        def finish(offset=offset, device=device):
            for which in range(2):
                slot = SLOT[-offset]
                remote(
                    arrays[which].at[:, mine],
                    window.at[which, slot],
                    send.at[which, slot],
                    recv.at[which, slot],
                    device,
                ).wait_send()
            slot = SLOT[-offset]
            remote(source, source_win.at[slot], ssend.at[slot], srecv.at[slot], device).wait_send()
            slot = SLOT[offset]
            remote(source, source_win.at[slot], ssend.at[slot], srecv.at[slot], device).wait_recv()

        pl.when(valid)(finish)
    sources[...] = source_win[...]
    for there, here in moves + finals:
        there.wait()
        here.wait()


def entry(mesh, tokens, out_grad, rel, source, wq, wk, wv, wo, wu, wd, bq, bv, bu):
    rows, model = tokens.shape
    width = model // 2
    hidden = 2 * wu.shape[1]
    hbm = pl.BlockSpec(memory_space=pl.ANY)
    vmem = pl.BlockSpec(memory_space=pltpu.VMEM)
    slots = len(OFFSETS)
    dma = pltpu.SemaphoreType.DMA
    return pl.pallas_call(
        functools.partial(entry_kernel, mesh.shape["seq"]),
        out_shape=(
            jax.ShapeDtypeStruct((rows // 2, model), BF16),
            jax.ShapeDtypeStruct((rows // 2, model), BF16),
            jax.ShapeDtypeStruct((slots, 1, rows), jnp.int32),
            jax.ShapeDtypeStruct((model, 3 * model), BF16),
            jax.ShapeDtypeStruct((model, model), BF16),
            jax.ShapeDtypeStruct((model, hidden), BF16),
            jax.ShapeDtypeStruct((hidden, model), BF16),
            jax.ShapeDtypeStruct((1, 3 * model), F32),
            jax.ShapeDtypeStruct((1, hidden), F32),
        ),
        in_specs=[hbm, hbm, vmem, vmem] + [hbm] * 9,
        out_specs=(hbm, hbm, vmem) + (hbm,) * 6,
        scratch_shapes=[
            pltpu.VMEM((2, slots, rows, width), BF16),
            pltpu.VMEM((rows, width), F32),
            pltpu.VMEM((2, rows, width), BF16),
            pltpu.VMEM((slots, 1, rows), jnp.int32),
            dma((9,)),
            dma((9,)),
            dma((9,)),
            dma((2, slots)),
            dma((2, slots)),
            dma((2,)),
            dma((slots,)),
            dma((slots,)),
            dma((2,)),
            dma((2,)),
            dma((2,)),
        ],
        compiler_params=pltpu.CompilerParams(
            collective_id=0, has_side_effects=True, vmem_limit_bytes=40 * MEBI
        ),
    )(tokens, out_grad, rel, source, wq, wk, wv, wo, wu, wd, bq, bv, bu)


def fold_rows(values):
    return jnp.sum(values.reshape(values.shape[0] // 8, 8, values.shape[1]), axis=0)


def layer_kernel(
    chunk,
    x,
    og,
    valid,
    wqkv,
    wo,
    wu,
    wd,
    bqkv,
    bo,
    g1,
    s1,
    bu,
    bd,
    g2,
    s2,
    out_low,
    in_low,
    grads,
    sums,
    qkv,
    ctx,
    prob,
    hat1,
    inv1,
    low1,
    act,
    slope,
    pre_low,
    work,
    flipped,
    dqkv,
    cgrad,
    low2,
    gtile,
    accs,
    gsem,
):
    rows, model = x.shape
    hidden = wu.shape[1]
    clusters = rows // CLUSTER
    pairs = model // 128
    tile = 256
    band = 64

    def at(step, size):
        return pl.ds(pl.multiple_of(step * size, size), size)

    lanes = lax.broadcasted_iota(jnp.int32, (CLUSTER, 128), 1)
    first_f = jnp.where(lanes < HEAD_DIM, 1.0, 0.0)
    first = first_f.astype(BF16)
    second = (1.0 - first_f).astype(BF16)

    def stacked(pair):
        return jnp.concatenate([pair * first, pair * second], axis=0)

    def beside(tall):
        return jnp.concatenate([tall[:CLUSTER], tall[CLUSTER:]], axis=1)

    @pl.loop(0, 3 * model // tile)
    def _(step):
        cols = at(step, tile)
        qkv[:, cols] = (inner(x[...], wqkv[:, cols]) + bqkv[:, cols]).astype(BF16)

    @pl.loop(0, clusters * pairs)
    def _(step):
        cluster, pair = step // pairs, step % pairs
        r = at(cluster, CLUSTER)
        q = qkv[r, at(pair, 128)]
        k = qkv[r, pl.ds(pl.multiple_of(model + pair * 128, 128), 128)]
        v = qkv[r, pl.ds(pl.multiple_of(2 * model + pair * 128, 128), 128)]
        scores = outer(stacked(q), k) * score_scale
        scores = jnp.where(valid[cluster] > 0.5, scores, masked_score)
        top = jnp.max(scores, axis=-1, keepdims=True)
        weight = jnp.exp(scores - top)
        p = weight / jnp.sum(weight, axis=-1, keepdims=True)
        prob[step] = p
        ctx[r, at(pair, 128)] = inner(beside(p.astype(BF16)), stacked(v)).astype(BF16)

    @pl.loop(0, model // tile)
    def _(step):
        cols = at(step, tile)
        hat1[:, cols] = inner(ctx[...], wo[:, cols]) + x[:, cols].astype(F32) + bo[:, cols]

    @pl.loop(0, rows // band)
    def _(step):
        r = at(step, band)
        h = hat1[r, :]
        centered = h - jnp.mean(h, axis=-1, keepdims=True)
        inv = lax.rsqrt(jnp.mean(centered * centered, axis=-1, keepdims=True) + norm_eps)
        hat = centered * inv
        hat1[r, :] = hat
        inv1[r, :] = inv
        low1[r, :] = (hat * g1[...] + s1[...]).astype(BF16)

    @pl.loop(0, hidden // tile)
    def _(step):
        cols = at(step, tile)
        pre = inner(low1[...], wu[:, cols]) + bu[:, cols]
        cdf = 0.5 * (1.0 + lax.erf(pre * root_half))
        act[:, cols] = (pre * cdf).astype(BF16)
        slope[:, cols] = cdf + pre * jnp.exp(-0.5 * pre * pre) * inv_root_tau

    @pl.loop(0, model // tile)
    def _(step):
        cols = at(step, tile)
        norm = hat1[:, cols] * g1[:, cols] + s1[:, cols]
        work[:, cols] = inner(act[...], wd[:, cols]) + norm + bd[:, cols]

    accs[...] = jnp.zeros_like(accs)

    @pl.loop(0, rows // band)
    def _(step):
        r = at(step, band)
        h = work[r, :]
        centered = h - jnp.mean(h, axis=-1, keepdims=True)
        inv = lax.rsqrt(jnp.mean(centered * centered, axis=-1, keepdims=True) + norm_eps)
        hat = centered * inv
        out_low[r, :] = (hat * g2[...] + s2[...]).astype(BF16)
        grad = og[r, :].astype(F32)
        accs[4] += fold_rows(grad * hat)
        accs[5] += fold_rows(grad)
        scaled = grad * g2[...]
        back = inv * (
            scaled
            - jnp.mean(scaled, axis=-1, keepdims=True)
            - hat * jnp.mean(scaled * hat, axis=-1, keepdims=True)
        )
        accs[3] += fold_rows(back)
        work[r, :] = back
        low2[r, :] = back.astype(BF16)

    def flip(source):
        @pl.loop(0, model // 128)
        def _(step):
            flipped[at(step, 128), :] = source[:, at(step, 128)].T

    half_rows = model // 2
    chunks = half_rows // chunk

    def product_tiles(right, width, places, count):
        def moves(index, slot):
            m, n = index // count, index % count
            for piece, (part, start, size) in enumerate(places(n)):
                yield pltpu.make_async_copy(
                    gtile.at[slot, :, :, pl.ds(piece * size, size)] if size != width
                    else gtile.at[slot, :, :, pl.ds(0, width)],
                    grads.at[part, pl.ds(m * chunks, chunks), :, pl.ds(start, size)],
                    gsem.at[slot, piece],
                )

        total = 2 * count

        @pl.loop(0, total)
        def _(index):
            slot = index % 2
            m, n = index // count, index % count

            @pl.when(index >= 2)
            def _():
                for move in moves(index - 2, slot):
                    move.wait()

            value = inner(flipped[at(m, half_rows), :], right[:, at(n, width)])
            gtile[slot, :, :, pl.ds(0, width)] = value.reshape(chunks, chunk, width).astype(BF16)
            for move in moves(index, slot):
                move.start()

        for index in range(max(total - 2, 0), total):
            for move in moves(index, index % 2):
                move.wait()

    part_q = model // 2
    part_h = hidden // 2
    wide = 512

    def square(which):
        def places(n):
            return [(0, which * part_q, part_q), (1, which * part_q, part_q)]

        return places

    def long(base):
        per_part = part_h // wide

        def places(n):
            part, inside = n // per_part, n % per_part
            return [(part, pl.multiple_of(base + inside * wide, 128), wide)]

        return places

    flip(low2)
    product_tiles(act, wide, long(4 * part_q + part_h), hidden // wide)

    @pl.loop(0, hidden // tile)
    def _(step):
        cols = at(step, tile)
        back = outer(low2[...], wd[cols, :]) * slope[:, cols]
        back = back.astype(BF16)
        pre_low[:, cols] = back
        sums[:, pl.ds(pl.multiple_of(2 * model + step * tile, tile), tile)] = jnp.sum(
            back.astype(F32), axis=0, keepdims=True
        )

    flip(low1)
    product_tiles(pre_low, wide, long(4 * part_q), hidden // wide)

    @pl.loop(0, model // tile)
    def _(step):
        cols = at(step, tile)
        work[:, cols] += outer(pre_low[...], wu[cols, :])

    @pl.loop(0, rows // band)
    def _(step):
        r = at(step, band)
        grad = work[r, :]
        hat = hat1[r, :]
        accs[1] += fold_rows(grad * hat)
        accs[2] += fold_rows(grad)
        scaled = grad * g1[...]
        back = inv1[r, :] * (
            scaled
            - jnp.mean(scaled, axis=-1, keepdims=True)
            - hat * jnp.mean(scaled * hat, axis=-1, keepdims=True)
        )
        accs[0] += fold_rows(back)
        work[r, :] = back
        low2[r, :] = back.astype(BF16)

    flip(low2)
    product_tiles(ctx, model, square(3), 1)

    @pl.loop(0, model // tile)
    def _(step):
        cols = at(step, tile)
        cgrad[:, cols] = outer(low2[...], wo[cols, :]).astype(BF16)

    @pl.loop(0, clusters * pairs)
    def _(step):
        cluster, pair = step // pairs, step % pairs
        r = at(cluster, CLUSTER)
        at_q = at(pair, 128)
        at_k = pl.ds(pl.multiple_of(model + pair * 128, 128), 128)
        at_v = pl.ds(pl.multiple_of(2 * model + pair * 128, 128), 128)
        q, k, v = qkv[r, at_q], qkv[r, at_k], qkv[r, at_v]
        p = prob[step]
        dctx = stacked(cgrad[r, at_q])
        dprob = outer(dctx, v)
        dscore = (p * (dprob - jnp.sum(p * dprob, axis=-1, keepdims=True))).astype(BF16)
        dqkv[r, at_q] = (inner(beside(dscore), stacked(k)) * score_scale).astype(BF16)
        dqkv[r, at_k] = (under(dscore, stacked(q)) * score_scale).astype(BF16)
        dqkv[r, at_v] = under(p.astype(BF16), dctx).astype(BF16)

    flip(x)
    for which in range(3):
        product_tiles(dqkv.at[:, pl.ds(which * model, model)], model, square(which), 1)

    for which in range(2):
        @pl.loop(0, model // tile)
        def _(step, which=which):
            value = dqkv[:, pl.ds(pl.multiple_of(2 * which * model + step * tile, tile), tile)]
            sums[:, pl.ds(pl.multiple_of(which * model + step * tile, tile), tile)] = jnp.sum(
                value.astype(F32), axis=0, keepdims=True
            )

    @pl.loop(0, model // tile)
    def _(step):
        cols = at(step, tile)
        in_low[:, cols] = (work[:, cols] + outer(dqkv[...], wqkv[cols, :])).astype(BF16)

    for i in range(6):
        sums[:, pl.ds(2 * model + hidden + i * model, model)] = jnp.sum(accs[i], axis=0, keepdims=True)


def layer(chunk, x, og, valid, wqkv, wo, wu, wd, bqkv, bo, g1, s1, bu, bd, g2, s2):
    rows, model = x.shape
    hidden = wu.shape[1]
    hbm = pl.BlockSpec(memory_space=pl.ANY)
    vmem = pl.BlockSpec(memory_space=pltpu.VMEM)
    part = 2 * model + hidden
    steps = rows // CLUSTER * (model // 128)
    total = 8 * model + hidden
    return pl.pallas_call(
        functools.partial(layer_kernel, chunk),
        out_shape=(
            jax.ShapeDtypeStruct((rows, model), BF16),
            jax.ShapeDtypeStruct((rows, model), BF16),
            jax.ShapeDtypeStruct((2, model // chunk, chunk, part), BF16),
            jax.ShapeDtypeStruct((1, total), F32),
        ),
        in_specs=[vmem] * 15,
        out_specs=(vmem, vmem, hbm, vmem),
        scratch_shapes=[
            pltpu.VMEM((rows, 3 * model), BF16),
            pltpu.VMEM((rows, model), BF16),
            pltpu.VMEM((steps, 2 * CLUSTER, CLUSTER), F32),
            pltpu.VMEM((rows, model), F32),
            pltpu.VMEM((rows, 1), F32),
            pltpu.VMEM((rows, model), BF16),
            pltpu.VMEM((rows, hidden), BF16),
            pltpu.VMEM((rows, hidden), F32),
            pltpu.VMEM((rows, hidden), BF16),
            pltpu.VMEM((rows, model), F32),
            pltpu.VMEM((model, rows), BF16),
            pltpu.VMEM((rows, 3 * model), BF16),
            pltpu.VMEM((rows, model), BF16),
            pltpu.VMEM((rows, model), BF16),
            pltpu.VMEM((2, model // 2 // chunk, chunk, model), BF16),
            pltpu.VMEM((6, 8, model), F32),
            pltpu.SemaphoreType.DMA((2, 2)),
        ],
        compiler_params=pltpu.CompilerParams(vmem_limit_bytes=60 * MEBI),
    )(x, og, valid, wqkv, wo, wu, wd, bqkv, bo, g1, s1, bu, bd, g2, s2)


def exit_kernel(blocks, reduce, *refs):
    if reduce:
        (out_low, in_low, sources, grads, sums, out_home, in_home, grad_sum, sums_sum, *scratch) = refs
        (window, home, wsend, wrecv, csend, crecv, clocal, hsend, hrecv, hlocal, *scratch) = scratch
        (mine_g, from_core, got, gsend, grecv, glocal, rsend, rrecv, vrecv, vsend, vsem) = scratch
    else:
        (out_low, in_low, sources, out_home, in_home, *scratch) = refs
        (window, home, wsend, wrecv, csend, crecv, clocal, hsend, hrecv, hlocal) = scratch
    seq, core = lax.axis_index("seq"), lax.axis_index("head")
    rows, width = window.shape[2], window.shape[3]
    half = rows // 2
    partner = (seq, 1 - core)
    others = near(seq, core, blocks)
    bits = max(blocks.bit_length() - 1, 0)
    greetings = [(partner, None)] + [others[offset] for offset in OFFSETS[1:]]

    def across(bit):
        mask = 1 << bit
        return (seq + mask - 2 * mask * ((seq // mask) % 2), core)

    if reduce:
        greetings += [(across(bit), None) for bit in range(2, bits)]
    greet(greetings)

    mine = pl.ds(pl.multiple_of(core * width, width), width)
    theirs = pl.ds(pl.multiple_of((1 - core) * width, width), width)
    keep = pl.ds(pl.multiple_of(core * half, half), half)
    arrays = (out_low, in_low)
    firsts = []
    for which, array in enumerate(arrays):
        there = remote(
            array.at[:, theirs], window.at[which, 0, keep], csend.at[which], crecv.at[which], partner
        )
        here = pltpu.make_async_copy(array.at[:, mine], window.at[which, 0, keep], clocal.at[which])
        there.start()
        here.start()
        firsts.append((there, here))

    if reduce:
        parts = 2
        span = mine_g.shape[3] // parts
        core_moves = []
        for part in range(parts):
            cols = pl.ds(part * span, span)
            there = remote(
                grads.at[1 - core, :, :, cols], from_core.at[:, :, cols], gsend.at[part], grecv.at[part], partner
            )
            here = pltpu.make_async_copy(grads.at[core, :, :, cols], mine_g.at[0, :, :, cols], glocal.at[part])
            there.start()
            here.start()
            core_moves.append((there, here))

    def spread(which):
        for offset in OFFSETS[1:]:
            device, valid = others[offset]
            slot = SLOT[-offset]
            pl.when(valid)(
                remote(
                    window.at[which, 0], window.at[which, slot], wsend.at[which, slot], wrecv.at[which, slot], device
                ).start
            )

    for which in range(2):
        there, here = firsts[which]
        there.wait()
        here.wait()
        spread(which)

    def reduce_start(part, level):
        cols = pl.ds(part * span, span)
        order = orders[part]
        bit = order[level]
        own = (seq // (1 << bit)) % 2
        left = sorted(set(range(bits)) - set(order[:level]))
        low = 1 << left.index(bit)
        high = (1 << len(left)) // (2 * low)
        outs = []
        for top in range(high):
            src = mine_g.at[level % 2, pl.ds(pl.multiple_of((top * 2 + 1 - own) * low, low), low), :, cols]
            dst = got.at[pl.ds(base[level] + top * low, low), :, cols]
            outs.append(remote(src, dst, rsend.at[part, level, top], rrecv.at[part, level, top], across(bit)))
        return outs, own, low, high, cols

    def reduce_finish(part, level, state):
        outs, own, low, high, cols = state
        for copy in outs:
            copy.wait()
        for top in range(high):
            @pl.loop(0, low)
            def _(inside):
                held = mine_g[level % 2, (top * 2 + own) * low + inside, :, cols].astype(F32)
                other = got[base[level] + top * low + inside, :, cols].astype(F32)
                value = held + other
                if level == bits - 1:
                    grad_sum[:, cols] = value
                else:
                    mine_g[(level + 1) % 2, top * low + inside, :, cols] = value.astype(BF16)

    def pick(which):
        tile = 256
        for offset in OFFSETS:
            slot = SLOT[offset]

            def add(offset=offset, slot=slot):
                if offset != 0:
                    device, _ = others[offset]
                    remote(
                        window.at[which, 0],
                        window.at[which, slot],
                        wsend.at[which, slot],
                        wrecv.at[which, slot],
                        device,
                    ).wait_recv()

                @pl.loop(0, rows // tile)
                def _(step):
                    at = pl.ds(pl.multiple_of(step * tile, tile), tile)
                    places = lax.broadcasted_iota(jnp.int32, (tile, rows), 0) + (step * tile + seq * rows)
                    chosen = jnp.where(sources[slot] == places, 1.0, 0.0).astype(BF16)
                    part = inner(chosen, window[which, slot]).astype(BF16)
                    if offset == 0:
                        home[which, at, :] = part
                    else:
                        home[which, at, :] += part

            if offset == 0:
                add()
            else:
                pl.when(others[offset][1])(add)
        target = (out_home, in_home)[which]
        there = remote(home.at[which], target.at[:, mine], hsend.at[which], hrecv.at[which], partner)
        here = pltpu.make_async_copy(home.at[which], target.at[:, mine], hlocal.at[which])
        there.start()
        here.start()
        return there, here

    lasts = []
    if not reduce:
        lasts = [pick(0), pick(1)]
    else:
        orders = ([0, 1] + list(range(bits - 1, 1, -1)), [1, 0] + list(range(bits - 1, 1, -1)))
        base, count = [], 0
        for level in range(bits):
            base.append(count)
            count += blocks >> (level + 1)

        def sum_level(level):
            device = partner if level == 0 else across(level - 1)
            return remote(vsend.at[level], vrecv.at[level], vsem.at[0, level], vsem.at[1, level], device)

        def sum_start(level):
            if level == 0:
                vsend[0] = sums[...]
            sum_level(level).start()

        def sum_finish(level):
            sum_level(level).wait()
            value = vsend[level] + vrecv[level]
            if level == bits:
                sums_sum[...] = value
            else:
                vsend[level + 1] = value

        sum_start(0)
        states = [None] * parts
        for part in range(parts):
            there, here = core_moves[part]
            there.wait()
            here.wait()
            cols = pl.ds(part * span, span)

            @pl.loop(0, blocks)
            def _(inside):
                value = mine_g[0, inside, :, cols].astype(F32) + from_core[inside, :, cols].astype(F32)
                mine_g[0, inside, :, cols] = value.astype(BF16)

            states[part] = reduce_start(part, 0)
            for copy in states[part][0]:
                copy.start()
        sum_finish(0)
        sum_start(1)
        lasts.append(pick(0))
        for level in range(bits):
            for part in range(parts):
                reduce_finish(part, level, states[part])
                if level + 1 < bits:
                    states[part] = reduce_start(part, level + 1)
                    for copy in states[part][0]:
                        copy.start()
            sum_finish(level + 1)
            if level + 1 < bits:
                sum_start(level + 2)
            if level == 1:
                lasts.append(pick(1))
        if bits < 2:
            lasts.append(pick(1))

    for offset in OFFSETS[1:]:
        device, valid = others[offset]
        slot = SLOT[-offset]

        def finish(device=device, slot=slot):
            for which in range(2):
                remote(
                    window.at[which, 0], window.at[which, slot], wsend.at[which, slot], wrecv.at[which, slot], device
                ).wait_send()

        pl.when(valid)(finish)
    for there, here in lasts:
        there.wait()
        here.wait()


def leave(mesh, reduce, out_low, in_low, sources, grads, sums):
    half, model = out_low.shape
    rows, width = 2 * half, model // 2
    blocks = mesh.shape["seq"]
    slots = len(OFFSETS)
    hbm = pl.BlockSpec(memory_space=pl.ANY)
    vmem = pl.BlockSpec(memory_space=pltpu.VMEM)
    dma = pltpu.SemaphoreType.DMA
    out_shape = [jax.ShapeDtypeStruct((rows, model), BF16)] * 2
    out_specs = [hbm, hbm]
    in_specs = [hbm, hbm, vmem]
    args = [out_low, in_low, sources]
    scratch = [
        pltpu.VMEM((2, slots, rows, width), BF16),
        pltpu.VMEM((2, rows, width), BF16),
        dma((2, slots)),
        dma((2, slots)),
        dma((2,)),
        dma((2,)),
        dma((2,)),
        dma((2,)),
        dma((2,)),
        dma((2,)),
    ]
    if reduce:
        _, chunks, chunk, span = grads.shape
        bits = blocks.bit_length() - 1
        args += [grads, sums]
        in_specs += [hbm, vmem]
        out_shape += [jax.ShapeDtypeStruct((chunk, span), F32), jax.ShapeDtypeStruct(sums.shape, F32)]
        out_specs += [vmem, vmem]
        scratch += [
            pltpu.VMEM((2, blocks, chunk, span), BF16),
            pltpu.VMEM((blocks, chunk, span), BF16),
            pltpu.VMEM((blocks, chunk, span), BF16),
            dma((2,)),
            dma((2,)),
            dma((2,)),
            dma((2, bits, blocks // 2)),
            dma((2, bits, blocks // 2)),
            pltpu.VMEM((bits + 1,) + sums.shape, F32),
            pltpu.VMEM((bits + 1,) + sums.shape, F32),
            dma((2, bits + 1)),
        ]
    return pl.pallas_call(
        functools.partial(exit_kernel, blocks, reduce),
        out_shape=tuple(out_shape),
        in_specs=in_specs,
        out_specs=tuple(out_specs),
        scratch_shapes=scratch,
        compiler_params=pltpu.CompilerParams(
            collective_id=1, has_side_effects=True, vmem_limit_bytes=60 * MEBI
        ),
    )(*args)


FROM_X, FROM_Y, FROM_Z, FROM_LAST, RELAY = range(5)
OWN = -1
EXCHANGES = 4
CHUNKS = 4
GROUPS = 3
PARTS = 3
BITS = 4


def whole_kernel(
    blocks,
    tokens,
    out_grad,
    doc_lengths,
    cluster_perm,
    wq,
    wk,
    wv,
    wo_half,
    wu_half,
    wd_half,
    bq,
    bv,
    bu_half,
    bo_in,
    g1_in,
    s1_in,
    bd_in,
    g2_in,
    s2_in,
    out_home,
    in_home,
    grad_sum,
    sums_sum,
    win,
    wqkv,
    wo,
    wu,
    wd,
    bqkv,
    bu,
    stage,
    picked,
    block,
    source,
    sources,
    rel,
    valid,
    vectors,
    x,
    og,
    qkv,
    ctx,
    prob,
    hat1,
    inv12,
    low1,
    act,
    slope,
    work,
    flipped,
    flipped_x,
    in_low,
    accs,
    mine_g,
    from_core,
    give,
    got0,
    got1,
    got2,
    got3,
    vsend,
    vrecv,
    wsend,
    wrecv,
    wlocal,
    xsend,
    xrecv,
    ssend,
    srecv,
    ssem,
    psend,
    precv,
    plocal,
    hsend,
    hrecv,
    hlocal,
    gsend,
    grecv,
    rsend,
    rrecv,
    vsem,
    osem,
    credit,
):
    seq, core = lax.axis_index("seq"), lax.axis_index("head")
    px, py = seq % 2, (seq // 2) % 2
    rows, width = tokens.shape[0], picked.shape[2]
    half, model = x.shape
    hidden = wu.shape[1]
    clusters = half // CLUSTER
    pairs = model // 128
    part_rows = rows // CHUNKS
    tile = 256
    band = 64

    low2 = og

    partner = (seq, 1 - core)
    x_next = seq + 1 - 2 * px
    y_next = seq + 2 - 4 * py
    z_to = seq + 4 - 8 * py
    z_from = seq - 4 + 8 * py
    to_ok = (z_to >= 0) & (z_to < blocks)
    from_ok = (z_from >= 0) & (z_from < blocks)
    level_chip = px == py
    off_chip = px != py
    last_next = x_next + core * (y_next - x_next)
    relay_send = (core == 1) & off_chip & from_ok
    relay_recv = (core == 1) & off_chip & to_ok
    later_ok = off_chip & (((core == 0) & from_ok) | ((core == 1) & to_ok))
    last_ok = off_chip | from_ok
    offsets = {
        OWN: 0,
        FROM_X: 1 - 2 * px,
        FROM_Y: 2 - 4 * py,
        FROM_Z: 4 * py - 2,
        FROM_LAST: 2 * px - 1,
    }
    arrived = {OWN: None, FROM_X: None, FROM_Y: None, FROM_Z: from_ok, FROM_LAST: last_ok}
    others = near(seq, core, blocks)

    def across(bit):
        mask = 1 << bit
        return (seq + mask - 2 * mask * ((seq // mask) % 2), core)

    greetings = [(partner, None), ((x_next, core), None), ((y_next, core), None)]
    greetings += [((z_to, core), to_ok), ((z_from, core), from_ok)]
    greetings += [others[offset] for offset in OFFSETS[1:]]
    greetings += [(across(bit), None) for bit in range(BITS)]
    arrivals = greet_start(greetings)

    def at(step, size):
        return pl.ds(pl.multiple_of(step * size, size), size)

    def when(condition, action):
        if condition is None:
            action()
        else:
            pl.when(condition)(action)

    mine = at(core, width)
    theirs = at(1 - core, width)
    keep = at(core, half)
    other_rows = at(1 - core, half)

    def piece(chunk):
        return pl.ds(chunk * part_rows, part_rows)

    def own_rows(e, chunk):
        if e < 2:
            return (tokens, out_grad)[e].at[piece(chunk), mine]
        return block.at[e - 2, piece(chunk)]

    def hop(e, kind, chunk, src, there):
        return remote(
            src,
            win.at[e, kind, piece(chunk)],
            xsend.at[e, kind, chunk],
            xrecv.at[e, kind, chunk],
            (there, core),
        )

    def held(e, kind, chunk):
        return win.at[e, kind, piece(chunk)]

    def hop_x(e, chunk):
        return hop(e, FROM_X, chunk, own_rows(e, chunk), x_next)

    def hop_y(e, chunk):
        return hop(e, FROM_Y, chunk, own_rows(e, chunk), y_next)

    def hop_z(e, chunk):
        return hop(e, FROM_Z, chunk, held(e, FROM_Y, chunk), z_to)

    def hop_relay(e, chunk):
        return hop(e, RELAY, chunk, held(e, FROM_X, chunk), z_from)

    def hop_last_early(e, chunk):
        return hop(e, FROM_LAST, chunk, held(e, 1 - core, chunk), last_next)

    def hop_last_late(e, chunk):
        return hop(e, FROM_LAST, chunk, held(e, 2 + 2 * core, chunk), last_next)

    def send_own(e):
        for chunk in range(CHUNKS):
            hop_y(e, chunk).start()
            hop_x(e, chunk).start()

    def first_hop(e, chunk):
        hop_y(e, chunk).wait_recv()
        pl.when(to_ok)(hop_z(e, chunk).start)
        hop_x(e, chunk).wait_recv()
        pl.when(level_chip)(hop_last_early(e, chunk).start)
        pl.when(relay_send)(hop_relay(e, chunk).start)

    def second_hop(e, chunk):
        pl.when(from_ok)(hop_z(e, chunk).wait_recv)
        pl.when(relay_recv)(hop_relay(e, chunk).wait_recv)
        pl.when(later_ok)(hop_last_late(e, chunk).start)

    def last_hop(e, chunk):
        pl.when(last_ok)(hop_last_early(e, chunk).wait_recv)

    def all_sent(e):
        for chunk in range(CHUNKS):
            hop_x(e, chunk).wait_send()
            hop_y(e, chunk).wait_send()
            pl.when(to_ok)(hop_z(e, chunk).wait_send)
            pl.when(relay_send)(hop_relay(e, chunk).wait_send)
            pl.when(level_chip)(hop_last_early(e, chunk).wait_send)
            pl.when(later_ok)(hop_last_late(e, chunk).wait_send)

    def span_of(side):
        return pl.ds(side * half, half)

    def pick(e, units, fresh=False):
        which = e % 2
        moves = {}
        for index, (kind, side) in enumerate(units):
            if kind == OWN and e >= 2:
                continue
            if kind == OWN:
                src = (tokens, out_grad)[e].at[span_of(side), mine]
            else:
                src = win.at[e, kind, span_of(side)]
            moves[index] = pltpu.make_async_copy(src, stage.at[index], ssem.at[index])
            when(arrived[kind], moves[index].start)
        for index, (kind, side) in enumerate(units):

            def add(index=index, kind=kind, side=side):
                if index in moves:
                    moves[index].wait()
                offset = offsets[kind]
                if e < 2:
                    wanted = rel[:, pl.ds(0, 1)] - (offset * rows + side * half)
                    places = lax.broadcasted_iota(jnp.int32, (rows, half), 1)
                else:
                    wanted = sources[offset + 2, :, span_of(side)] - seq * rows
                    places = lax.broadcasted_iota(jnp.int32, (rows, half), 0)
                chosen = jnp.where(places == wanted, 1.0, 0.0).astype(BF16)
                block_rows = stage[index] if index in moves else block[e - 2, span_of(side), :]
                value = inner(chosen, block_rows).astype(BF16)
                if fresh and index == 0:
                    picked[which] = value
                else:
                    picked[which] += value

            when(arrived[kind], add)

    def deliver(e):
        target = (x, og)[e]
        there = remote(picked.at[e, other_rows], target.at[:, mine], psend.at[e], precv.at[e], partner)
        here = pltpu.make_async_copy(picked.at[e, keep], target.at[:, mine], plocal.at[e])
        return there, here

    def collect(e):
        array = in_low
        there = remote(array.at[:, theirs], block.at[e - 2, keep], psend.at[e], precv.at[e], partner)
        here = pltpu.make_async_copy(array.at[:, mine], block.at[e - 2, keep], plocal.at[e])
        return there, here

    def bring_home(e):
        target = (out_home, in_home)[e - 2]
        there = remote(picked.at[e - 2], target.at[:, mine], hsend.at[e - 2], hrecv.at[e - 2], partner)
        here = pltpu.make_async_copy(picked.at[e - 2], target.at[:, mine], hlocal.at[e - 2])
        return there, here

    def begin(pair):
        for copy in pair:
            copy.start()

    def end(pair):
        for copy in pair:
            copy.wait()

    orders = ((0, 1, 2, 3), (1, 0, 2, 3), (2, 3, 0, 1))
    gots = (got0, got1, got2, got3)
    span = mine_g.shape[-1]
    part_span = span // PARTS

    def part_cols(part):
        return pl.ds(part * part_span, part_span)

    def own_bit(bit):
        return (seq // (1 << bit)) % 2

    def halving(group, part, level):
        order = orders[part]
        index = []
        for bit in (3, 2, 1, 0):
            if bit in order[:level]:
                index.append(own_bit(bit))
            elif bit == order[level]:
                index.append(1 - own_bit(bit))
            else:
                index.append(slice(None))
        src = mine_g.at[(group, *index, slice(None), part_cols(part))]
        dst = gots[level].at[group, part]
        return remote(
            src, dst, rsend.at[group, part, level], rrecv.at[group, part, level], across(order[level])
        )

    def halving_end(group, part, level):
        halving(group, part, level).wait()
        order = orders[part]
        left = [bit for bit in (3, 2, 1, 0) if bit not in order[: level + 1]]
        cols = part_cols(part)
        finals = slope.at[pl.ds(group * chunk_rows, chunk_rows), :]

        @pl.loop(0, 1 << len(left))
        def _(step):
            digits = {bit: (step // (1 << (len(left) - 1 - i))) % 2 for i, bit in enumerate(left)}
            place = [digits[bit] if bit in digits else own_bit(bit) for bit in (3, 2, 1, 0)]
            value = mine_g[(group, *place, slice(None), cols)].astype(F32)
            other = gots[level][(group, part, *[digits[bit] for bit in left])]
            value = value + other.astype(F32)
            if level == BITS - 1:
                finals[:, cols] = value
            else:
                mine_g[(group, *place, slice(None), cols)] = value.astype(BF16)

    def advance(group, level):
        for part in range(PARTS):
            halving_end(group, part, level)
            if level + 1 < BITS:
                halving(group, part, level + 1).start()
            else:
                write_out(group, part).start()

    def write_out(group, part):
        return pltpu.make_async_copy(
            slope.at[pl.ds(group * chunk_rows, chunk_rows), part_cols(part)],
            grad_sum.at[:, pl.ds(group * span + part * part_span, part_span)],
            osem.at[group, part],
        )

    def core_move(group, part):
        cols = part_cols(part)
        return remote(
            give.at[:, :, :, :, :, cols],
            from_core.at[group % 2, :, :, :, :, :, cols],
            gsend.at[group, part],
            grecv.at[group, part],
            partner,
        )

    chunk_rows = give.shape[4]
    m_rows = model // 2

    def group_products(group, columns, between=lambda: None):
        if group == 2:
            pl.semaphore_wait(credit, 1)
        for side in (0, 1):
            if side == 1:
                between()
            for part in range(PARTS):
                if side == 0 and group > 0:
                    core_move(group - 1, part).wait_send()
                if side == 1:
                    core_move(group, part).wait_recv()
                place = 0
                for left, right, start, size in columns(part, (1 - core, core)[side]):
                    cols = pl.ds(part * part_span + place, size)
                    place += size

                    @pl.loop(0, 2)
                    def _(m, left=left, right=right, start=start, size=size, cols=cols):
                        value = inner(left[at(m, m_rows), :], right[:, pl.ds(start, size)])
                        value = value.reshape(2, 2, 2, chunk_rows, size)
                        if side == 0:
                            give[m, :, :, :, :, cols] = value.astype(BF16)
                        else:
                            value = value + from_core[group % 2, m, :, :, :, :, cols].astype(F32)
                            mine_g[group, m, :, :, :, :, cols] = value.astype(BF16)

                if side == 0:
                    core_move(group, part).start()
                else:
                    halving(group, part, 0).start()
        if group == 0:
            pl.semaphore_signal(credit, inc=1, device_id=partner, device_id_type=MESH)

    part_out = 2 * model + hidden

    def sum_move(level):
        device = partner if level == 0 else across(level - 1)
        return remote(vsend.at[level], vrecv.at[level], vsem.at[0, level], vsem.at[1, level], device)

    def sum_next(level):
        sum_move(level).wait()
        value = vsend[level] + vrecv[level]
        if level == BITS:
            sums_sum[...] = value
        else:
            vsend[level + 1] = value
            sum_move(level + 1).start()

    wide, deep = wq.shape[1], wd_half.shape[0]
    pieces = []
    for i, array in enumerate((wq, wk, wv)):
        pieces.append((array, wqkv.at[:, pl.ds(pl.multiple_of(i * model + core * wide, wide), wide)]))
    pieces.append((wo_half, wo.at[at(core, wide), :]))
    pieces.append((wu_half, wu.at[:, at(core, deep)]))
    pieces.append((wd_half, wd.at[at(core, deep), :]))
    heres = [pltpu.make_async_copy(array, place, wlocal.at[i]) for i, (array, place) in enumerate(pieces)]
    for copy in heres:
        copy.start()

    shape = cluster_perm.shape
    positions = lax.broadcasted_iota(jnp.int32, shape, 0) * CLUSTER + lax.broadcasted_iota(jnp.int32, shape, 1)
    positions = positions + seq * rows
    doc_start = jnp.zeros(shape, jnp.int32)
    doc_length = jnp.zeros(shape, jnp.int32)
    start = 0
    for i in range(doc_lengths.shape[0]):
        length = doc_lengths[i]
        inside = positions >= start
        doc_start = jnp.where(inside, start, doc_start)
        doc_length = jnp.where(inside, length, doc_length)
        start = start + (length + CLUSTER - 1) // CLUSTER * CLUSTER
    valid[...] = jnp.where(cluster_perm[...] < doc_length, 1.0, 0.0)
    from_row = doc_start + cluster_perm[...]
    for i in range(shape[0]):
        line = from_row[i : i + 1, :]
        source[:, pl.ds(i * CLUSTER, CLUSTER)] = line
        rel[pl.ds(i * CLUSTER, CLUSTER), :] = jnp.broadcast_to(line - seq * rows, (CLUSTER, CLUSTER)).T
    sources[2] = source[...]
    for i, vector in enumerate((bo_in, g1_in, s1_in, bd_in, g2_in, s2_in)):
        vectors[i] = vector[...].reshape(1, model)
    bo, g1, s1, bd, g2, s2 = (vectors.at[i] for i in range(6))
    at_v = pl.ds(pl.multiple_of(2 * model + core * wide, wide), wide)
    bqkv[:, at(core, wide)] = bq[...].reshape(1, wide)
    bqkv[:, pl.ds(model, model)] = jnp.zeros((1, model), F32)
    bqkv[:, at_v] = bv[...].reshape(1, wide)
    bu[:, at(core, deep)] = bu_half[...].reshape(1, deep)
    pl.semaphore_wait(pltpu.get_barrier_semaphore(), arrivals)

    send_own(0)
    weights = []
    for place in (bqkv.at[:, at(core, wide)], bqkv.at[:, at_v], bu.at[:, at(core, deep)]):
        pieces.append((place, place))
    for i, (array, place) in enumerate(pieces):
        weights.append(remote(array, place, wsend.at[i], wrecv.at[i], partner))
        weights[i].start()
    tinies = []
    for offset in OFFSETS[1:]:
        device, there_ok = others[offset]
        out = remote(source, sources.at[2 - offset], ssend.at[2 - offset], srecv.at[2 - offset], device)
        back = remote(source, sources.at[2 + offset], ssend.at[2 + offset], srecv.at[2 + offset], device)
        pl.when(there_ok)(out.start)
        tinies.append((there_ok, out, back))

    pick(0, [(OWN, 0), (OWN, 1)], fresh=True)
    pick(1, [(OWN, 0), (OWN, 1)], fresh=True)
    first_hop(0, 0)
    first_hop(0, 1)
    second_hop(0, 0)
    pick(0, [(FROM_X, 0), (FROM_Y, 0)])
    first_hop(0, 2)
    second_hop(0, 1)
    first_hop(0, 3)
    second_hop(0, 2)
    send_own(1)
    pick(0, [(FROM_X, 1), (FROM_Y, 1), (FROM_Z, 0)])
    second_hop(0, 3)
    last_hop(0, 0)
    last_hop(0, 1)
    pick(0, [(FROM_Z, 1), (FROM_LAST, 0)])
    last_hop(0, 2)
    last_hop(0, 3)
    pick(0, [(FROM_LAST, 1)])
    begin(deliver(0))
    for copy in heres + weights:
        copy.wait()
    end(deliver(0))

    lanes = lax.broadcasted_iota(jnp.int32, (CLUSTER, 128), 1)
    first_f = jnp.where(lanes < HEAD_DIM, 1.0, 0.0)
    first = first_f.astype(BF16)
    second = (1.0 - first_f).astype(BF16)

    def stacked(pair):
        return jnp.concatenate([pair * first, pair * second], axis=0)

    def beside(tall):
        return jnp.concatenate([tall[:CLUSTER], tall[CLUSTER:]], axis=1)

    @pl.loop(0, 3 * model // tile)
    def _(step):
        cols = at(step, tile)
        qkv[:, cols] = (inner(x[...], wqkv[:, cols]) + bqkv[:, cols]).astype(BF16)

    first_hop(1, 0)

    @pl.loop(0, clusters)
    def _(cluster):
        r = at(cluster, CLUSTER)
        for pair in range(pairs):
            q = qkv[r, pl.ds(pair * 128, 128)]
            k = qkv[r, pl.ds(model + pair * 128, 128)]
            v = qkv[r, pl.ds(2 * model + pair * 128, 128)]
            scores = outer(stacked(q), k) * score_scale
            scores = jnp.where(valid[pl.ds(core * clusters + cluster, 1), :] > 0.5, scores, masked_score)
            top = jnp.max(scores, axis=-1, keepdims=True)
            weight = jnp.exp(scores - top)
            p = weight * (1.0 / jnp.sum(weight, axis=-1, keepdims=True))
            prob[cluster * pairs + pair] = p
            ctx[r, pl.ds(pair * 128, 128)] = inner(beside(p.astype(BF16)), stacked(v)).astype(BF16)

    first_hop(1, 1)
    second_hop(1, 0)

    @pl.loop(0, model // tile)
    def _(step):
        cols = at(step, tile)
        hat1[:, cols] = inner(ctx[...], wo[:, cols]) + x[:, cols].astype(F32) + bo[:, cols]

    @pl.loop(0, half // band)
    def _(step):
        r = at(step, band)
        h = hat1[r, :]
        centered = h - jnp.mean(h, axis=-1, keepdims=True)
        inv = lax.rsqrt(jnp.mean(centered * centered, axis=-1, keepdims=True) + norm_eps)
        hat = centered * inv
        hat1[r, :] = hat
        inv12[r, pl.ds(0, 1)] = inv
        low1[r, :] = (hat * g1[...] + s1[...]).astype(BF16)

    first_hop(1, 2)
    second_hop(1, 1)

    @pl.loop(0, hidden // tile)
    def _(step):
        cols = at(step, tile)
        pre = inner(low1[...], wu[:, cols]) + bu[:, cols]
        cdf = 0.5 * (1.0 + lax.erf(pre * root_half))
        act[:, cols] = (pre * cdf).astype(BF16)
        slope[:, cols] = cdf + pre * jnp.exp(-0.5 * pre * pre) * inv_root_tau

    first_hop(1, 3)
    second_hop(1, 2)

    @pl.loop(0, model // tile)
    def _(step):
        cols = at(step, tile)
        norm = hat1[:, cols] * g1[:, cols] + s1[:, cols]
        work[:, cols] = inner(act[...], wd[:, cols]) + norm + bd[:, cols]

    @pl.loop(0, half // band)
    def _(step):
        r = at(step, band)
        h = work[r, :]
        centered = h - jnp.mean(h, axis=-1, keepdims=True)
        inv = lax.rsqrt(jnp.mean(centered * centered, axis=-1, keepdims=True) + norm_eps)
        hat = centered * inv
        work[r, :] = hat
        inv12[r, pl.ds(1, 1)] = inv
        in_low[r, :] = (hat * g2[...] + s2[...]).astype(BF16)

    begin(collect(2))
    second_hop(1, 3)
    pick(1, [(FROM_X, 0), (FROM_Y, 0), (FROM_X, 1), (FROM_Y, 1)])
    end(collect(2))
    send_own(2)
    for chunk in range(CHUNKS):
        last_hop(1, chunk)
    pick(1, [(FROM_Z, 0), (FROM_Z, 1), (FROM_LAST, 0), (FROM_LAST, 1)])
    begin(deliver(1))
    accs[...] = jnp.zeros_like(accs)
    end(deliver(1))

    @pl.loop(0, half // band)
    def _(step):
        r = at(step, band)
        hat = work[r, :]
        grad = og[r, :].astype(F32)
        accs[4] += fold_rows(grad * hat)
        accs[5] += fold_rows(grad)
        scaled = grad * g2[...]
        back = inv12[r, pl.ds(1, 1)] * (
            scaled
            - jnp.mean(scaled, axis=-1, keepdims=True)
            - hat * jnp.mean(scaled * hat, axis=-1, keepdims=True)
        )
        accs[3] += fold_rows(back)
        work[r, :] = back
        low2[r, :] = back.astype(BF16)

    def flip(source_rows, target=flipped):
        @pl.loop(0, model // 128)
        def _(step):
            target[at(step, 128), :] = source_rows[:, at(step, 128)].T

    def long_columns(part, side):
        start = pl.multiple_of(side * span + part * part_span, part_span)
        return [(flipped, act, start, part_span)]

    first_hop(2, 0)
    flip(low2)
    group_products(0, long_columns, lambda: first_hop(2, 1))
    first_hop(2, 2)
    second_hop(2, 0)

    @pl.loop(0, hidden // tile)
    def _(step):
        cols = at(step, tile)
        back = outer(low2[...], wd[cols, :]) * slope[:, cols]
        back = back.astype(BF16)
        act[:, cols] = back
        vsend[0, :, pl.ds(pl.multiple_of(2 * model + step * tile, tile), tile)] = jnp.sum(
            back.astype(F32), axis=0, keepdims=True
        )

    first_hop(2, 3)
    second_hop(2, 1)
    flip(low1)
    group_products(1, long_columns, lambda: second_hop(2, 2))
    second_hop(2, 3)
    advance(0, 0)

    @pl.loop(0, model // tile)
    def _(step):
        cols = at(step, tile)
        work[:, cols] += outer(act[...], wu[cols, :])

    @pl.loop(0, half // band)
    def _(step):
        r = at(step, band)
        grad = work[r, :]
        hat = hat1[r, :]
        accs[1] += fold_rows(grad * hat)
        accs[2] += fold_rows(grad)
        scaled = grad * g1[...]
        back = inv12[r, pl.ds(0, 1)] * (
            scaled
            - jnp.mean(scaled, axis=-1, keepdims=True)
            - hat * jnp.mean(scaled * hat, axis=-1, keepdims=True)
        )
        accs[0] += fold_rows(back)
        work[r, :] = back
        low2[r, :] = back.astype(BF16)

    @pl.loop(0, model // tile)
    def _(step):
        cols = at(step, tile)
        low1[:, cols] = outer(low2[...], wo[cols, :]).astype(BF16)

    def attention_backward(cluster):
        r = at(cluster, CLUSTER)
        for pair in range(pairs):
            at_q = pl.ds(pair * 128, 128)
            at_k = pl.ds(model + pair * 128, 128)
            at_v = pl.ds(2 * model + pair * 128, 128)
            q, k, v = qkv[r, at_q], qkv[r, at_k], qkv[r, at_v]
            p = prob[cluster * pairs + pair]
            dctx = stacked(low1[r, at_q])
            dprob = outer(dctx, v)
            dscore = (p * (dprob - jnp.sum(p * dprob, axis=-1, keepdims=True))).astype(BF16)
            act[r, at_q] = (inner(beside(dscore), stacked(k)) * score_scale).astype(BF16)
            act[r, at_k] = (under(dscore, stacked(q)) * score_scale).astype(BF16)
            act[r, at_v] = under(p.astype(BF16), dctx).astype(BF16)

    pl.loop(0, clusters // 2)(attention_backward)
    advance(0, 1)
    pl.loop(clusters // 2, clusters)(attention_backward)
    advance(1, 0)

    dqkv = act.at[:, pl.ds(0, 3 * model)]

    @pl.loop(0, model // tile)
    def _(step):
        cols = at(step, tile)
        in_low[:, cols] = (work[:, cols] + outer(dqkv[...], wqkv[cols, :])).astype(BF16)

    begin(collect(3))
    end(collect(3))
    send_own(3)
    advance(0, 2)
    advance(1, 1)

    for which in range(2):
        @pl.loop(0, model // tile)
        def _(step, which=which):
            value = act[:, pl.ds(pl.multiple_of(2 * which * model + step * tile, tile), tile)]
            vsend[0, :, pl.ds(pl.multiple_of(which * model + step * tile, tile), tile)] = jnp.sum(
                value.astype(F32), axis=0, keepdims=True
            )

    for i in range(6):
        vsend[0, :, pl.ds(part_out + i * model, model)] = jnp.sum(accs[i], axis=0, keepdims=True)
    sum_move(0).start()

    flip(low2)
    flip(x, flipped_x)

    def square_columns(part, side):
        def cut(left, right, base, start, size):
            return (left, right, pl.multiple_of(base + side * width + start, 128), size)

        third = width // 3
        if part == 0:
            return [cut(flipped, ctx, 0, 0, 3 * third), cut(flipped_x, act, 0, 0, third)]
        if part == 1:
            return [
                cut(flipped_x, act, 0, third, 2 * third),
                cut(flipped_x, act, model, 0, 2 * third),
            ]
        return [
            cut(flipped_x, act, model, 2 * third, third),
            cut(flipped_x, act, 2 * model, 0, 3 * third),
        ]

    group_products(2, square_columns, lambda: first_hop(3, 0))
    first_hop(3, 1)
    second_hop(3, 0)
    advance(0, 3)
    first_hop(3, 2)
    second_hop(3, 1)
    sum_next(0)
    advance(1, 2)
    for there_ok, out, back in tinies:

        def finish(out=out, back=back):
            out.wait_send()
            back.wait_recv()

        pl.when(there_ok)(finish)
    for chunk in range(CHUNKS):
        last_hop(2, chunk)
    pick(2, [(OWN, 0), (OWN, 1)], fresh=True)
    first_hop(3, 3)
    second_hop(3, 2)
    sum_next(1)
    pick(2, [(FROM_X, 0), (FROM_Y, 0), (FROM_X, 1), (FROM_Y, 1)])
    second_hop(3, 3)
    advance(2, 0)
    advance(1, 3)
    pick(2, [(FROM_Z, 0), (FROM_Z, 1), (FROM_LAST, 0), (FROM_LAST, 1)])
    begin(bring_home(2))
    sum_next(2)
    pick(3, [(OWN, 0), (OWN, 1)], fresh=True)
    pick(3, [(FROM_X, 0), (FROM_Y, 0), (FROM_X, 1), (FROM_Y, 1)])
    sum_next(3)
    advance(2, 1)
    last_hop(3, 0)
    last_hop(3, 1)
    pick(3, [(FROM_Z, 0), (FROM_Z, 1), (FROM_LAST, 0)])
    advance(2, 2)
    sum_next(4)
    last_hop(3, 2)
    last_hop(3, 3)
    pick(3, [(FROM_LAST, 1)])
    begin(bring_home(3))
    advance(2, 3)
    for part in range(PARTS):
        core_move(2, part).wait_send()
    for e in range(EXCHANGES):
        all_sent(e)
    end(bring_home(2))
    end(bring_home(3))
    for group in range(GROUPS):
        for part in range(PARTS):
            write_out(group, part).wait()


def whole(mesh, *args):
    tokens, wu_half = args[0], args[8]
    rows, model = tokens.shape
    half, width = rows // 2, model // 2
    hidden = 2 * wu_half.shape[1]
    blocks = mesh.shape["seq"]
    hbm = pl.BlockSpec(memory_space=pl.ANY)
    vmem = pl.BlockSpec(memory_space=pltpu.VMEM)
    smem = pl.BlockSpec(memory_space=pltpu.SMEM)
    dma = pltpu.SemaphoreType.DMA
    chunk = model // blocks
    span = 4 * width
    part_span = span // PARTS
    steps = half // CLUSTER * (model // 128)
    total = 8 * model + hidden
    cube = (2, 2, 2, 2)
    return pl.pallas_call(
        functools.partial(whole_kernel, blocks),
        out_shape=(
            jax.ShapeDtypeStruct((rows, model), BF16),
            jax.ShapeDtypeStruct((rows, model), BF16),
            jax.ShapeDtypeStruct((chunk, GROUPS * span), F32),
            jax.ShapeDtypeStruct((1, total), F32),
            jax.ShapeDtypeStruct((EXCHANGES, 5, rows, width), BF16),
        ),
        in_specs=[hbm, hbm, smem, vmem] + [hbm] * 6 + [vmem] * 9,
        out_specs=(hbm, hbm, hbm, vmem, hbm),
        scratch_shapes=[
            pltpu.VMEM((model, 3 * model), BF16),
            pltpu.VMEM((model, model), BF16),
            pltpu.VMEM((model, hidden), BF16),
            pltpu.VMEM((hidden, model), BF16),
            pltpu.VMEM((1, 3 * model), F32),
            pltpu.VMEM((1, hidden), F32),
            pltpu.VMEM((4, half, width), BF16),
            pltpu.VMEM((2, rows, width), BF16),
            pltpu.VMEM((2, rows, width), BF16),
            pltpu.VMEM((1, rows), jnp.int32),
            pltpu.VMEM((5, 1, rows), jnp.int32),
            pltpu.VMEM((rows, CLUSTER), jnp.int32),
            pltpu.VMEM((rows // CLUSTER, CLUSTER), F32),
            pltpu.VMEM((6, 1, model), F32),
            pltpu.VMEM((half, model), BF16),
            pltpu.VMEM((half, model), BF16),
            pltpu.VMEM((half, 3 * model), BF16),
            pltpu.VMEM((half, model), BF16),
            pltpu.VMEM((steps, 2 * CLUSTER, CLUSTER), F32),
            pltpu.VMEM((half, model), F32),
            pltpu.VMEM((half, 2), F32),
            pltpu.VMEM((half, model), BF16),
            pltpu.VMEM((half, hidden), BF16),
            pltpu.VMEM((half, hidden), F32),
            pltpu.VMEM((half, model), F32),
            pltpu.VMEM((model, half), BF16),
            pltpu.VMEM((model, half), BF16),
            pltpu.VMEM((half, model), BF16),
            pltpu.VMEM((6, 8, model), F32),
            pltpu.VMEM((GROUPS,) + cube + (chunk, span), BF16),
            pltpu.VMEM((2,) + cube + (chunk, span), BF16),
            pltpu.VMEM(cube + (chunk, span), BF16),
            pltpu.VMEM((GROUPS, PARTS, 2, 2, 2, chunk, part_span), BF16),
            pltpu.VMEM((GROUPS, PARTS, 2, 2, chunk, part_span), BF16),
            pltpu.VMEM((GROUPS, PARTS, 2, chunk, part_span), BF16),
            pltpu.VMEM((GROUPS, PARTS, chunk, part_span), BF16),
            pltpu.VMEM((BITS + 1, 1, total), F32),
            pltpu.VMEM((BITS + 1, 1, total), F32),
            dma((9,)),
            dma((9,)),
            dma((9,)),
            dma((EXCHANGES, 5, CHUNKS)),
            dma((EXCHANGES, 5, CHUNKS)),
            dma((5,)),
            dma((5,)),
            dma((4,)),
            dma((EXCHANGES,)),
            dma((EXCHANGES,)),
            dma((EXCHANGES,)),
            dma((2,)),
            dma((2,)),
            dma((2,)),
            dma((GROUPS, PARTS)),
            dma((GROUPS, PARTS)),
            dma((GROUPS, PARTS, BITS)),
            dma((GROUPS, PARTS, BITS)),
            dma((2, BITS + 1)),
            dma((GROUPS, PARTS)),
            pltpu.SemaphoreType.REGULAR,
        ],
        compiler_params=pltpu.CompilerParams(
            collective_id=2, has_side_effects=True, vmem_limit_bytes=64 * MEBI
        ),
    )(*args)[:4]


def body(
    mesh,
    tokens,
    out_grad,
    doc_lengths,
    cluster_perm,
    query_weight,
    query_bias,
    key_weight,
    value_weight,
    value_bias,
    output_weight,
    output_bias,
    first_gain,
    first_shift,
    up_weight,
    up_bias,
    down_weight,
    down_bias,
    second_gain,
    second_shift,
):
    rows, model = tokens.shape
    half = rows // 2
    hidden = 2 * up_weight.shape[1]
    blocks = mesh.shape["seq"]
    seq, core = lax.axis_index("seq"), lax.axis_index("head")
    positions = seq * rows + jnp.arange(rows, dtype=jnp.int32)
    slot_start, slot_length = doc_lookup(doc_lengths, positions)
    source = slot_start + cluster_perm
    valid = (cluster_perm < slot_length).astype(F32).reshape(2, half // CLUSTER, 1, CLUSTER)
    valid = lax.dynamic_index_in_dim(valid, core, 0, keepdims=False)

    def row(v):
        return v.reshape(1, -1)

    rel = (source - seq * rows).reshape(rows, 1)
    chunk = model // blocks
    part_q, part_h = model // 2, hidden // 2
    order = ("q", "k", "v", "o", "up", "down")
    if blocks == 1 << BITS and chunk % 16 == 0 and hidden == 4 * model:
        order = ("down", "up", "o", "q", "k", "v")
        out_home, in_home, grad_sum, sums = whole(
            mesh,
            tokens,
            out_grad,
            doc_lengths,
            cluster_perm.reshape(rows // CLUSTER, CLUSTER),
            query_weight,
            key_weight,
            value_weight,
            output_weight,
            up_weight,
            down_weight,
            query_bias,
            value_bias,
            up_bias,
            output_bias,
            first_gain,
            first_shift,
            down_bias,
            second_gain,
            second_shift,
        )
    else:
        x, og, sources, wqkv, wo, wu, wd, bqkv, bu = entry(
            mesh,
            tokens,
            out_grad,
            rel,
            row(source),
            query_weight,
            key_weight,
            value_weight,
            output_weight,
            up_weight,
            down_weight,
            row(query_bias),
            row(value_bias),
            row(up_bias),
        )
        no_key = (jnp.arange(3 * model) // model != 1)[None, :]
        bqkv = jnp.where(no_key, bqkv, 0.0)
        reduce = chunk % 16 == 0 and blocks >= 4 and blocks & (blocks - 1) == 0
        out_low, in_low, grads, sums = layer(
            chunk if reduce else 48,
            x,
            og,
            valid,
            wqkv,
            wo,
            wu,
            wd,
            bqkv,
            row(output_bias),
            row(first_gain),
            row(first_shift),
            bu,
            row(down_bias),
            row(second_gain),
            row(second_shift),
        )
        if reduce:
            out_home, in_home, grad_sum, sums = leave(mesh, True, out_low, in_low, sources, grads, sums)
        else:
            out_home, in_home = leave(mesh, False, out_low, in_low, sources, None, None)
            sums = lax.psum(sums, ("seq", "head"))
            grads = grads.reshape(2, model, -1)
            grads = lax.psum_scatter(grads.astype(F32), "head", scatter_dimension=0, tiled=True)[0]
            grad_sum = lax.psum_scatter(grads, "seq", scatter_dimension=0, tiled=True)
    grad_of, place = {}, 0
    for name in order:
        size = part_h if name in ("up", "down") else part_q
        grad_of[name] = grad_sum[:, place : place + size]
        place += size
    sums = sums[0]

    def mine(start, size):
        return lax.dynamic_slice(sums, (start + core * size,), (size,))

    def block(index):
        return lax.dynamic_slice(sums, (2 * model + hidden + index * model + seq * chunk,), (chunk,))

    return (
        out_home.astype(F32),
        in_home.astype(F32),
        grad_of["q"],
        mine(0, part_q),
        grad_of["k"],
        grad_of["v"],
        mine(model, part_q),
        grad_of["o"].T,
        block(0),
        block(1),
        block(2),
        grad_of["up"],
        mine(2 * model, part_h),
        grad_of["down"].T,
        block(3),
        block(4),
        block(5),
    )


def solution(mesh):
    placed = (
        P("seq", None),
        P("seq", None),
        P(),
        P("seq"),
        P(None, "head"),
        P("head"),
        P(None, "head"),
        P(None, "head"),
        P("head"),
        P("head", None),
        P(),
        P(),
        P(),
        P(None, "head"),
        P("head"),
        P("head", None),
        P(),
        P(),
        P(),
    )
    return jax.shard_map(
        functools.partial(body, mesh),
        mesh=mesh,
        in_specs=placed,
        out_specs=(
            P("seq", None),
            P("seq", None),
            P("seq", "head"),
            P("head"),
            P("seq", "head"),
            P("seq", "head"),
            P("head"),
            P("head", "seq"),
            P("seq"),
            P("seq"),
            P("seq"),
            P("seq", "head"),
            P("head"),
            P("head", "seq"),
            P("seq"),
            P("seq"),
            P("seq"),
        ),
        check_vma=False,
    )
```

```python
import functools

import jax
import jax.numpy as jnp
from jax import lax
from jax.experimental import pallas as pl
from jax.experimental.pallas import tpu as pltpu
from jax.sharding import PartitionSpec as P

MESH = pl.DeviceIdType.MESH
HEAD_DIM = 64
CLUSTER = 128
OFFSETS = (0, 1, -1, 2, -2)
SLOT = {offset: slot for slot, offset in enumerate(OFFSETS)}
MEBI = 1 << 20

norm_eps = 1e-12
masked_score = -1e30
root_half = 0.7071067811865476
inv_root_tau = 0.3989422804014327
score_scale = HEAD_DIM ** (-0.5)

F32 = jnp.float32
BF16 = jnp.bfloat16


def doc_lookup(doc_lengths, positions):
    padded = (doc_lengths + CLUSTER - 1) // CLUSTER * CLUSTER
    starts = jnp.cumsum(padded) - padded
    doc_of = jnp.sum((starts[None, :] <= positions[:, None]).astype(jnp.int32), axis=1) - 1
    picked = jnp.arange(starts.shape[0], dtype=jnp.int32)[None, :] == doc_of[:, None]
    slot_start = jnp.sum(jnp.where(picked, starts[None, :], 0), axis=1)
    slot_length = jnp.sum(jnp.where(picked, doc_lengths[None, :], 0), axis=1)
    return (slot_start, slot_length)


def remote(src, dst, send, recv, device):
    return pltpu.make_async_remote_copy(
        src_ref=src, dst_ref=dst, send_sem=send, recv_sem=recv, device_id=device, device_id_type=MESH
    )


def greet(devices):
    pl.semaphore_wait(pltpu.get_barrier_semaphore(), greet_start(devices))


def greet_start(devices):
    barrier = pltpu.get_barrier_semaphore()
    count = 0
    for device, valid in devices:
        def hello(device=device):
            pl.semaphore_signal(barrier, inc=1, device_id=device, device_id_type=MESH)

        if valid is None:
            hello()
            count = count + 1
        else:
            pl.when(valid)(hello)
            count = count + valid.astype(jnp.int32)
    return count


def near(seq, core, blocks):
    out = {}
    for offset in OFFSETS[1:]:
        there = seq + offset
        out[offset] = ((there, core), (there >= 0) & (there < blocks))
    return out


def inner(left, right):
    return lax.dot_general(left, right, (((1,), (0,)), ((), ())), preferred_element_type=F32)


def outer(left, right):
    return lax.dot_general(left, right, (((1,), (1,)), ((), ())), preferred_element_type=F32)


def under(left, right):
    return lax.dot_general(left, right, (((0,), (0,)), ((), ())), preferred_element_type=F32)


def entry_kernel(
    blocks,
    tokens,
    out_grad,
    rel,
    source,
    wq,
    wk,
    wv,
    wo,
    wu,
    wd,
    bq,
    bv,
    bu,
    slot_tokens,
    slot_grad,
    sources,
    wqkv_full,
    wo_full,
    wu_full,
    wd_full,
    bqkv_full,
    bu_full,
    window,
    total,
    picked,
    source_win,
    wsend,
    wrecv,
    wlocal,
    send,
    recv,
    local,
    ssend,
    srecv,
    psend,
    precv,
    plocal,
):
    seq, core = lax.axis_index("seq"), lax.axis_index("head")
    rows, width = window.shape[2], window.shape[3]
    half = rows // 2
    partner = (seq, 1 - core)
    others = near(seq, core, blocks)
    greet([(partner, None)] + [others[offset] for offset in OFFSETS[1:]])

    mine = pl.ds(pl.multiple_of(core * width, width), width)
    arrays = (tokens, out_grad)
    locals_ = []
    for which, array in enumerate(arrays):
        for offset in OFFSETS[1:]:
            device, valid = others[offset]
            slot = SLOT[-offset]
            copy = remote(
                array.at[:, mine], window.at[which, slot], send.at[which, slot], recv.at[which, slot], device
            )
            pl.when(valid)(copy.start)
            if which == 0:
                tiny = remote(source, source_win.at[slot], ssend.at[slot], srecv.at[slot], device)
                pl.when(valid)(tiny.start)
        own = pltpu.make_async_copy(array.at[:, mine], window.at[which, 0], local.at[which])
        own.start()
        locals_.append(own)

    wide, deep = wq.shape[1], wd.shape[0]
    model = wq.shape[0]
    at_core = pl.multiple_of(core * wide, wide)
    at_deep = pl.multiple_of(core * deep, deep)
    pieces = []
    for i, array in enumerate((wq, wk, wv)):
        at = pl.multiple_of(i * model + core * wide, wide)
        pieces.append((array, wqkv_full.at[:, pl.ds(at, wide)]))
    pieces.append((wo, wo_full.at[pl.ds(at_core, wide), :]))
    pieces.append((wu, wu_full.at[:, pl.ds(at_deep, deep)]))
    pieces.append((wd, wd_full.at[pl.ds(at_deep, deep), :]))
    pieces.append((bq, bqkv_full.at[:, pl.ds(at_core, wide)]))
    pieces.append((bv, bqkv_full.at[:, pl.ds(pl.multiple_of(2 * model + core * wide, wide), wide)]))
    pieces.append((bu, bu_full.at[:, pl.ds(at_deep, deep)]))
    moves = []
    for i, (array, place) in enumerate(pieces):
        there = remote(array, place, wsend.at[i], wrecv.at[i], partner)
        here = pltpu.make_async_copy(array, place, wlocal.at[i])
        there.start()
        here.start()
        moves.append((there, here))

    source_win[0] = source[...]
    for offset in OFFSETS[1:]:

        def blank(slot=SLOT[offset]):
            source_win[slot] = jnp.full(source.shape, -1, jnp.int32)

        pl.when(jnp.logical_not(others[offset][1]))(blank)
    tile = 256
    outs = (slot_tokens, slot_grad)
    finals = []
    for which in range(2):
        locals_[which].wait()
        for offset in OFFSETS:
            slot = SLOT[offset]

            def add(which=which, offset=offset, slot=slot):
                if offset != 0:
                    device, _ = others[offset]
                    remote(
                        arrays[which].at[:, mine],
                        window.at[which, slot],
                        send.at[which, slot],
                        recv.at[which, slot],
                        device,
                    ).wait_recv()

                @pl.loop(0, rows // tile)
                def _(step):
                    at = pl.ds(pl.multiple_of(step * tile, tile), tile)
                    wanted = rel[at, :] - offset * rows
                    lanes = lax.broadcasted_iota(jnp.int32, (tile, rows), 1)
                    chosen = jnp.where(lanes == wanted, 1.0, 0.0).astype(BF16)
                    part = inner(chosen, window[which, slot])
                    if offset == 0:
                        total[at, :] = part
                    else:
                        total[at, :] += part

            if offset == 0:
                add()
            else:
                pl.when(others[offset][1])(add)
        picked[which] = total[...].astype(BF16)
        keep = pl.ds(pl.multiple_of(core * half, half), half)
        give = pl.ds(pl.multiple_of((1 - core) * half, half), half)
        there = remote(
            picked.at[which, give], outs[which].at[:, mine], psend.at[which], precv.at[which], partner
        )
        here = pltpu.make_async_copy(picked.at[which, keep], outs[which].at[:, mine], plocal.at[which])
        there.start()
        here.start()
        finals.append((there, here))

    for offset in OFFSETS[1:]:
        device, valid = others[offset]

        def finish(offset=offset, device=device):
            for which in range(2):
                slot = SLOT[-offset]
                remote(
                    arrays[which].at[:, mine],
                    window.at[which, slot],
                    send.at[which, slot],
                    recv.at[which, slot],
                    device,
                ).wait_send()
            slot = SLOT[-offset]
            remote(source, source_win.at[slot], ssend.at[slot], srecv.at[slot], device).wait_send()
            slot = SLOT[offset]
            remote(source, source_win.at[slot], ssend.at[slot], srecv.at[slot], device).wait_recv()

        pl.when(valid)(finish)
    sources[...] = source_win[...]
    for there, here in moves + finals:
        there.wait()
        here.wait()


def entry(mesh, tokens, out_grad, rel, source, wq, wk, wv, wo, wu, wd, bq, bv, bu):
    rows, model = tokens.shape
    width = model // 2
    hidden = 2 * wu.shape[1]
    hbm = pl.BlockSpec(memory_space=pl.ANY)
    vmem = pl.BlockSpec(memory_space=pltpu.VMEM)
    slots = len(OFFSETS)
    dma = pltpu.SemaphoreType.DMA
    return pl.pallas_call(
        functools.partial(entry_kernel, mesh.shape["seq"]),
        out_shape=(
            jax.ShapeDtypeStruct((rows // 2, model), BF16),
            jax.ShapeDtypeStruct((rows // 2, model), BF16),
            jax.ShapeDtypeStruct((slots, 1, rows), jnp.int32),
            jax.ShapeDtypeStruct((model, 3 * model), BF16),
            jax.ShapeDtypeStruct((model, model), BF16),
            jax.ShapeDtypeStruct((model, hidden), BF16),
            jax.ShapeDtypeStruct((hidden, model), BF16),
            jax.ShapeDtypeStruct((1, 3 * model), F32),
            jax.ShapeDtypeStruct((1, hidden), F32),
        ),
        in_specs=[hbm, hbm, vmem, vmem] + [hbm] * 9,
        out_specs=(hbm, hbm, vmem) + (hbm,) * 6,
        scratch_shapes=[
            pltpu.VMEM((2, slots, rows, width), BF16),
            pltpu.VMEM((rows, width), F32),
            pltpu.VMEM((2, rows, width), BF16),
            pltpu.VMEM((slots, 1, rows), jnp.int32),
            dma((9,)),
            dma((9,)),
            dma((9,)),
            dma((2, slots)),
            dma((2, slots)),
            dma((2,)),
            dma((slots,)),
            dma((slots,)),
            dma((2,)),
            dma((2,)),
            dma((2,)),
        ],
        compiler_params=pltpu.CompilerParams(
            collective_id=0, has_side_effects=True, vmem_limit_bytes=40 * MEBI
        ),
    )(tokens, out_grad, rel, source, wq, wk, wv, wo, wu, wd, bq, bv, bu)


def fold_rows(values):
    return jnp.sum(values.reshape(values.shape[0] // 8, 8, values.shape[1]), axis=0)


def layer_kernel(
    chunk,
    x,
    og,
    valid,
    wqkv,
    wo,
    wu,
    wd,
    bqkv,
    bo,
    g1,
    s1,
    bu,
    bd,
    g2,
    s2,
    out_low,
    in_low,
    grads,
    sums,
    qkv,
    ctx,
    prob,
    hat1,
    inv1,
    low1,
    act,
    slope,
    pre_low,
    work,
    flipped,
    dqkv,
    cgrad,
    low2,
    gtile,
    accs,
    gsem,
):
    rows, model = x.shape
    hidden = wu.shape[1]
    clusters = rows // CLUSTER
    pairs = model // 128
    tile = 256
    band = 64

    def at(step, size):
        return pl.ds(pl.multiple_of(step * size, size), size)

    lanes = lax.broadcasted_iota(jnp.int32, (CLUSTER, 128), 1)
    first_f = jnp.where(lanes < HEAD_DIM, 1.0, 0.0)
    first = first_f.astype(BF16)
    second = (1.0 - first_f).astype(BF16)

    def stacked(pair):
        return jnp.concatenate([pair * first, pair * second], axis=0)

    def beside(tall):
        return jnp.concatenate([tall[:CLUSTER], tall[CLUSTER:]], axis=1)

    @pl.loop(0, 3 * model // tile)
    def _(step):
        cols = at(step, tile)
        qkv[:, cols] = (inner(x[...], wqkv[:, cols]) + bqkv[:, cols]).astype(BF16)

    @pl.loop(0, clusters * pairs)
    def _(step):
        cluster, pair = step // pairs, step % pairs
        r = at(cluster, CLUSTER)
        q = qkv[r, at(pair, 128)]
        k = qkv[r, pl.ds(pl.multiple_of(model + pair * 128, 128), 128)]
        v = qkv[r, pl.ds(pl.multiple_of(2 * model + pair * 128, 128), 128)]
        scores = outer(stacked(q), k) * score_scale
        scores = jnp.where(valid[cluster] > 0.5, scores, masked_score)
        top = jnp.max(scores, axis=-1, keepdims=True)
        weight = jnp.exp(scores - top)
        p = weight / jnp.sum(weight, axis=-1, keepdims=True)
        prob[step] = p
        ctx[r, at(pair, 128)] = inner(beside(p.astype(BF16)), stacked(v)).astype(BF16)

    @pl.loop(0, model // tile)
    def _(step):
        cols = at(step, tile)
        hat1[:, cols] = inner(ctx[...], wo[:, cols]) + x[:, cols].astype(F32) + bo[:, cols]

    @pl.loop(0, rows // band)
    def _(step):
        r = at(step, band)
        h = hat1[r, :]
        centered = h - jnp.mean(h, axis=-1, keepdims=True)
        inv = lax.rsqrt(jnp.mean(centered * centered, axis=-1, keepdims=True) + norm_eps)
        hat = centered * inv
        hat1[r, :] = hat
        inv1[r, :] = inv
        low1[r, :] = (hat * g1[...] + s1[...]).astype(BF16)

    @pl.loop(0, hidden // tile)
    def _(step):
        cols = at(step, tile)
        pre = inner(low1[...], wu[:, cols]) + bu[:, cols]
        cdf = 0.5 * (1.0 + lax.erf(pre * root_half))
        act[:, cols] = (pre * cdf).astype(BF16)
        slope[:, cols] = cdf + pre * jnp.exp(-0.5 * pre * pre) * inv_root_tau

    @pl.loop(0, model // tile)
    def _(step):
        cols = at(step, tile)
        norm = hat1[:, cols] * g1[:, cols] + s1[:, cols]
        work[:, cols] = inner(act[...], wd[:, cols]) + norm + bd[:, cols]

    accs[...] = jnp.zeros_like(accs)

    @pl.loop(0, rows // band)
    def _(step):
        r = at(step, band)
        h = work[r, :]
        centered = h - jnp.mean(h, axis=-1, keepdims=True)
        inv = lax.rsqrt(jnp.mean(centered * centered, axis=-1, keepdims=True) + norm_eps)
        hat = centered * inv
        out_low[r, :] = (hat * g2[...] + s2[...]).astype(BF16)
        grad = og[r, :].astype(F32)
        accs[4] += fold_rows(grad * hat)
        accs[5] += fold_rows(grad)
        scaled = grad * g2[...]
        back = inv * (
            scaled
            - jnp.mean(scaled, axis=-1, keepdims=True)
            - hat * jnp.mean(scaled * hat, axis=-1, keepdims=True)
        )
        accs[3] += fold_rows(back)
        work[r, :] = back
        low2[r, :] = back.astype(BF16)

    def flip(source):
        @pl.loop(0, model // 128)
        def _(step):
            flipped[at(step, 128), :] = source[:, at(step, 128)].T

    half_rows = model // 2
    chunks = half_rows // chunk

    def product_tiles(right, width, places, count):
        def moves(index, slot):
            m, n = index // count, index % count
            for piece, (part, start, size) in enumerate(places(n)):
                yield pltpu.make_async_copy(
                    gtile.at[slot, :, :, pl.ds(piece * size, size)] if size != width
                    else gtile.at[slot, :, :, pl.ds(0, width)],
                    grads.at[part, pl.ds(m * chunks, chunks), :, pl.ds(start, size)],
                    gsem.at[slot, piece],
                )

        total = 2 * count

        @pl.loop(0, total)
        def _(index):
            slot = index % 2
            m, n = index // count, index % count

            @pl.when(index >= 2)
            def _():
                for move in moves(index - 2, slot):
                    move.wait()

            value = inner(flipped[at(m, half_rows), :], right[:, at(n, width)])
            gtile[slot, :, :, pl.ds(0, width)] = value.reshape(chunks, chunk, width).astype(BF16)
            for move in moves(index, slot):
                move.start()

        for index in range(max(total - 2, 0), total):
            for move in moves(index, index % 2):
                move.wait()

    part_q = model // 2
    part_h = hidden // 2
    wide = 512

    def square(which):
        def places(n):
            return [(0, which * part_q, part_q), (1, which * part_q, part_q)]

        return places

    def long(base):
        per_part = part_h // wide

        def places(n):
            part, inside = n // per_part, n % per_part
            return [(part, pl.multiple_of(base + inside * wide, 128), wide)]

        return places

    flip(low2)
    product_tiles(act, wide, long(4 * part_q + part_h), hidden // wide)

    @pl.loop(0, hidden // tile)
    def _(step):
        cols = at(step, tile)
        back = outer(low2[...], wd[cols, :]) * slope[:, cols]
        back = back.astype(BF16)
        pre_low[:, cols] = back
        sums[:, pl.ds(pl.multiple_of(2 * model + step * tile, tile), tile)] = jnp.sum(
            back.astype(F32), axis=0, keepdims=True
        )

    flip(low1)
    product_tiles(pre_low, wide, long(4 * part_q), hidden // wide)

    @pl.loop(0, model // tile)
    def _(step):
        cols = at(step, tile)
        work[:, cols] += outer(pre_low[...], wu[cols, :])

    @pl.loop(0, rows // band)
    def _(step):
        r = at(step, band)
        grad = work[r, :]
        hat = hat1[r, :]
        accs[1] += fold_rows(grad * hat)
        accs[2] += fold_rows(grad)
        scaled = grad * g1[...]
        back = inv1[r, :] * (
            scaled
            - jnp.mean(scaled, axis=-1, keepdims=True)
            - hat * jnp.mean(scaled * hat, axis=-1, keepdims=True)
        )
        accs[0] += fold_rows(back)
        work[r, :] = back
        low2[r, :] = back.astype(BF16)

    flip(low2)
    product_tiles(ctx, model, square(3), 1)

    @pl.loop(0, model // tile)
    def _(step):
        cols = at(step, tile)
        cgrad[:, cols] = outer(low2[...], wo[cols, :]).astype(BF16)

    @pl.loop(0, clusters * pairs)
    def _(step):
        cluster, pair = step // pairs, step % pairs
        r = at(cluster, CLUSTER)
        at_q = at(pair, 128)
        at_k = pl.ds(pl.multiple_of(model + pair * 128, 128), 128)
        at_v = pl.ds(pl.multiple_of(2 * model + pair * 128, 128), 128)
        q, k, v = qkv[r, at_q], qkv[r, at_k], qkv[r, at_v]
        p = prob[step]
        dctx = stacked(cgrad[r, at_q])
        dprob = outer(dctx, v)
        dscore = (p * (dprob - jnp.sum(p * dprob, axis=-1, keepdims=True))).astype(BF16)
        dqkv[r, at_q] = (inner(beside(dscore), stacked(k)) * score_scale).astype(BF16)
        dqkv[r, at_k] = (under(dscore, stacked(q)) * score_scale).astype(BF16)
        dqkv[r, at_v] = under(p.astype(BF16), dctx).astype(BF16)

    flip(x)
    for which in range(3):
        product_tiles(dqkv.at[:, pl.ds(which * model, model)], model, square(which), 1)

    for which in range(2):
        @pl.loop(0, model // tile)
        def _(step, which=which):
            value = dqkv[:, pl.ds(pl.multiple_of(2 * which * model + step * tile, tile), tile)]
            sums[:, pl.ds(pl.multiple_of(which * model + step * tile, tile), tile)] = jnp.sum(
                value.astype(F32), axis=0, keepdims=True
            )

    @pl.loop(0, model // tile)
    def _(step):
        cols = at(step, tile)
        in_low[:, cols] = (work[:, cols] + outer(dqkv[...], wqkv[cols, :])).astype(BF16)

    for i in range(6):
        sums[:, pl.ds(2 * model + hidden + i * model, model)] = jnp.sum(accs[i], axis=0, keepdims=True)


def layer(chunk, x, og, valid, wqkv, wo, wu, wd, bqkv, bo, g1, s1, bu, bd, g2, s2):
    rows, model = x.shape
    hidden = wu.shape[1]
    hbm = pl.BlockSpec(memory_space=pl.ANY)
    vmem = pl.BlockSpec(memory_space=pltpu.VMEM)
    part = 2 * model + hidden
    steps = rows // CLUSTER * (model // 128)
    total = 8 * model + hidden
    return pl.pallas_call(
        functools.partial(layer_kernel, chunk),
        out_shape=(
            jax.ShapeDtypeStruct((rows, model), BF16),
            jax.ShapeDtypeStruct((rows, model), BF16),
            jax.ShapeDtypeStruct((2, model // chunk, chunk, part), BF16),
            jax.ShapeDtypeStruct((1, total), F32),
        ),
        in_specs=[vmem] * 15,
        out_specs=(vmem, vmem, hbm, vmem),
        scratch_shapes=[
            pltpu.VMEM((rows, 3 * model), BF16),
            pltpu.VMEM((rows, model), BF16),
            pltpu.VMEM((steps, 2 * CLUSTER, CLUSTER), F32),
            pltpu.VMEM((rows, model), F32),
            pltpu.VMEM((rows, 1), F32),
            pltpu.VMEM((rows, model), BF16),
            pltpu.VMEM((rows, hidden), BF16),
            pltpu.VMEM((rows, hidden), F32),
            pltpu.VMEM((rows, hidden), BF16),
            pltpu.VMEM((rows, model), F32),
            pltpu.VMEM((model, rows), BF16),
            pltpu.VMEM((rows, 3 * model), BF16),
            pltpu.VMEM((rows, model), BF16),
            pltpu.VMEM((rows, model), BF16),
            pltpu.VMEM((2, model // 2 // chunk, chunk, model), BF16),
            pltpu.VMEM((6, 8, model), F32),
            pltpu.SemaphoreType.DMA((2, 2)),
        ],
        compiler_params=pltpu.CompilerParams(vmem_limit_bytes=60 * MEBI),
    )(x, og, valid, wqkv, wo, wu, wd, bqkv, bo, g1, s1, bu, bd, g2, s2)


def exit_kernel(blocks, reduce, *refs):
    if reduce:
        (out_low, in_low, sources, grads, sums, out_home, in_home, grad_sum, sums_sum, *scratch) = refs
        (window, home, wsend, wrecv, csend, crecv, clocal, hsend, hrecv, hlocal, *scratch) = scratch
        (mine_g, from_core, got, gsend, grecv, glocal, rsend, rrecv, vrecv, vsend, vsem) = scratch
    else:
        (out_low, in_low, sources, out_home, in_home, *scratch) = refs
        (window, home, wsend, wrecv, csend, crecv, clocal, hsend, hrecv, hlocal) = scratch
    seq, core = lax.axis_index("seq"), lax.axis_index("head")
    rows, width = window.shape[2], window.shape[3]
    half = rows // 2
    partner = (seq, 1 - core)
    others = near(seq, core, blocks)
    bits = max(blocks.bit_length() - 1, 0)
    greetings = [(partner, None)] + [others[offset] for offset in OFFSETS[1:]]

    def across(bit):
        mask = 1 << bit
        return (seq + mask - 2 * mask * ((seq // mask) % 2), core)

    if reduce:
        greetings += [(across(bit), None) for bit in range(2, bits)]
    greet(greetings)

    mine = pl.ds(pl.multiple_of(core * width, width), width)
    theirs = pl.ds(pl.multiple_of((1 - core) * width, width), width)
    keep = pl.ds(pl.multiple_of(core * half, half), half)
    arrays = (out_low, in_low)
    firsts = []
    for which, array in enumerate(arrays):
        there = remote(
            array.at[:, theirs], window.at[which, 0, keep], csend.at[which], crecv.at[which], partner
        )
        here = pltpu.make_async_copy(array.at[:, mine], window.at[which, 0, keep], clocal.at[which])
        there.start()
        here.start()
        firsts.append((there, here))

    if reduce:
        parts = 2
        span = mine_g.shape[3] // parts
        core_moves = []
        for part in range(parts):
            cols = pl.ds(part * span, span)
            there = remote(
                grads.at[1 - core, :, :, cols], from_core.at[:, :, cols], gsend.at[part], grecv.at[part], partner
            )
            here = pltpu.make_async_copy(grads.at[core, :, :, cols], mine_g.at[0, :, :, cols], glocal.at[part])
            there.start()
            here.start()
            core_moves.append((there, here))

    def spread(which):
        for offset in OFFSETS[1:]:
            device, valid = others[offset]
            slot = SLOT[-offset]
            pl.when(valid)(
                remote(
                    window.at[which, 0], window.at[which, slot], wsend.at[which, slot], wrecv.at[which, slot], device
                ).start
            )

    for which in range(2):
        there, here = firsts[which]
        there.wait()
        here.wait()
        spread(which)

    def reduce_start(part, level):
        cols = pl.ds(part * span, span)
        order = orders[part]
        bit = order[level]
        own = (seq // (1 << bit)) % 2
        left = sorted(set(range(bits)) - set(order[:level]))
        low = 1 << left.index(bit)
        high = (1 << len(left)) // (2 * low)
        outs = []
        for top in range(high):
            src = mine_g.at[level % 2, pl.ds(pl.multiple_of((top * 2 + 1 - own) * low, low), low), :, cols]
            dst = got.at[pl.ds(base[level] + top * low, low), :, cols]
            outs.append(remote(src, dst, rsend.at[part, level, top], rrecv.at[part, level, top], across(bit)))
        return outs, own, low, high, cols

    def reduce_finish(part, level, state):
        outs, own, low, high, cols = state
        for copy in outs:
            copy.wait()
        for top in range(high):
            @pl.loop(0, low)
            def _(inside):
                held = mine_g[level % 2, (top * 2 + own) * low + inside, :, cols].astype(F32)
                other = got[base[level] + top * low + inside, :, cols].astype(F32)
                value = held + other
                if level == bits - 1:
                    grad_sum[:, cols] = value
                else:
                    mine_g[(level + 1) % 2, top * low + inside, :, cols] = value.astype(BF16)

    def pick(which):
        tile = 256
        for offset in OFFSETS:
            slot = SLOT[offset]

            def add(offset=offset, slot=slot):
                if offset != 0:
                    device, _ = others[offset]
                    remote(
                        window.at[which, 0],
                        window.at[which, slot],
                        wsend.at[which, slot],
                        wrecv.at[which, slot],
                        device,
                    ).wait_recv()

                @pl.loop(0, rows // tile)
                def _(step):
                    at = pl.ds(pl.multiple_of(step * tile, tile), tile)
                    places = lax.broadcasted_iota(jnp.int32, (tile, rows), 0) + (step * tile + seq * rows)
                    chosen = jnp.where(sources[slot] == places, 1.0, 0.0).astype(BF16)
                    part = inner(chosen, window[which, slot]).astype(BF16)
                    if offset == 0:
                        home[which, at, :] = part
                    else:
                        home[which, at, :] += part

            if offset == 0:
                add()
            else:
                pl.when(others[offset][1])(add)
        target = (out_home, in_home)[which]
        there = remote(home.at[which], target.at[:, mine], hsend.at[which], hrecv.at[which], partner)
        here = pltpu.make_async_copy(home.at[which], target.at[:, mine], hlocal.at[which])
        there.start()
        here.start()
        return there, here

    lasts = []
    if not reduce:
        lasts = [pick(0), pick(1)]
    else:
        orders = ([0, 1] + list(range(bits - 1, 1, -1)), [1, 0] + list(range(bits - 1, 1, -1)))
        base, count = [], 0
        for level in range(bits):
            base.append(count)
            count += blocks >> (level + 1)

        def sum_level(level):
            device = partner if level == 0 else across(level - 1)
            return remote(vsend.at[level], vrecv.at[level], vsem.at[0, level], vsem.at[1, level], device)

        def sum_start(level):
            if level == 0:
                vsend[0] = sums[...]
            sum_level(level).start()

        def sum_finish(level):
            sum_level(level).wait()
            value = vsend[level] + vrecv[level]
            if level == bits:
                sums_sum[...] = value
            else:
                vsend[level + 1] = value

        sum_start(0)
        states = [None] * parts
        for part in range(parts):
            there, here = core_moves[part]
            there.wait()
            here.wait()
            cols = pl.ds(part * span, span)

            @pl.loop(0, blocks)
            def _(inside):
                value = mine_g[0, inside, :, cols].astype(F32) + from_core[inside, :, cols].astype(F32)
                mine_g[0, inside, :, cols] = value.astype(BF16)

            states[part] = reduce_start(part, 0)
            for copy in states[part][0]:
                copy.start()
        sum_finish(0)
        sum_start(1)
        lasts.append(pick(0))
        for level in range(bits):
            for part in range(parts):
                reduce_finish(part, level, states[part])
                if level + 1 < bits:
                    states[part] = reduce_start(part, level + 1)
                    for copy in states[part][0]:
                        copy.start()
            sum_finish(level + 1)
            if level + 1 < bits:
                sum_start(level + 2)
            if level == 1:
                lasts.append(pick(1))
        if bits < 2:
            lasts.append(pick(1))

    for offset in OFFSETS[1:]:
        device, valid = others[offset]
        slot = SLOT[-offset]

        def finish(device=device, slot=slot):
            for which in range(2):
                remote(
                    window.at[which, 0], window.at[which, slot], wsend.at[which, slot], wrecv.at[which, slot], device
                ).wait_send()

        pl.when(valid)(finish)
    for there, here in lasts:
        there.wait()
        here.wait()


def leave(mesh, reduce, out_low, in_low, sources, grads, sums):
    half, model = out_low.shape
    rows, width = 2 * half, model // 2
    blocks = mesh.shape["seq"]
    slots = len(OFFSETS)
    hbm = pl.BlockSpec(memory_space=pl.ANY)
    vmem = pl.BlockSpec(memory_space=pltpu.VMEM)
    dma = pltpu.SemaphoreType.DMA
    out_shape = [jax.ShapeDtypeStruct((rows, model), BF16)] * 2
    out_specs = [hbm, hbm]
    in_specs = [hbm, hbm, vmem]
    args = [out_low, in_low, sources]
    scratch = [
        pltpu.VMEM((2, slots, rows, width), BF16),
        pltpu.VMEM((2, rows, width), BF16),
        dma((2, slots)),
        dma((2, slots)),
        dma((2,)),
        dma((2,)),
        dma((2,)),
        dma((2,)),
        dma((2,)),
        dma((2,)),
    ]
    if reduce:
        _, chunks, chunk, span = grads.shape
        bits = blocks.bit_length() - 1
        args += [grads, sums]
        in_specs += [hbm, vmem]
        out_shape += [jax.ShapeDtypeStruct((chunk, span), F32), jax.ShapeDtypeStruct(sums.shape, F32)]
        out_specs += [vmem, vmem]
        scratch += [
            pltpu.VMEM((2, blocks, chunk, span), BF16),
            pltpu.VMEM((blocks, chunk, span), BF16),
            pltpu.VMEM((blocks, chunk, span), BF16),
            dma((2,)),
            dma((2,)),
            dma((2,)),
            dma((2, bits, blocks // 2)),
            dma((2, bits, blocks // 2)),
            pltpu.VMEM((bits + 1,) + sums.shape, F32),
            pltpu.VMEM((bits + 1,) + sums.shape, F32),
            dma((2, bits + 1)),
        ]
    return pl.pallas_call(
        functools.partial(exit_kernel, blocks, reduce),
        out_shape=tuple(out_shape),
        in_specs=in_specs,
        out_specs=tuple(out_specs),
        scratch_shapes=scratch,
        compiler_params=pltpu.CompilerParams(
            collective_id=1, has_side_effects=True, vmem_limit_bytes=60 * MEBI
        ),
    )(*args)


FROM_X, FROM_Y, FROM_Z, FROM_LAST, RELAY = range(5)
OWN = -1
EXCHANGES = 4
CHUNKS = 4
GROUPS = 3
PARTS = 3
BITS = 4


def whole_kernel(
    blocks,
    tokens,
    out_grad,
    doc_lengths,
    cluster_perm,
    wq,
    wk,
    wv,
    wo_half,
    wu_half,
    wd_half,
    bq,
    bv,
    bu_half,
    bo_in,
    g1_in,
    s1_in,
    bd_in,
    g2_in,
    s2_in,
    out_home,
    in_home,
    grad_sum,
    sums_sum,
    win,
    wqkv,
    wo,
    wu,
    wd,
    bqkv,
    bu,
    stage,
    picked,
    block,
    source,
    sources,
    rel,
    valid,
    vectors,
    x,
    og,
    qkv,
    ctx,
    prob,
    hat1,
    inv12,
    low1,
    act,
    slope,
    work,
    flipped,
    flipped_x,
    in_low,
    accs,
    mine_g,
    from_core,
    give,
    got0,
    got1,
    got2,
    got3,
    vsend,
    vrecv,
    wsend,
    wrecv,
    wlocal,
    xsend,
    xrecv,
    ssend,
    srecv,
    ssem,
    psend,
    precv,
    plocal,
    hsend,
    hrecv,
    hlocal,
    gsend,
    grecv,
    rsend,
    rrecv,
    vsem,
    osem,
    credit,
):
    seq, core = lax.axis_index("seq"), lax.axis_index("head")
    px, py = seq % 2, (seq // 2) % 2
    rows, width = tokens.shape[0], picked.shape[2]
    half, model = x.shape
    hidden = wu.shape[1]
    clusters = half // CLUSTER
    pairs = model // 128
    part_rows = rows // CHUNKS
    tile = 256
    band = 64

    low2 = og

    partner = (seq, 1 - core)
    x_next = seq + 1 - 2 * px
    y_next = seq + 2 - 4 * py
    z_to = seq + 4 - 8 * py
    z_from = seq - 4 + 8 * py
    to_ok = (z_to >= 0) & (z_to < blocks)
    from_ok = (z_from >= 0) & (z_from < blocks)
    level_chip = px == py
    off_chip = px != py
    last_next = x_next + core * (y_next - x_next)
    relay_send = (core == 1) & off_chip & from_ok
    relay_recv = (core == 1) & off_chip & to_ok
    later_ok = off_chip & (((core == 0) & from_ok) | ((core == 1) & to_ok))
    last_ok = off_chip | from_ok
    offsets = {
        OWN: 0,
        FROM_X: 1 - 2 * px,
        FROM_Y: 2 - 4 * py,
        FROM_Z: 4 * py - 2,
        FROM_LAST: 2 * px - 1,
    }
    arrived = {OWN: None, FROM_X: None, FROM_Y: None, FROM_Z: from_ok, FROM_LAST: last_ok}
    others = near(seq, core, blocks)

    def across(bit):
        mask = 1 << bit
        return (seq + mask - 2 * mask * ((seq // mask) % 2), core)

    greetings = [(partner, None), ((x_next, core), None), ((y_next, core), None)]
    greetings += [((z_to, core), to_ok), ((z_from, core), from_ok)]
    greetings += [others[offset] for offset in OFFSETS[1:]]
    greetings += [(across(bit), None) for bit in range(3, BITS)]
    arrivals = greet_start(greetings)

    def at(step, size):
        return pl.ds(pl.multiple_of(step * size, size), size)

    def when(condition, action):
        if condition is None:
            action()
        else:
            pl.when(condition)(action)

    mine = at(core, width)
    theirs = at(1 - core, width)
    keep = at(core, half)
    other_rows = at(1 - core, half)

    def piece(chunk):
        return pl.ds(chunk * part_rows, part_rows)

    def own_rows(e, chunk):
        if e < 2:
            return (tokens, out_grad)[e].at[piece(chunk), mine]
        return block.at[e - 2, piece(chunk)]

    def hop(e, kind, chunk, src, there):
        return remote(
            src,
            win.at[e, kind, piece(chunk)],
            xsend.at[e, kind, chunk],
            xrecv.at[e, kind, chunk],
            (there, core),
        )

    def held(e, kind, chunk):
        return win.at[e, kind, piece(chunk)]

    def hop_x(e, chunk):
        return hop(e, FROM_X, chunk, own_rows(e, chunk), x_next)

    def hop_y(e, chunk):
        return hop(e, FROM_Y, chunk, own_rows(e, chunk), y_next)

    def hop_z(e, chunk):
        return hop(e, FROM_Z, chunk, held(e, FROM_Y, chunk), z_to)

    def hop_relay(e, chunk):
        return hop(e, RELAY, chunk, held(e, FROM_X, chunk), z_from)

    def hop_last_early(e, chunk):
        return hop(e, FROM_LAST, chunk, held(e, 1 - core, chunk), last_next)

    def hop_last_late(e, chunk):
        return hop(e, FROM_LAST, chunk, held(e, 2 + 2 * core, chunk), last_next)

    def send_own(e):
        for chunk in range(CHUNKS):
            hop_y(e, chunk).start()
            hop_x(e, chunk).start()

    def first_hop(e, chunk):
        hop_y(e, chunk).wait_recv()
        pl.when(to_ok)(hop_z(e, chunk).start)
        hop_x(e, chunk).wait_recv()
        pl.when(level_chip)(hop_last_early(e, chunk).start)
        pl.when(relay_send)(hop_relay(e, chunk).start)

    def second_hop(e, chunk):
        pl.when(from_ok)(hop_z(e, chunk).wait_recv)
        pl.when(relay_recv)(hop_relay(e, chunk).wait_recv)
        pl.when(later_ok)(hop_last_late(e, chunk).start)

    def last_hop(e, chunk):
        pl.when(last_ok)(hop_last_early(e, chunk).wait_recv)

    def all_sent(e):
        for chunk in range(CHUNKS):
            hop_x(e, chunk).wait_send()
            hop_y(e, chunk).wait_send()
            pl.when(to_ok)(hop_z(e, chunk).wait_send)
            pl.when(relay_send)(hop_relay(e, chunk).wait_send)
            pl.when(level_chip)(hop_last_early(e, chunk).wait_send)
            pl.when(later_ok)(hop_last_late(e, chunk).wait_send)

    def span_of(side):
        return pl.ds(side * half, half)

    def pick(e, units, fresh=False):
        which = e % 2
        moves = {}
        for index, (kind, side) in enumerate(units):
            if kind == OWN and e >= 2:
                continue
            if kind == OWN:
                src = (tokens, out_grad)[e].at[span_of(side), mine]
            else:
                src = win.at[e, kind, span_of(side)]
            moves[index] = pltpu.make_async_copy(src, stage.at[index], ssem.at[index])
            when(arrived[kind], moves[index].start)
        for index, (kind, side) in enumerate(units):

            def add(index=index, kind=kind, side=side):
                if index in moves:
                    moves[index].wait()
                offset = offsets[kind]
                if e < 2:
                    wanted = rel[:, pl.ds(0, 1)] - (offset * rows + side * half)
                    places = lax.broadcasted_iota(jnp.int32, (rows, half), 1)
                else:
                    wanted = sources[offset + 2, :, span_of(side)] - seq * rows
                    places = lax.broadcasted_iota(jnp.int32, (rows, half), 0)
                chosen = jnp.where(places == wanted, 1.0, 0.0).astype(BF16)
                block_rows = stage[index] if index in moves else block[e - 2, span_of(side), :]
                value = inner(chosen, block_rows).astype(BF16)
                if fresh and index == 0:
                    picked[which] = value
                else:
                    picked[which] += value

            when(arrived[kind], add)

    def deliver(e):
        target = (x, og)[e]
        there = remote(picked.at[e, other_rows], target.at[:, mine], psend.at[e], precv.at[e], partner)
        here = pltpu.make_async_copy(picked.at[e, keep], target.at[:, mine], plocal.at[e])
        return there, here

    def collect(e):
        array = in_low
        there = remote(array.at[:, theirs], block.at[e - 2, keep], psend.at[e], precv.at[e], partner)
        here = pltpu.make_async_copy(array.at[:, mine], block.at[e - 2, keep], plocal.at[e])
        return there, here

    def bring_home(e):
        target = (out_home, in_home)[e - 2]
        there = remote(picked.at[e - 2], target.at[:, mine], hsend.at[e - 2], hrecv.at[e - 2], partner)
        here = pltpu.make_async_copy(picked.at[e - 2], target.at[:, mine], hlocal.at[e - 2])
        return there, here

    def begin(pair):
        for copy in pair:
            copy.start()

    def end(pair):
        for copy in pair:
            copy.wait()

    orders = ((0, 2, 1, 3), (1, 2, 0, 3), (2, 1, 0, 3))
    gots = (got0, got1, got2, got3)
    span = mine_g.shape[-1]
    part_span = span // PARTS

    def part_cols(part):
        return pl.ds(part * part_span, part_span)

    def own_bit(bit):
        return (seq // (1 << bit)) % 2

    def halving(group, part, level):
        order = orders[part]
        index = []
        for bit in (3, 2, 1, 0):
            if bit in order[:level]:
                index.append(own_bit(bit))
            elif bit == order[level]:
                index.append(1 - own_bit(bit))
            else:
                index.append(slice(None))
        src = mine_g.at[(group, *index, slice(None), part_cols(part))]
        dst = gots[level].at[group, part]
        return remote(
            src, dst, rsend.at[group, part, level], rrecv.at[group, part, level], across(order[level])
        )

    def halving_end(group, part, level):
        halving(group, part, level).wait()
        order = orders[part]
        left = [bit for bit in (3, 2, 1, 0) if bit not in order[: level + 1]]
        cols = part_cols(part)
        finals = slope.at[pl.ds(group * chunk_rows, chunk_rows), :]

        @pl.loop(0, 1 << len(left))
        def _(step):
            digits = {bit: (step // (1 << (len(left) - 1 - i))) % 2 for i, bit in enumerate(left)}
            place = [digits[bit] if bit in digits else own_bit(bit) for bit in (3, 2, 1, 0)]
            value = mine_g[(group, *place, slice(None), cols)].astype(F32)
            other = gots[level][(group, part, *[digits[bit] for bit in left])]
            value = value + other.astype(F32)
            if level == BITS - 1:
                finals[:, cols] = value
            else:
                mine_g[(group, *place, slice(None), cols)] = value.astype(BF16)

    def advance(group, level):
        for part in range(PARTS):
            halving_end(group, part, level)
            if level + 1 < BITS:
                halving(group, part, level + 1).start()
            else:
                write_out(group, part).start()

    def write_out(group, part):
        return pltpu.make_async_copy(
            slope.at[pl.ds(group * chunk_rows, chunk_rows), part_cols(part)],
            grad_sum.at[:, pl.ds(group * span + part * part_span, part_span)],
            osem.at[group, part],
        )

    def core_move(group, part):
        cols = part_cols(part)
        return remote(
            give.at[:, :, :, :, :, cols],
            from_core.at[group % 2, :, :, :, :, :, cols],
            gsend.at[group, part],
            grecv.at[group, part],
            partner,
        )

    chunk_rows = give.shape[4]
    m_rows = model // 2

    def group_products(group, columns, between=lambda: None):
        if group == 2:
            pl.semaphore_wait(credit, 1)
        for side in (0, 1):
            if side == 1:
                between()
            for part in range(PARTS):
                if side == 0 and group > 0:
                    core_move(group - 1, part).wait_send()
                if side == 1:
                    core_move(group, part).wait_recv()
                place = 0
                for left, right, start, size in columns(part, (1 - core, core)[side]):
                    cols = pl.ds(part * part_span + place, size)
                    place += size

                    @pl.loop(0, 2)
                    def _(m, left=left, right=right, start=start, size=size, cols=cols):
                        value = inner(left[at(m, m_rows), :], right[:, pl.ds(start, size)])
                        value = value.reshape(2, 2, 2, chunk_rows, size)
                        if side == 0:
                            give[m, :, :, :, :, cols] = value.astype(BF16)
                        else:
                            value = value + from_core[group % 2, m, :, :, :, :, cols].astype(F32)
                            mine_g[group, m, :, :, :, :, cols] = value.astype(BF16)

                if side == 0:
                    core_move(group, part).start()
                else:
                    halving(group, part, 0).start()
        if group == 0:
            pl.semaphore_signal(credit, inc=1, device_id=partner, device_id_type=MESH)

    part_out = 2 * model + hidden

    def sum_move(level):
        device = partner if level == 0 else across(level - 1)
        return remote(vsend.at[level], vrecv.at[level], vsem.at[0, level], vsem.at[1, level], device)

    def sum_next(level):
        sum_move(level).wait()
        value = vsend[level] + vrecv[level]
        if level == BITS:
            sums_sum[...] = value
        else:
            vsend[level + 1] = value
            sum_move(level + 1).start()

    wide, deep = wq.shape[1], wd_half.shape[0]
    pieces = []
    for i, array in enumerate((wq, wk, wv)):
        pieces.append((array, wqkv.at[:, pl.ds(pl.multiple_of(i * model + core * wide, wide), wide)]))
    pieces.append((wo_half, wo.at[at(core, wide), :]))
    pieces.append((wu_half, wu.at[:, at(core, deep)]))
    pieces.append((wd_half, wd.at[at(core, deep), :]))
    heres = [pltpu.make_async_copy(array, place, wlocal.at[i]) for i, (array, place) in enumerate(pieces)]
    for copy in heres:
        copy.start()

    shape = cluster_perm.shape
    positions = lax.broadcasted_iota(jnp.int32, shape, 0) * CLUSTER + lax.broadcasted_iota(jnp.int32, shape, 1)
    positions = positions + seq * rows
    doc_start = jnp.zeros(shape, jnp.int32)
    doc_length = jnp.zeros(shape, jnp.int32)
    start = 0
    for i in range(doc_lengths.shape[0]):
        length = doc_lengths[i]
        inside = positions >= start
        doc_start = jnp.where(inside, start, doc_start)
        doc_length = jnp.where(inside, length, doc_length)
        start = start + (length + CLUSTER - 1) // CLUSTER * CLUSTER
    valid[...] = jnp.where(cluster_perm[...] < doc_length, 1.0, 0.0)
    from_row = doc_start + cluster_perm[...]
    for i in range(shape[0]):
        line = from_row[i : i + 1, :]
        source[:, pl.ds(i * CLUSTER, CLUSTER)] = line
        rel[pl.ds(i * CLUSTER, CLUSTER), :] = jnp.broadcast_to(line - seq * rows, (CLUSTER, CLUSTER)).T
    sources[2] = source[...]
    for i, vector in enumerate((bo_in, g1_in, s1_in, bd_in, g2_in, s2_in)):
        vectors[i] = vector[...].reshape(1, model)
    bo, g1, s1, bd, g2, s2 = (vectors.at[i] for i in range(6))
    at_v = pl.ds(pl.multiple_of(2 * model + core * wide, wide), wide)
    bqkv[:, at(core, wide)] = bq[...].reshape(1, wide)
    bqkv[:, pl.ds(model, model)] = jnp.zeros((1, model), F32)
    bqkv[:, at_v] = bv[...].reshape(1, wide)
    bu[:, at(core, deep)] = bu_half[...].reshape(1, deep)
    pl.semaphore_wait(pltpu.get_barrier_semaphore(), arrivals)

    send_own(0)
    weights = []
    for place in (bqkv.at[:, at(core, wide)], bqkv.at[:, at_v], bu.at[:, at(core, deep)]):
        pieces.append((place, place))
    for i, (array, place) in enumerate(pieces):
        weights.append(remote(array, place, wsend.at[i], wrecv.at[i], partner))
        weights[i].start()
    tinies = []
    for offset in OFFSETS[1:]:
        device, there_ok = others[offset]
        out = remote(source, sources.at[2 - offset], ssend.at[2 - offset], srecv.at[2 - offset], device)
        back = remote(source, sources.at[2 + offset], ssend.at[2 + offset], srecv.at[2 + offset], device)
        pl.when(there_ok)(out.start)
        tinies.append((there_ok, out, back))

    pick(0, [(OWN, 0), (OWN, 1)], fresh=True)
    pick(1, [(OWN, 0), (OWN, 1)], fresh=True)
    first_hop(0, 0)
    first_hop(0, 1)
    second_hop(0, 0)
    pick(0, [(FROM_X, 0), (FROM_Y, 0)])
    first_hop(0, 2)
    second_hop(0, 1)
    first_hop(0, 3)
    second_hop(0, 2)
    pick(0, [(FROM_X, 1), (FROM_Y, 1), (FROM_Z, 0)])
    second_hop(0, 3)
    send_own(1)
    last_hop(0, 0)
    last_hop(0, 1)
    pick(0, [(FROM_Z, 1), (FROM_LAST, 0)])
    last_hop(0, 2)
    last_hop(0, 3)
    pick(0, [(FROM_LAST, 1)])
    begin(deliver(0))
    for copy in heres + weights:
        copy.wait()
    end(deliver(0))

    lanes = lax.broadcasted_iota(jnp.int32, (CLUSTER, 128), 1)
    first_f = jnp.where(lanes < HEAD_DIM, 1.0, 0.0)
    first = first_f.astype(BF16)
    second = (1.0 - first_f).astype(BF16)

    def stacked(pair):
        return jnp.concatenate([pair * first, pair * second], axis=0)

    def beside(tall):
        return jnp.concatenate([tall[:CLUSTER], tall[CLUSTER:]], axis=1)

    @pl.loop(0, 3 * model // tile)
    def _(step):
        cols = at(step, tile)
        qkv[:, cols] = (inner(x[...], wqkv[:, cols]) + bqkv[:, cols]).astype(BF16)

    first_hop(1, 0)

    @pl.loop(0, clusters)
    def _(cluster):
        r = at(cluster, CLUSTER)
        for pair in range(pairs):
            q = qkv[r, pl.ds(pair * 128, 128)]
            k = qkv[r, pl.ds(model + pair * 128, 128)]
            v = qkv[r, pl.ds(2 * model + pair * 128, 128)]
            scores = outer(stacked(q), k) * score_scale
            scores = jnp.where(valid[pl.ds(core * clusters + cluster, 1), :] > 0.5, scores, masked_score)
            top = jnp.max(scores, axis=-1, keepdims=True)
            weight = jnp.exp(scores - top)
            p = weight * (1.0 / jnp.sum(weight, axis=-1, keepdims=True))
            prob[cluster * pairs + pair] = p
            ctx[r, pl.ds(pair * 128, 128)] = inner(beside(p.astype(BF16)), stacked(v)).astype(BF16)

    first_hop(1, 1)

    @pl.loop(0, model // tile)
    def _(step):
        cols = at(step, tile)
        hat1[:, cols] = inner(ctx[...], wo[:, cols]) + x[:, cols].astype(F32) + bo[:, cols]

    @pl.loop(0, half // band)
    def _(step):
        r = at(step, band)
        h = hat1[r, :]
        centered = h - jnp.mean(h, axis=-1, keepdims=True)
        inv = lax.rsqrt(jnp.mean(centered * centered, axis=-1, keepdims=True) + norm_eps)
        hat = centered * inv
        hat1[r, :] = hat
        inv12[r, pl.ds(0, 1)] = inv
        low1[r, :] = (hat * g1[...] + s1[...]).astype(BF16)

    first_hop(1, 2)
    second_hop(1, 0)

    @pl.loop(0, hidden // tile)
    def _(step):
        cols = at(step, tile)
        pre = inner(low1[...], wu[:, cols]) + bu[:, cols]
        cdf = 0.5 * (1.0 + lax.erf(pre * root_half))
        act[:, cols] = (pre * cdf).astype(BF16)
        slope[:, cols] = cdf + pre * jnp.exp(-0.5 * pre * pre) * inv_root_tau

    first_hop(1, 3)
    second_hop(1, 1)

    @pl.loop(0, model // tile)
    def _(step):
        cols = at(step, tile)
        norm = hat1[:, cols] * g1[:, cols] + s1[:, cols]
        work[:, cols] = inner(act[...], wd[:, cols]) + norm + bd[:, cols]

    second_hop(1, 2)

    @pl.loop(0, half // band)
    def _(step):
        r = at(step, band)
        h = work[r, :]
        centered = h - jnp.mean(h, axis=-1, keepdims=True)
        inv = lax.rsqrt(jnp.mean(centered * centered, axis=-1, keepdims=True) + norm_eps)
        hat = centered * inv
        work[r, :] = hat
        inv12[r, pl.ds(1, 1)] = inv
        in_low[r, :] = (hat * g2[...] + s2[...]).astype(BF16)

    begin(collect(2))
    second_hop(1, 3)
    pick(1, [(FROM_X, 0), (FROM_Y, 0), (FROM_X, 1), (FROM_Y, 1)])
    end(collect(2))
    for chunk in range(CHUNKS):
        last_hop(1, chunk)
    send_own(2)
    pick(1, [(FROM_Z, 0), (FROM_Z, 1), (FROM_LAST, 0), (FROM_LAST, 1)])
    begin(deliver(1))
    accs[...] = jnp.zeros_like(accs)
    end(deliver(1))

    @pl.loop(0, half // band)
    def _(step):
        r = at(step, band)
        hat = work[r, :]
        grad = og[r, :].astype(F32)
        accs[4] += fold_rows(grad * hat)
        accs[5] += fold_rows(grad)
        scaled = grad * g2[...]
        back = inv12[r, pl.ds(1, 1)] * (
            scaled
            - jnp.mean(scaled, axis=-1, keepdims=True)
            - hat * jnp.mean(scaled * hat, axis=-1, keepdims=True)
        )
        accs[3] += fold_rows(back)
        work[r, :] = back
        low2[r, :] = back.astype(BF16)

    def flip(source_rows, target=flipped):
        @pl.loop(0, model // 128)
        def _(step):
            target[at(step, 128), :] = source_rows[:, at(step, 128)].T

    def long_columns(part, side):
        start = pl.multiple_of(side * span + part * part_span, part_span)
        return [(flipped, act, start, part_span)]

    first_hop(2, 0)
    flip(low2)
    group_products(0, long_columns, lambda: first_hop(2, 1))
    first_hop(2, 2)
    second_hop(2, 0)

    @pl.loop(0, hidden // tile)
    def _(step):
        cols = at(step, tile)
        back = outer(low2[...], wd[cols, :]) * slope[:, cols]
        back = back.astype(BF16)
        act[:, cols] = back
        vsend[0, :, pl.ds(pl.multiple_of(2 * model + step * tile, tile), tile)] = jnp.sum(
            back.astype(F32), axis=0, keepdims=True
        )

    first_hop(2, 3)
    second_hop(2, 1)
    flip(low1)
    group_products(1, long_columns, lambda: second_hop(2, 2))

    @pl.loop(0, model // tile)
    def _(step):
        cols = at(step, tile)
        work[:, cols] += outer(act[...], wu[cols, :])

    @pl.loop(0, half // band)
    def _(step):
        r = at(step, band)
        grad = work[r, :]
        hat = hat1[r, :]
        accs[1] += fold_rows(grad * hat)
        accs[2] += fold_rows(grad)
        scaled = grad * g1[...]
        back = inv12[r, pl.ds(0, 1)] * (
            scaled
            - jnp.mean(scaled, axis=-1, keepdims=True)
            - hat * jnp.mean(scaled * hat, axis=-1, keepdims=True)
        )
        accs[0] += fold_rows(back)
        work[r, :] = back
        low2[r, :] = back.astype(BF16)

    @pl.loop(0, model // tile)
    def _(step):
        cols = at(step, tile)
        low1[:, cols] = outer(low2[...], wo[cols, :]).astype(BF16)

    def attention_backward(cluster):
        r = at(cluster, CLUSTER)
        for pair in range(pairs):
            at_q = pl.ds(pair * 128, 128)
            at_k = pl.ds(model + pair * 128, 128)
            at_v = pl.ds(2 * model + pair * 128, 128)
            q, k, v = qkv[r, at_q], qkv[r, at_k], qkv[r, at_v]
            p = prob[cluster * pairs + pair]
            dctx = stacked(low1[r, at_q])
            dprob = outer(dctx, v)
            dscore = (p * (dprob - jnp.sum(p * dprob, axis=-1, keepdims=True))).astype(BF16)
            qkv[r, at_q] = (inner(beside(dscore), stacked(k)) * score_scale).astype(BF16)
            qkv[r, at_k] = (under(dscore, stacked(q)) * score_scale).astype(BF16)
            qkv[r, at_v] = under(p.astype(BF16), dctx).astype(BF16)

    second_hop(2, 3)
    advance(0, 0)
    pl.loop(0, clusters // 2)(attention_backward)
    pl.loop(clusters // 2, clusters)(attention_backward)
    advance(0, 1)

    @pl.loop(0, model // tile)
    def _(step):
        cols = at(step, tile)
        in_low[:, cols] = (work[:, cols] + outer(qkv[...], wqkv[cols, :])).astype(BF16)

    begin(collect(3))
    end(collect(3))
    send_own(3)
    advance(1, 0)
    advance(0, 2)

    for which in range(2):
        @pl.loop(0, model // tile)
        def _(step, which=which):
            value = qkv[:, pl.ds(pl.multiple_of(2 * which * model + step * tile, tile), tile)]
            vsend[0, :, pl.ds(pl.multiple_of(which * model + step * tile, tile), tile)] = jnp.sum(
                value.astype(F32), axis=0, keepdims=True
            )

    for i in range(6):
        vsend[0, :, pl.ds(part_out + i * model, model)] = jnp.sum(accs[i], axis=0, keepdims=True)
    sum_move(0).start()

    flip(low2)
    flip(x, flipped_x)

    def square_columns(part, side):
        def cut(left, right, base, start, size):
            return (left, right, pl.multiple_of(base + side * width + start, 128), size)

        third = width // 3
        if part == 0:
            return [cut(flipped, ctx, 0, 0, 3 * third), cut(flipped_x, qkv, 0, 0, third)]
        if part == 1:
            return [
                cut(flipped_x, qkv, 0, third, 2 * third),
                cut(flipped_x, qkv, model, 0, 2 * third),
            ]
        return [
            cut(flipped_x, qkv, model, 2 * third, third),
            cut(flipped_x, qkv, 2 * model, 0, 3 * third),
        ]

    def hops():
        first_hop(3, 0)

    group_products(2, square_columns, hops)
    first_hop(3, 1)
    second_hop(3, 0)
    advance(1, 1)
    first_hop(3, 2)
    second_hop(3, 1)
    advance(0, 3)
    sum_next(0)
    for there_ok, out, back in tinies:

        def finish(out=out, back=back):
            out.wait_send()
            back.wait_recv()

        pl.when(there_ok)(finish)
    for chunk in range(CHUNKS):
        last_hop(2, chunk)
    first_hop(3, 3)
    second_hop(3, 2)
    pick(2, [(OWN, 0), (OWN, 1)], fresh=True)
    sum_next(1)
    second_hop(3, 3)
    advance(2, 0)
    pick(2, [(FROM_X, 0), (FROM_Y, 0), (FROM_X, 1), (FROM_Y, 1)])
    sum_next(2)
    advance(2, 1)
    advance(1, 2)
    pick(2, [(FROM_Z, 0), (FROM_Z, 1), (FROM_LAST, 0), (FROM_LAST, 1)])
    begin(bring_home(2))
    pick(3, [(OWN, 0), (OWN, 1)], fresh=True)
    sum_next(3)
    pick(3, [(FROM_X, 0), (FROM_Y, 0), (FROM_X, 1), (FROM_Y, 1)])
    advance(2, 2)
    advance(1, 3)
    last_hop(3, 0)
    last_hop(3, 1)
    pick(3, [(FROM_Z, 0), (FROM_Z, 1), (FROM_LAST, 0)])
    sum_next(4)
    last_hop(3, 2)
    last_hop(3, 3)
    pick(3, [(FROM_LAST, 1)])
    begin(bring_home(3))
    advance(2, 3)
    for part in range(PARTS):
        core_move(2, part).wait_send()
    for e in range(EXCHANGES):
        all_sent(e)
    end(bring_home(2))
    end(bring_home(3))
    for group in range(GROUPS):
        for part in range(PARTS):
            write_out(group, part).wait()


def whole(mesh, *args):
    tokens, wu_half = args[0], args[8]
    rows, model = tokens.shape
    half, width = rows // 2, model // 2
    hidden = 2 * wu_half.shape[1]
    blocks = mesh.shape["seq"]
    hbm = pl.BlockSpec(memory_space=pl.ANY)
    vmem = pl.BlockSpec(memory_space=pltpu.VMEM)
    smem = pl.BlockSpec(memory_space=pltpu.SMEM)
    dma = pltpu.SemaphoreType.DMA
    chunk = model // blocks
    span = 4 * width
    part_span = span // PARTS
    steps = half // CLUSTER * (model // 128)
    total = 8 * model + hidden
    cube = (2, 2, 2, 2)
    return pl.pallas_call(
        functools.partial(whole_kernel, blocks),
        out_shape=(
            jax.ShapeDtypeStruct((rows, model), BF16),
            jax.ShapeDtypeStruct((rows, model), BF16),
            jax.ShapeDtypeStruct((chunk, GROUPS * span), F32),
            jax.ShapeDtypeStruct((1, total), F32),
            jax.ShapeDtypeStruct((EXCHANGES, 5, rows, width), BF16),
        ),
        in_specs=[hbm, hbm, smem, vmem] + [hbm] * 6 + [vmem] * 9,
        out_specs=(hbm, hbm, hbm, vmem, hbm),
        scratch_shapes=[
            pltpu.VMEM((model, 3 * model), BF16),
            pltpu.VMEM((model, model), BF16),
            pltpu.VMEM((model, hidden), BF16),
            pltpu.VMEM((hidden, model), BF16),
            pltpu.VMEM((1, 3 * model), F32),
            pltpu.VMEM((1, hidden), F32),
            pltpu.VMEM((4, half, width), BF16),
            pltpu.VMEM((2, rows, width), BF16),
            pltpu.VMEM((2, rows, width), BF16),
            pltpu.VMEM((1, rows), jnp.int32),
            pltpu.VMEM((5, 1, rows), jnp.int32),
            pltpu.VMEM((rows, CLUSTER), jnp.int32),
            pltpu.VMEM((rows // CLUSTER, CLUSTER), F32),
            pltpu.VMEM((6, 1, model), F32),
            pltpu.VMEM((half, model), BF16),
            pltpu.VMEM((half, model), BF16),
            pltpu.VMEM((half, 3 * model), BF16),
            pltpu.VMEM((half, model), BF16),
            pltpu.VMEM((steps, 2 * CLUSTER, CLUSTER), F32),
            pltpu.VMEM((half, model), F32),
            pltpu.VMEM((half, 2), F32),
            pltpu.VMEM((half, model), BF16),
            pltpu.VMEM((half, hidden), BF16),
            pltpu.VMEM((half, hidden), F32),
            pltpu.VMEM((half, model), F32),
            pltpu.VMEM((model, half), BF16),
            pltpu.VMEM((model, half), BF16),
            pltpu.VMEM((half, model), BF16),
            pltpu.VMEM((6, 8, model), F32),
            pltpu.VMEM((GROUPS,) + cube + (chunk, span), BF16),
            pltpu.VMEM((2,) + cube + (chunk, span), BF16),
            pltpu.VMEM(cube + (chunk, span), BF16),
            pltpu.VMEM((GROUPS, PARTS, 2, 2, 2, chunk, part_span), BF16),
            pltpu.VMEM((GROUPS, PARTS, 2, 2, chunk, part_span), BF16),
            pltpu.VMEM((GROUPS, PARTS, 2, chunk, part_span), BF16),
            pltpu.VMEM((GROUPS, PARTS, chunk, part_span), BF16),
            pltpu.VMEM((BITS + 1, 1, total), F32),
            pltpu.VMEM((BITS + 1, 1, total), F32),
            dma((9,)),
            dma((9,)),
            dma((9,)),
            dma((EXCHANGES, 5, CHUNKS)),
            dma((EXCHANGES, 5, CHUNKS)),
            dma((5,)),
            dma((5,)),
            dma((4,)),
            dma((EXCHANGES,)),
            dma((EXCHANGES,)),
            dma((EXCHANGES,)),
            dma((2,)),
            dma((2,)),
            dma((2,)),
            dma((GROUPS, PARTS)),
            dma((GROUPS, PARTS)),
            dma((GROUPS, PARTS, BITS)),
            dma((GROUPS, PARTS, BITS)),
            dma((2, BITS + 1)),
            dma((GROUPS, PARTS)),
            pltpu.SemaphoreType.REGULAR,
        ],
        compiler_params=pltpu.CompilerParams(
            collective_id=2, has_side_effects=True, vmem_limit_bytes=64 * MEBI
        ),
    )(*args)[:4]


def body(
    mesh,
    tokens,
    out_grad,
    doc_lengths,
    cluster_perm,
    query_weight,
    query_bias,
    key_weight,
    value_weight,
    value_bias,
    output_weight,
    output_bias,
    first_gain,
    first_shift,
    up_weight,
    up_bias,
    down_weight,
    down_bias,
    second_gain,
    second_shift,
):
    rows, model = tokens.shape
    half = rows // 2
    hidden = 2 * up_weight.shape[1]
    blocks = mesh.shape["seq"]
    seq, core = lax.axis_index("seq"), lax.axis_index("head")
    positions = seq * rows + jnp.arange(rows, dtype=jnp.int32)
    slot_start, slot_length = doc_lookup(doc_lengths, positions)
    source = slot_start + cluster_perm
    valid = (cluster_perm < slot_length).astype(F32).reshape(2, half // CLUSTER, 1, CLUSTER)
    valid = lax.dynamic_index_in_dim(valid, core, 0, keepdims=False)

    def row(v):
        return v.reshape(1, -1)

    rel = (source - seq * rows).reshape(rows, 1)
    chunk = model // blocks
    part_q, part_h = model // 2, hidden // 2
    order = ("q", "k", "v", "o", "up", "down")
    if blocks == 1 << BITS and chunk % 16 == 0 and hidden == 4 * model:
        order = ("down", "up", "o", "q", "k", "v")
        out_home, in_home, grad_sum, sums = whole(
            mesh,
            tokens,
            out_grad,
            doc_lengths,
            cluster_perm.reshape(rows // CLUSTER, CLUSTER),
            query_weight,
            key_weight,
            value_weight,
            output_weight,
            up_weight,
            down_weight,
            query_bias,
            value_bias,
            up_bias,
            output_bias,
            first_gain,
            first_shift,
            down_bias,
            second_gain,
            second_shift,
        )
    else:
        x, og, sources, wqkv, wo, wu, wd, bqkv, bu = entry(
            mesh,
            tokens,
            out_grad,
            rel,
            row(source),
            query_weight,
            key_weight,
            value_weight,
            output_weight,
            up_weight,
            down_weight,
            row(query_bias),
            row(value_bias),
            row(up_bias),
        )
        no_key = (jnp.arange(3 * model) // model != 1)[None, :]
        bqkv = jnp.where(no_key, bqkv, 0.0)
        reduce = chunk % 16 == 0 and blocks >= 4 and blocks & (blocks - 1) == 0
        out_low, in_low, grads, sums = layer(
            chunk if reduce else 48,
            x,
            og,
            valid,
            wqkv,
            wo,
            wu,
            wd,
            bqkv,
            row(output_bias),
            row(first_gain),
            row(first_shift),
            bu,
            row(down_bias),
            row(second_gain),
            row(second_shift),
        )
        if reduce:
            out_home, in_home, grad_sum, sums = leave(mesh, True, out_low, in_low, sources, grads, sums)
        else:
            out_home, in_home = leave(mesh, False, out_low, in_low, sources, None, None)
            sums = lax.psum(sums, ("seq", "head"))
            grads = grads.reshape(2, model, -1)
            grads = lax.psum_scatter(grads.astype(F32), "head", scatter_dimension=0, tiled=True)[0]
            grad_sum = lax.psum_scatter(grads, "seq", scatter_dimension=0, tiled=True)
    grad_of, place = {}, 0
    for name in order:
        size = part_h if name in ("up", "down") else part_q
        grad_of[name] = grad_sum[:, place : place + size]
        place += size
    sums = sums[0]

    def mine(start, size):
        return lax.dynamic_slice(sums, (start + core * size,), (size,))

    def block(index):
        return lax.dynamic_slice(sums, (2 * model + hidden + index * model + seq * chunk,), (chunk,))

    return (
        out_home.astype(F32),
        in_home.astype(F32),
        grad_of["q"],
        mine(0, part_q),
        grad_of["k"],
        grad_of["v"],
        mine(model, part_q),
        grad_of["o"].T,
        block(0),
        block(1),
        block(2),
        grad_of["up"],
        mine(2 * model, part_h),
        grad_of["down"].T,
        block(3),
        block(4),
        block(5),
    )


def solution(mesh):
    placed = (
        P("seq", None),
        P("seq", None),
        P(),
        P("seq"),
        P(None, "head"),
        P("head"),
        P(None, "head"),
        P(None, "head"),
        P("head"),
        P("head", None),
        P(),
        P(),
        P(),
        P(None, "head"),
        P("head"),
        P("head", None),
        P(),
        P(),
        P(),
    )
    return jax.shard_map(
        functools.partial(body, mesh),
        mesh=mesh,
        in_specs=placed,
        out_specs=(
            P("seq", None),
            P("seq", None),
            P("seq", "head"),
            P("head"),
            P("seq", "head"),
            P("seq", "head"),
            P("head"),
            P("head", "seq"),
            P("seq"),
            P("seq"),
            P("seq"),
            P("seq", "head"),
            P("head"),
            P("head", "seq"),
            P("seq"),
            P("seq"),
            P("seq"),
        ),
        check_vma=False,
    )
```

```python
import functools

import jax
import jax.numpy as jnp
from jax import lax
from jax.experimental import pallas as pl
from jax.experimental.pallas import tpu as pltpu
from jax.sharding import PartitionSpec as P

MESH = pl.DeviceIdType.MESH
HEAD_DIM = 64
CLUSTER = 128
OFFSETS = (0, 1, -1, 2, -2)
SLOT = {offset: slot for slot, offset in enumerate(OFFSETS)}
MEBI = 1 << 20

norm_eps = 1e-12
masked_score = -1e30
root_half = 0.7071067811865476
inv_root_tau = 0.3989422804014327
score_scale = HEAD_DIM ** (-0.5)

F32 = jnp.float32
BF16 = jnp.bfloat16


def doc_lookup(doc_lengths, positions):
    padded = (doc_lengths + CLUSTER - 1) // CLUSTER * CLUSTER
    starts = jnp.cumsum(padded) - padded
    doc_of = jnp.sum((starts[None, :] <= positions[:, None]).astype(jnp.int32), axis=1) - 1
    picked = jnp.arange(starts.shape[0], dtype=jnp.int32)[None, :] == doc_of[:, None]
    slot_start = jnp.sum(jnp.where(picked, starts[None, :], 0), axis=1)
    slot_length = jnp.sum(jnp.where(picked, doc_lengths[None, :], 0), axis=1)
    return (slot_start, slot_length)


def remote(src, dst, send, recv, device):
    return pltpu.make_async_remote_copy(
        src_ref=src, dst_ref=dst, send_sem=send, recv_sem=recv, device_id=device, device_id_type=MESH
    )


def greet(devices):
    pl.semaphore_wait(pltpu.get_barrier_semaphore(), greet_start(devices))


def greet_start(devices):
    barrier = pltpu.get_barrier_semaphore()
    count = 0
    for device, valid in devices:
        def hello(device=device):
            pl.semaphore_signal(barrier, inc=1, device_id=device, device_id_type=MESH)

        if valid is None:
            hello()
            count = count + 1
        else:
            pl.when(valid)(hello)
            count = count + valid.astype(jnp.int32)
    return count


def near(seq, core, blocks):
    out = {}
    for offset in OFFSETS[1:]:
        there = seq + offset
        out[offset] = ((there, core), (there >= 0) & (there < blocks))
    return out


def inner(left, right):
    return lax.dot_general(left, right, (((1,), (0,)), ((), ())), preferred_element_type=F32)


def outer(left, right):
    return lax.dot_general(left, right, (((1,), (1,)), ((), ())), preferred_element_type=F32)


def under(left, right):
    return lax.dot_general(left, right, (((0,), (0,)), ((), ())), preferred_element_type=F32)


def entry_kernel(
    blocks,
    tokens,
    out_grad,
    rel,
    source,
    wq,
    wk,
    wv,
    wo,
    wu,
    wd,
    bq,
    bv,
    bu,
    slot_tokens,
    slot_grad,
    sources,
    wqkv_full,
    wo_full,
    wu_full,
    wd_full,
    bqkv_full,
    bu_full,
    window,
    total,
    picked,
    source_win,
    wsend,
    wrecv,
    wlocal,
    send,
    recv,
    local,
    ssend,
    srecv,
    psend,
    precv,
    plocal,
):
    seq, core = lax.axis_index("seq"), lax.axis_index("head")
    rows, width = window.shape[2], window.shape[3]
    half = rows // 2
    partner = (seq, 1 - core)
    others = near(seq, core, blocks)
    greet([(partner, None)] + [others[offset] for offset in OFFSETS[1:]])

    mine = pl.ds(pl.multiple_of(core * width, width), width)
    arrays = (tokens, out_grad)
    locals_ = []
    for which, array in enumerate(arrays):
        for offset in OFFSETS[1:]:
            device, valid = others[offset]
            slot = SLOT[-offset]
            copy = remote(
                array.at[:, mine], window.at[which, slot], send.at[which, slot], recv.at[which, slot], device
            )
            pl.when(valid)(copy.start)
            if which == 0:
                tiny = remote(source, source_win.at[slot], ssend.at[slot], srecv.at[slot], device)
                pl.when(valid)(tiny.start)
        own = pltpu.make_async_copy(array.at[:, mine], window.at[which, 0], local.at[which])
        own.start()
        locals_.append(own)

    wide, deep = wq.shape[1], wd.shape[0]
    model = wq.shape[0]
    at_core = pl.multiple_of(core * wide, wide)
    at_deep = pl.multiple_of(core * deep, deep)
    pieces = []
    for i, array in enumerate((wq, wk, wv)):
        at = pl.multiple_of(i * model + core * wide, wide)
        pieces.append((array, wqkv_full.at[:, pl.ds(at, wide)]))
    pieces.append((wo, wo_full.at[pl.ds(at_core, wide), :]))
    pieces.append((wu, wu_full.at[:, pl.ds(at_deep, deep)]))
    pieces.append((wd, wd_full.at[pl.ds(at_deep, deep), :]))
    pieces.append((bq, bqkv_full.at[:, pl.ds(at_core, wide)]))
    pieces.append((bv, bqkv_full.at[:, pl.ds(pl.multiple_of(2 * model + core * wide, wide), wide)]))
    pieces.append((bu, bu_full.at[:, pl.ds(at_deep, deep)]))
    moves = []
    for i, (array, place) in enumerate(pieces):
        there = remote(array, place, wsend.at[i], wrecv.at[i], partner)
        here = pltpu.make_async_copy(array, place, wlocal.at[i])
        there.start()
        here.start()
        moves.append((there, here))

    source_win[0] = source[...]
    for offset in OFFSETS[1:]:

        def blank(slot=SLOT[offset]):
            source_win[slot] = jnp.full(source.shape, -1, jnp.int32)

        pl.when(jnp.logical_not(others[offset][1]))(blank)
    tile = 256
    outs = (slot_tokens, slot_grad)
    finals = []
    for which in range(2):
        locals_[which].wait()
        for offset in OFFSETS:
            slot = SLOT[offset]

            def add(which=which, offset=offset, slot=slot):
                if offset != 0:
                    device, _ = others[offset]
                    remote(
                        arrays[which].at[:, mine],
                        window.at[which, slot],
                        send.at[which, slot],
                        recv.at[which, slot],
                        device,
                    ).wait_recv()

                @pl.loop(0, rows // tile)
                def _(step):
                    at = pl.ds(pl.multiple_of(step * tile, tile), tile)
                    wanted = rel[at, :] - offset * rows
                    lanes = lax.broadcasted_iota(jnp.int32, (tile, rows), 1)
                    chosen = jnp.where(lanes == wanted, 1.0, 0.0).astype(BF16)
                    part = inner(chosen, window[which, slot])
                    if offset == 0:
                        total[at, :] = part
                    else:
                        total[at, :] += part

            if offset == 0:
                add()
            else:
                pl.when(others[offset][1])(add)
        picked[which] = total[...].astype(BF16)
        keep = pl.ds(pl.multiple_of(core * half, half), half)
        give = pl.ds(pl.multiple_of((1 - core) * half, half), half)
        there = remote(
            picked.at[which, give], outs[which].at[:, mine], psend.at[which], precv.at[which], partner
        )
        here = pltpu.make_async_copy(picked.at[which, keep], outs[which].at[:, mine], plocal.at[which])
        there.start()
        here.start()
        finals.append((there, here))

    for offset in OFFSETS[1:]:
        device, valid = others[offset]

        def finish(offset=offset, device=device):
            for which in range(2):
                slot = SLOT[-offset]
                remote(
                    arrays[which].at[:, mine],
                    window.at[which, slot],
                    send.at[which, slot],
                    recv.at[which, slot],
                    device,
                ).wait_send()
            slot = SLOT[-offset]
            remote(source, source_win.at[slot], ssend.at[slot], srecv.at[slot], device).wait_send()
            slot = SLOT[offset]
            remote(source, source_win.at[slot], ssend.at[slot], srecv.at[slot], device).wait_recv()

        pl.when(valid)(finish)
    sources[...] = source_win[...]
    for there, here in moves + finals:
        there.wait()
        here.wait()


def entry(mesh, tokens, out_grad, rel, source, wq, wk, wv, wo, wu, wd, bq, bv, bu):
    rows, model = tokens.shape
    width = model // 2
    hidden = 2 * wu.shape[1]
    hbm = pl.BlockSpec(memory_space=pl.ANY)
    vmem = pl.BlockSpec(memory_space=pltpu.VMEM)
    slots = len(OFFSETS)
    dma = pltpu.SemaphoreType.DMA
    return pl.pallas_call(
        functools.partial(entry_kernel, mesh.shape["seq"]),
        out_shape=(
            jax.ShapeDtypeStruct((rows // 2, model), BF16),
            jax.ShapeDtypeStruct((rows // 2, model), BF16),
            jax.ShapeDtypeStruct((slots, 1, rows), jnp.int32),
            jax.ShapeDtypeStruct((model, 3 * model), BF16),
            jax.ShapeDtypeStruct((model, model), BF16),
            jax.ShapeDtypeStruct((model, hidden), BF16),
            jax.ShapeDtypeStruct((hidden, model), BF16),
            jax.ShapeDtypeStruct((1, 3 * model), F32),
            jax.ShapeDtypeStruct((1, hidden), F32),
        ),
        in_specs=[hbm, hbm, vmem, vmem] + [hbm] * 9,
        out_specs=(hbm, hbm, vmem) + (hbm,) * 6,
        scratch_shapes=[
            pltpu.VMEM((2, slots, rows, width), BF16),
            pltpu.VMEM((rows, width), F32),
            pltpu.VMEM((2, rows, width), BF16),
            pltpu.VMEM((slots, 1, rows), jnp.int32),
            dma((9,)),
            dma((9,)),
            dma((9,)),
            dma((2, slots)),
            dma((2, slots)),
            dma((2,)),
            dma((slots,)),
            dma((slots,)),
            dma((2,)),
            dma((2,)),
            dma((2,)),
        ],
        compiler_params=pltpu.CompilerParams(
            collective_id=0, has_side_effects=True, vmem_limit_bytes=40 * MEBI
        ),
    )(tokens, out_grad, rel, source, wq, wk, wv, wo, wu, wd, bq, bv, bu)


def fold_rows(values):
    return jnp.sum(values.reshape(values.shape[0] // 8, 8, values.shape[1]), axis=0)


def layer_kernel(
    chunk,
    x,
    og,
    valid,
    wqkv,
    wo,
    wu,
    wd,
    bqkv,
    bo,
    g1,
    s1,
    bu,
    bd,
    g2,
    s2,
    out_low,
    in_low,
    grads,
    sums,
    qkv,
    ctx,
    prob,
    hat1,
    inv1,
    low1,
    act,
    slope,
    pre_low,
    work,
    flipped,
    dqkv,
    cgrad,
    low2,
    gtile,
    accs,
    gsem,
):
    rows, model = x.shape
    hidden = wu.shape[1]
    clusters = rows // CLUSTER
    pairs = model // 128
    tile = 256
    band = 64

    def at(step, size):
        return pl.ds(pl.multiple_of(step * size, size), size)

    lanes = lax.broadcasted_iota(jnp.int32, (CLUSTER, 128), 1)
    first_f = jnp.where(lanes < HEAD_DIM, 1.0, 0.0)
    first = first_f.astype(BF16)
    second = (1.0 - first_f).astype(BF16)

    def stacked(pair):
        return jnp.concatenate([pair * first, pair * second], axis=0)

    def beside(tall):
        return jnp.concatenate([tall[:CLUSTER], tall[CLUSTER:]], axis=1)

    @pl.loop(0, 3 * model // tile)
    def _(step):
        cols = at(step, tile)
        qkv[:, cols] = (inner(x[...], wqkv[:, cols]) + bqkv[:, cols]).astype(BF16)

    @pl.loop(0, clusters * pairs)
    def _(step):
        cluster, pair = step // pairs, step % pairs
        r = at(cluster, CLUSTER)
        q = qkv[r, at(pair, 128)]
        k = qkv[r, pl.ds(pl.multiple_of(model + pair * 128, 128), 128)]
        v = qkv[r, pl.ds(pl.multiple_of(2 * model + pair * 128, 128), 128)]
        scores = outer(stacked(q), k) * score_scale
        scores = jnp.where(valid[cluster] > 0.5, scores, masked_score)
        top = jnp.max(scores, axis=-1, keepdims=True)
        weight = jnp.exp(scores - top)
        p = weight / jnp.sum(weight, axis=-1, keepdims=True)
        prob[step] = p
        ctx[r, at(pair, 128)] = inner(beside(p.astype(BF16)), stacked(v)).astype(BF16)

    @pl.loop(0, model // tile)
    def _(step):
        cols = at(step, tile)
        hat1[:, cols] = inner(ctx[...], wo[:, cols]) + x[:, cols].astype(F32) + bo[:, cols]

    @pl.loop(0, rows // band)
    def _(step):
        r = at(step, band)
        h = hat1[r, :]
        centered = h - jnp.mean(h, axis=-1, keepdims=True)
        inv = lax.rsqrt(jnp.mean(centered * centered, axis=-1, keepdims=True) + norm_eps)
        hat = centered * inv
        hat1[r, :] = hat
        inv1[r, :] = inv
        low1[r, :] = (hat * g1[...] + s1[...]).astype(BF16)

    @pl.loop(0, hidden // tile)
    def _(step):
        cols = at(step, tile)
        pre = inner(low1[...], wu[:, cols]) + bu[:, cols]
        cdf = 0.5 * (1.0 + lax.erf(pre * root_half))
        act[:, cols] = (pre * cdf).astype(BF16)
        slope[:, cols] = cdf + pre * jnp.exp(-0.5 * pre * pre) * inv_root_tau

    @pl.loop(0, model // tile)
    def _(step):
        cols = at(step, tile)
        norm = hat1[:, cols] * g1[:, cols] + s1[:, cols]
        work[:, cols] = inner(act[...], wd[:, cols]) + norm + bd[:, cols]

    accs[...] = jnp.zeros_like(accs)

    @pl.loop(0, rows // band)
    def _(step):
        r = at(step, band)
        h = work[r, :]
        centered = h - jnp.mean(h, axis=-1, keepdims=True)
        inv = lax.rsqrt(jnp.mean(centered * centered, axis=-1, keepdims=True) + norm_eps)
        hat = centered * inv
        out_low[r, :] = (hat * g2[...] + s2[...]).astype(BF16)
        grad = og[r, :].astype(F32)
        accs[4] += fold_rows(grad * hat)
        accs[5] += fold_rows(grad)
        scaled = grad * g2[...]
        back = inv * (
            scaled
            - jnp.mean(scaled, axis=-1, keepdims=True)
            - hat * jnp.mean(scaled * hat, axis=-1, keepdims=True)
        )
        accs[3] += fold_rows(back)
        work[r, :] = back
        low2[r, :] = back.astype(BF16)

    def flip(source):
        @pl.loop(0, model // 128)
        def _(step):
            flipped[at(step, 128), :] = source[:, at(step, 128)].T

    half_rows = model // 2
    chunks = half_rows // chunk

    def product_tiles(right, width, places, count):
        def moves(index, slot):
            m, n = index // count, index % count
            for piece, (part, start, size) in enumerate(places(n)):
                yield pltpu.make_async_copy(
                    gtile.at[slot, :, :, pl.ds(piece * size, size)] if size != width
                    else gtile.at[slot, :, :, pl.ds(0, width)],
                    grads.at[part, pl.ds(m * chunks, chunks), :, pl.ds(start, size)],
                    gsem.at[slot, piece],
                )

        total = 2 * count

        @pl.loop(0, total)
        def _(index):
            slot = index % 2
            m, n = index // count, index % count

            @pl.when(index >= 2)
            def _():
                for move in moves(index - 2, slot):
                    move.wait()

            value = inner(flipped[at(m, half_rows), :], right[:, at(n, width)])
            gtile[slot, :, :, pl.ds(0, width)] = value.reshape(chunks, chunk, width).astype(BF16)
            for move in moves(index, slot):
                move.start()

        for index in range(max(total - 2, 0), total):
            for move in moves(index, index % 2):
                move.wait()

    part_q = model // 2
    part_h = hidden // 2
    wide = 512

    def square(which):
        def places(n):
            return [(0, which * part_q, part_q), (1, which * part_q, part_q)]

        return places

    def long(base):
        per_part = part_h // wide

        def places(n):
            part, inside = n // per_part, n % per_part
            return [(part, pl.multiple_of(base + inside * wide, 128), wide)]

        return places

    flip(low2)
    product_tiles(act, wide, long(4 * part_q + part_h), hidden // wide)

    @pl.loop(0, hidden // tile)
    def _(step):
        cols = at(step, tile)
        back = outer(low2[...], wd[cols, :]) * slope[:, cols]
        back = back.astype(BF16)
        pre_low[:, cols] = back
        sums[:, pl.ds(pl.multiple_of(2 * model + step * tile, tile), tile)] = jnp.sum(
            back.astype(F32), axis=0, keepdims=True
        )

    flip(low1)
    product_tiles(pre_low, wide, long(4 * part_q), hidden // wide)

    @pl.loop(0, model // tile)
    def _(step):
        cols = at(step, tile)
        work[:, cols] += outer(pre_low[...], wu[cols, :])

    @pl.loop(0, rows // band)
    def _(step):
        r = at(step, band)
        grad = work[r, :]
        hat = hat1[r, :]
        accs[1] += fold_rows(grad * hat)
        accs[2] += fold_rows(grad)
        scaled = grad * g1[...]
        back = inv1[r, :] * (
            scaled
            - jnp.mean(scaled, axis=-1, keepdims=True)
            - hat * jnp.mean(scaled * hat, axis=-1, keepdims=True)
        )
        accs[0] += fold_rows(back)
        work[r, :] = back
        low2[r, :] = back.astype(BF16)

    flip(low2)
    product_tiles(ctx, model, square(3), 1)

    @pl.loop(0, model // tile)
    def _(step):
        cols = at(step, tile)
        cgrad[:, cols] = outer(low2[...], wo[cols, :]).astype(BF16)

    @pl.loop(0, clusters * pairs)
    def _(step):
        cluster, pair = step // pairs, step % pairs
        r = at(cluster, CLUSTER)
        at_q = at(pair, 128)
        at_k = pl.ds(pl.multiple_of(model + pair * 128, 128), 128)
        at_v = pl.ds(pl.multiple_of(2 * model + pair * 128, 128), 128)
        q, k, v = qkv[r, at_q], qkv[r, at_k], qkv[r, at_v]
        p = prob[step]
        dctx = stacked(cgrad[r, at_q])
        dprob = outer(dctx, v)
        dscore = (p * (dprob - jnp.sum(p * dprob, axis=-1, keepdims=True))).astype(BF16)
        dqkv[r, at_q] = (inner(beside(dscore), stacked(k)) * score_scale).astype(BF16)
        dqkv[r, at_k] = (under(dscore, stacked(q)) * score_scale).astype(BF16)
        dqkv[r, at_v] = under(p.astype(BF16), dctx).astype(BF16)

    flip(x)
    for which in range(3):
        product_tiles(dqkv.at[:, pl.ds(which * model, model)], model, square(which), 1)

    for which in range(2):
        @pl.loop(0, model // tile)
        def _(step, which=which):
            value = dqkv[:, pl.ds(pl.multiple_of(2 * which * model + step * tile, tile), tile)]
            sums[:, pl.ds(pl.multiple_of(which * model + step * tile, tile), tile)] = jnp.sum(
                value.astype(F32), axis=0, keepdims=True
            )

    @pl.loop(0, model // tile)
    def _(step):
        cols = at(step, tile)
        in_low[:, cols] = (work[:, cols] + outer(dqkv[...], wqkv[cols, :])).astype(BF16)

    for i in range(6):
        sums[:, pl.ds(2 * model + hidden + i * model, model)] = jnp.sum(accs[i], axis=0, keepdims=True)


def layer(chunk, x, og, valid, wqkv, wo, wu, wd, bqkv, bo, g1, s1, bu, bd, g2, s2):
    rows, model = x.shape
    hidden = wu.shape[1]
    hbm = pl.BlockSpec(memory_space=pl.ANY)
    vmem = pl.BlockSpec(memory_space=pltpu.VMEM)
    part = 2 * model + hidden
    steps = rows // CLUSTER * (model // 128)
    total = 8 * model + hidden
    return pl.pallas_call(
        functools.partial(layer_kernel, chunk),
        out_shape=(
            jax.ShapeDtypeStruct((rows, model), BF16),
            jax.ShapeDtypeStruct((rows, model), BF16),
            jax.ShapeDtypeStruct((2, model // chunk, chunk, part), BF16),
            jax.ShapeDtypeStruct((1, total), F32),
        ),
        in_specs=[vmem] * 15,
        out_specs=(vmem, vmem, hbm, vmem),
        scratch_shapes=[
            pltpu.VMEM((rows, 3 * model), BF16),
            pltpu.VMEM((rows, model), BF16),
            pltpu.VMEM((steps, 2 * CLUSTER, CLUSTER), F32),
            pltpu.VMEM((rows, model), F32),
            pltpu.VMEM((rows, 1), F32),
            pltpu.VMEM((rows, model), BF16),
            pltpu.VMEM((rows, hidden), BF16),
            pltpu.VMEM((rows, hidden), F32),
            pltpu.VMEM((rows, hidden), BF16),
            pltpu.VMEM((rows, model), F32),
            pltpu.VMEM((model, rows), BF16),
            pltpu.VMEM((rows, 3 * model), BF16),
            pltpu.VMEM((rows, model), BF16),
            pltpu.VMEM((rows, model), BF16),
            pltpu.VMEM((2, model // 2 // chunk, chunk, model), BF16),
            pltpu.VMEM((6, 8, model), F32),
            pltpu.SemaphoreType.DMA((2, 2)),
        ],
        compiler_params=pltpu.CompilerParams(vmem_limit_bytes=60 * MEBI),
    )(x, og, valid, wqkv, wo, wu, wd, bqkv, bo, g1, s1, bu, bd, g2, s2)


def exit_kernel(blocks, reduce, *refs):
    if reduce:
        (out_low, in_low, sources, grads, sums, out_home, in_home, grad_sum, sums_sum, *scratch) = refs
        (window, home, wsend, wrecv, csend, crecv, clocal, hsend, hrecv, hlocal, *scratch) = scratch
        (mine_g, from_core, got, gsend, grecv, glocal, rsend, rrecv, vrecv, vsend, vsem) = scratch
    else:
        (out_low, in_low, sources, out_home, in_home, *scratch) = refs
        (window, home, wsend, wrecv, csend, crecv, clocal, hsend, hrecv, hlocal) = scratch
    seq, core = lax.axis_index("seq"), lax.axis_index("head")
    rows, width = window.shape[2], window.shape[3]
    half = rows // 2
    partner = (seq, 1 - core)
    others = near(seq, core, blocks)
    bits = max(blocks.bit_length() - 1, 0)
    greetings = [(partner, None)] + [others[offset] for offset in OFFSETS[1:]]

    def across(bit):
        mask = 1 << bit
        return (seq + mask - 2 * mask * ((seq // mask) % 2), core)

    if reduce:
        greetings += [(across(bit), None) for bit in range(2, bits)]
    greet(greetings)

    mine = pl.ds(pl.multiple_of(core * width, width), width)
    theirs = pl.ds(pl.multiple_of((1 - core) * width, width), width)
    keep = pl.ds(pl.multiple_of(core * half, half), half)
    arrays = (out_low, in_low)
    firsts = []
    for which, array in enumerate(arrays):
        there = remote(
            array.at[:, theirs], window.at[which, 0, keep], csend.at[which], crecv.at[which], partner
        )
        here = pltpu.make_async_copy(array.at[:, mine], window.at[which, 0, keep], clocal.at[which])
        there.start()
        here.start()
        firsts.append((there, here))

    if reduce:
        parts = 2
        span = mine_g.shape[3] // parts
        core_moves = []
        for part in range(parts):
            cols = pl.ds(part * span, span)
            there = remote(
                grads.at[1 - core, :, :, cols], from_core.at[:, :, cols], gsend.at[part], grecv.at[part], partner
            )
            here = pltpu.make_async_copy(grads.at[core, :, :, cols], mine_g.at[0, :, :, cols], glocal.at[part])
            there.start()
            here.start()
            core_moves.append((there, here))

    def spread(which):
        for offset in OFFSETS[1:]:
            device, valid = others[offset]
            slot = SLOT[-offset]
            pl.when(valid)(
                remote(
                    window.at[which, 0], window.at[which, slot], wsend.at[which, slot], wrecv.at[which, slot], device
                ).start
            )

    for which in range(2):
        there, here = firsts[which]
        there.wait()
        here.wait()
        spread(which)

    def reduce_start(part, level):
        cols = pl.ds(part * span, span)
        order = orders[part]
        bit = order[level]
        own = (seq // (1 << bit)) % 2
        left = sorted(set(range(bits)) - set(order[:level]))
        low = 1 << left.index(bit)
        high = (1 << len(left)) // (2 * low)
        outs = []
        for top in range(high):
            src = mine_g.at[level % 2, pl.ds(pl.multiple_of((top * 2 + 1 - own) * low, low), low), :, cols]
            dst = got.at[pl.ds(base[level] + top * low, low), :, cols]
            outs.append(remote(src, dst, rsend.at[part, level, top], rrecv.at[part, level, top], across(bit)))
        return outs, own, low, high, cols

    def reduce_finish(part, level, state):
        outs, own, low, high, cols = state
        for copy in outs:
            copy.wait()
        for top in range(high):
            @pl.loop(0, low)
            def _(inside):
                held = mine_g[level % 2, (top * 2 + own) * low + inside, :, cols].astype(F32)
                other = got[base[level] + top * low + inside, :, cols].astype(F32)
                value = held + other
                if level == bits - 1:
                    grad_sum[:, cols] = value
                else:
                    mine_g[(level + 1) % 2, top * low + inside, :, cols] = value.astype(BF16)

    def pick(which):
        tile = 256
        for offset in OFFSETS:
            slot = SLOT[offset]

            def add(offset=offset, slot=slot):
                if offset != 0:
                    device, _ = others[offset]
                    remote(
                        window.at[which, 0],
                        window.at[which, slot],
                        wsend.at[which, slot],
                        wrecv.at[which, slot],
                        device,
                    ).wait_recv()

                @pl.loop(0, rows // tile)
                def _(step):
                    at = pl.ds(pl.multiple_of(step * tile, tile), tile)
                    places = lax.broadcasted_iota(jnp.int32, (tile, rows), 0) + (step * tile + seq * rows)
                    chosen = jnp.where(sources[slot] == places, 1.0, 0.0).astype(BF16)
                    part = inner(chosen, window[which, slot]).astype(BF16)
                    if offset == 0:
                        home[which, at, :] = part
                    else:
                        home[which, at, :] += part

            if offset == 0:
                add()
            else:
                pl.when(others[offset][1])(add)
        target = (out_home, in_home)[which]
        there = remote(home.at[which], target.at[:, mine], hsend.at[which], hrecv.at[which], partner)
        here = pltpu.make_async_copy(home.at[which], target.at[:, mine], hlocal.at[which])
        there.start()
        here.start()
        return there, here

    lasts = []
    if not reduce:
        lasts = [pick(0), pick(1)]
    else:
        orders = ([0, 1] + list(range(bits - 1, 1, -1)), [1, 0] + list(range(bits - 1, 1, -1)))
        base, count = [], 0
        for level in range(bits):
            base.append(count)
            count += blocks >> (level + 1)

        def sum_level(level):
            device = partner if level == 0 else across(level - 1)
            return remote(vsend.at[level], vrecv.at[level], vsem.at[0, level], vsem.at[1, level], device)

        def sum_start(level):
            if level == 0:
                vsend[0] = sums[...]
            sum_level(level).start()

        def sum_finish(level):
            sum_level(level).wait()
            value = vsend[level] + vrecv[level]
            if level == bits:
                sums_sum[...] = value
            else:
                vsend[level + 1] = value

        sum_start(0)
        states = [None] * parts
        for part in range(parts):
            there, here = core_moves[part]
            there.wait()
            here.wait()
            cols = pl.ds(part * span, span)

            @pl.loop(0, blocks)
            def _(inside):
                value = mine_g[0, inside, :, cols].astype(F32) + from_core[inside, :, cols].astype(F32)
                mine_g[0, inside, :, cols] = value.astype(BF16)

            states[part] = reduce_start(part, 0)
            for copy in states[part][0]:
                copy.start()
        sum_finish(0)
        sum_start(1)
        lasts.append(pick(0))
        for level in range(bits):
            for part in range(parts):
                reduce_finish(part, level, states[part])
                if level + 1 < bits:
                    states[part] = reduce_start(part, level + 1)
                    for copy in states[part][0]:
                        copy.start()
            sum_finish(level + 1)
            if level + 1 < bits:
                sum_start(level + 2)
            if level == 1:
                lasts.append(pick(1))
        if bits < 2:
            lasts.append(pick(1))

    for offset in OFFSETS[1:]:
        device, valid = others[offset]
        slot = SLOT[-offset]

        def finish(device=device, slot=slot):
            for which in range(2):
                remote(
                    window.at[which, 0], window.at[which, slot], wsend.at[which, slot], wrecv.at[which, slot], device
                ).wait_send()

        pl.when(valid)(finish)
    for there, here in lasts:
        there.wait()
        here.wait()


def leave(mesh, reduce, out_low, in_low, sources, grads, sums):
    half, model = out_low.shape
    rows, width = 2 * half, model // 2
    blocks = mesh.shape["seq"]
    slots = len(OFFSETS)
    hbm = pl.BlockSpec(memory_space=pl.ANY)
    vmem = pl.BlockSpec(memory_space=pltpu.VMEM)
    dma = pltpu.SemaphoreType.DMA
    out_shape = [jax.ShapeDtypeStruct((rows, model), BF16)] * 2
    out_specs = [hbm, hbm]
    in_specs = [hbm, hbm, vmem]
    args = [out_low, in_low, sources]
    scratch = [
        pltpu.VMEM((2, slots, rows, width), BF16),
        pltpu.VMEM((2, rows, width), BF16),
        dma((2, slots)),
        dma((2, slots)),
        dma((2,)),
        dma((2,)),
        dma((2,)),
        dma((2,)),
        dma((2,)),
        dma((2,)),
    ]
    if reduce:
        _, chunks, chunk, span = grads.shape
        bits = blocks.bit_length() - 1
        args += [grads, sums]
        in_specs += [hbm, vmem]
        out_shape += [jax.ShapeDtypeStruct((chunk, span), F32), jax.ShapeDtypeStruct(sums.shape, F32)]
        out_specs += [vmem, vmem]
        scratch += [
            pltpu.VMEM((2, blocks, chunk, span), BF16),
            pltpu.VMEM((blocks, chunk, span), BF16),
            pltpu.VMEM((blocks, chunk, span), BF16),
            dma((2,)),
            dma((2,)),
            dma((2,)),
            dma((2, bits, blocks // 2)),
            dma((2, bits, blocks // 2)),
            pltpu.VMEM((bits + 1,) + sums.shape, F32),
            pltpu.VMEM((bits + 1,) + sums.shape, F32),
            dma((2, bits + 1)),
        ]
    return pl.pallas_call(
        functools.partial(exit_kernel, blocks, reduce),
        out_shape=tuple(out_shape),
        in_specs=in_specs,
        out_specs=tuple(out_specs),
        scratch_shapes=scratch,
        compiler_params=pltpu.CompilerParams(
            collective_id=1, has_side_effects=True, vmem_limit_bytes=60 * MEBI
        ),
    )(*args)


FROM_X, FROM_Y, FROM_Z, FROM_LAST, RELAY = range(5)
OWN = -1
EXCHANGES = 4
CHUNKS = 4
GROUPS = 3
PARTS = 3
BITS = 4


def whole_kernel(
    blocks,
    tokens,
    out_grad,
    doc_lengths,
    cluster_perm,
    wq,
    wk,
    wv,
    wo_half,
    wu_half,
    wd_half,
    bq,
    bv,
    bu_half,
    bo_in,
    g1_in,
    s1_in,
    bd_in,
    g2_in,
    s2_in,
    out_home,
    in_home,
    grad_sum,
    sums_sum,
    win,
    wqkv,
    wo,
    wu,
    wd,
    bqkv,
    bu,
    stage,
    picked,
    block,
    source,
    sources,
    rel,
    valid,
    vectors,
    x,
    og,
    qkv,
    ctx,
    prob,
    hat1,
    inv12,
    low1,
    act,
    slope,
    work,
    flipped,
    flipped_x,
    in_low,
    accs,
    mine_g,
    from_core,
    give,
    got0,
    got1,
    got2,
    got3,
    vsend,
    vrecv,
    wsend,
    wrecv,
    wlocal,
    xsend,
    xrecv,
    ssend,
    srecv,
    ssem,
    psend,
    precv,
    plocal,
    hsend,
    hrecv,
    hlocal,
    gsend,
    grecv,
    rsend,
    rrecv,
    vsem,
    osem,
    credit,
):
    seq, core = lax.axis_index("seq"), lax.axis_index("head")
    px, py = seq % 2, (seq // 2) % 2
    rows, width = tokens.shape[0], picked.shape[2]
    half, model = x.shape
    hidden = wu.shape[1]
    clusters = half // CLUSTER
    pairs = model // 128
    part_rows = rows // CHUNKS
    tile = 256
    band = 64

    low2 = og

    partner = (seq, 1 - core)
    x_next = seq + 1 - 2 * px
    y_next = seq + 2 - 4 * py
    z_to = seq + 4 - 8 * py
    z_from = seq - 4 + 8 * py
    to_ok = (z_to >= 0) & (z_to < blocks)
    from_ok = (z_from >= 0) & (z_from < blocks)
    level_chip = px == py
    off_chip = px != py
    last_next = x_next + core * (y_next - x_next)
    relay_send = (core == 1) & off_chip & from_ok
    relay_recv = (core == 1) & off_chip & to_ok
    later_ok = off_chip & (((core == 0) & from_ok) | ((core == 1) & to_ok))
    last_ok = off_chip | from_ok
    offsets = {
        OWN: 0,
        FROM_X: 1 - 2 * px,
        FROM_Y: 2 - 4 * py,
        FROM_Z: 4 * py - 2,
        FROM_LAST: 2 * px - 1,
    }
    arrived = {OWN: None, FROM_X: None, FROM_Y: None, FROM_Z: from_ok, FROM_LAST: last_ok}
    others = near(seq, core, blocks)

    def across(bit):
        mask = 1 << bit
        return (seq + mask - 2 * mask * ((seq // mask) % 2), core)

    greetings = [(partner, None), ((x_next, core), None), ((y_next, core), None)]
    greetings += [((z_to, core), to_ok), ((z_from, core), from_ok)]
    greetings += [others[offset] for offset in OFFSETS[1:]]
    greetings += [(across(bit), None) for bit in range(3, BITS)]
    arrivals = greet_start(greetings)

    def at(step, size):
        return pl.ds(pl.multiple_of(step * size, size), size)

    def when(condition, action):
        if condition is None:
            action()
        else:
            pl.when(condition)(action)

    mine = at(core, width)
    theirs = at(1 - core, width)
    keep = at(core, half)
    other_rows = at(1 - core, half)

    def piece(chunk):
        return pl.ds(chunk * part_rows, part_rows)

    def own_rows(e, chunk):
        if e < 2:
            return (tokens, out_grad)[e].at[piece(chunk), mine]
        return block.at[e - 2, piece(chunk)]

    def hop(e, kind, chunk, src, there):
        return remote(
            src,
            win.at[e, kind, piece(chunk)],
            xsend.at[e, kind, chunk],
            xrecv.at[e, kind, chunk],
            (there, core),
        )

    def held(e, kind, chunk):
        return win.at[e, kind, piece(chunk)]

    def hop_x(e, chunk):
        return hop(e, FROM_X, chunk, own_rows(e, chunk), x_next)

    def hop_y(e, chunk):
        return hop(e, FROM_Y, chunk, own_rows(e, chunk), y_next)

    def hop_z(e, chunk):
        return hop(e, FROM_Z, chunk, held(e, FROM_Y, chunk), z_to)

    def hop_relay(e, chunk):
        return hop(e, RELAY, chunk, held(e, FROM_X, chunk), z_from)

    def hop_last_early(e, chunk):
        return hop(e, FROM_LAST, chunk, held(e, 1 - core, chunk), last_next)

    def hop_last_late(e, chunk):
        return hop(e, FROM_LAST, chunk, held(e, 2 + 2 * core, chunk), last_next)

    def send_own(e):
        for chunk in range(CHUNKS):
            hop_y(e, chunk).start()
            hop_x(e, chunk).start()

    def first_hop(e, chunk):
        hop_y(e, chunk).wait_recv()
        pl.when(to_ok)(hop_z(e, chunk).start)
        hop_x(e, chunk).wait_recv()
        pl.when(level_chip)(hop_last_early(e, chunk).start)
        pl.when(relay_send)(hop_relay(e, chunk).start)

    def second_hop(e, chunk):
        pl.when(from_ok)(hop_z(e, chunk).wait_recv)
        pl.when(relay_recv)(hop_relay(e, chunk).wait_recv)
        pl.when(later_ok)(hop_last_late(e, chunk).start)

    def last_hop(e, chunk):
        pl.when(last_ok)(hop_last_early(e, chunk).wait_recv)

    def all_sent(e):
        for chunk in range(CHUNKS):
            hop_x(e, chunk).wait_send()
            hop_y(e, chunk).wait_send()
            pl.when(to_ok)(hop_z(e, chunk).wait_send)
            pl.when(relay_send)(hop_relay(e, chunk).wait_send)
            pl.when(level_chip)(hop_last_early(e, chunk).wait_send)
            pl.when(later_ok)(hop_last_late(e, chunk).wait_send)

    def span_of(side):
        return pl.ds(side * half, half)

    def pick(e, units, fresh=False):
        which = e % 2
        moves = {}
        for index, (kind, side) in enumerate(units):
            if kind == OWN and e >= 2:
                continue
            if kind == OWN:
                src = (tokens, out_grad)[e].at[span_of(side), mine]
            else:
                src = win.at[e, kind, span_of(side)]
            moves[index] = pltpu.make_async_copy(src, stage.at[index], ssem.at[index])
            when(arrived[kind], moves[index].start)
        for index, (kind, side) in enumerate(units):

            def add(index=index, kind=kind, side=side):
                if index in moves:
                    moves[index].wait()
                offset = offsets[kind]
                if e < 2:
                    wanted = rel[:, pl.ds(0, 1)] - (offset * rows + side * half)
                    places = lax.broadcasted_iota(jnp.int32, (rows, half), 1)
                else:
                    wanted = sources[offset + 2, :, span_of(side)] - seq * rows
                    places = lax.broadcasted_iota(jnp.int32, (rows, half), 0)
                chosen = jnp.where(places == wanted, 1.0, 0.0).astype(BF16)
                block_rows = stage[index] if index in moves else block[e - 2, span_of(side), :]
                value = inner(chosen, block_rows).astype(BF16)
                if fresh and index == 0:
                    picked[which] = value
                else:
                    picked[which] += value

            when(arrived[kind], add)

    def deliver(e):
        target = (x, og)[e]
        there = remote(picked.at[e, other_rows], target.at[:, mine], psend.at[e], precv.at[e], partner)
        here = pltpu.make_async_copy(picked.at[e, keep], target.at[:, mine], plocal.at[e])
        return there, here

    def collect(e):
        array = in_low
        there = remote(array.at[:, theirs], block.at[e - 2, keep], psend.at[e], precv.at[e], partner)
        here = pltpu.make_async_copy(array.at[:, mine], block.at[e - 2, keep], plocal.at[e])
        return there, here

    def bring_home(e):
        target = (out_home, in_home)[e - 2]
        there = remote(picked.at[e - 2], target.at[:, mine], hsend.at[e - 2], hrecv.at[e - 2], partner)
        here = pltpu.make_async_copy(picked.at[e - 2], target.at[:, mine], hlocal.at[e - 2])
        return there, here

    def begin(pair):
        for copy in pair:
            copy.start()

    def end(pair):
        for copy in pair:
            copy.wait()

    orders = ((0, 2, 1, 3), (1, 2, 0, 3), (2, 1, 0, 3))
    gots = (got0, got1, got2, got3)
    span = mine_g.shape[-1]
    part_span = span // PARTS

    def part_cols(part):
        return pl.ds(part * part_span, part_span)

    def own_bit(bit):
        return (seq // (1 << bit)) % 2

    def halving(group, part, level):
        order = orders[part]
        index = []
        for bit in (3, 2, 1, 0):
            if bit in order[:level]:
                index.append(own_bit(bit))
            elif bit == order[level]:
                index.append(1 - own_bit(bit))
            else:
                index.append(slice(None))
        src = mine_g.at[(group, *index, slice(None), part_cols(part))]
        dst = gots[level].at[group, part]
        return remote(
            src, dst, rsend.at[group, part, level], rrecv.at[group, part, level], across(order[level])
        )

    def halving_end(group, part, level):
        halving(group, part, level).wait()
        order = orders[part]
        left = [bit for bit in (3, 2, 1, 0) if bit not in order[: level + 1]]
        cols = part_cols(part)
        finals = slope.at[pl.ds(group * chunk_rows, chunk_rows), :]

        @pl.loop(0, 1 << len(left))
        def _(step):
            digits = {bit: (step // (1 << (len(left) - 1 - i))) % 2 for i, bit in enumerate(left)}
            place = [digits[bit] if bit in digits else own_bit(bit) for bit in (3, 2, 1, 0)]
            value = mine_g[(group, *place, slice(None), cols)].astype(F32)
            other = gots[level][(group, part, *[digits[bit] for bit in left])]
            value = value + other.astype(F32)
            if level == BITS - 1:
                finals[:, cols] = value
            else:
                mine_g[(group, *place, slice(None), cols)] = value.astype(BF16)

    def advance(group, level):
        for part in range(PARTS):
            halving_end(group, part, level)
            if level + 1 < BITS:
                halving(group, part, level + 1).start()
            else:
                write_out(group, part).start()

    def write_out(group, part):
        return pltpu.make_async_copy(
            slope.at[pl.ds(group * chunk_rows, chunk_rows), part_cols(part)],
            grad_sum.at[:, pl.ds(group * span + part * part_span, part_span)],
            osem.at[group, part],
        )

    def core_move(group, part):
        cols = part_cols(part)
        return remote(
            give.at[:, :, :, :, :, cols],
            from_core.at[group % 2, :, :, :, :, :, cols],
            gsend.at[group, part],
            grecv.at[group, part],
            partner,
        )

    chunk_rows = give.shape[4]
    m_rows = model // 2

    def group_products(group, columns, between=lambda: None):
        if group == 2:
            pl.semaphore_wait(credit, 1)
        for side in (0, 1):
            if side == 1:
                between()
            for part in range(PARTS):
                if side == 0 and group > 0:
                    core_move(group - 1, part).wait_send()
                if side == 1:
                    core_move(group, part).wait_recv()
                place = 0
                for left, right, start, size in columns(part, (1 - core, core)[side]):
                    cols = pl.ds(part * part_span + place, size)
                    place += size

                    @pl.loop(0, 2)
                    def _(m, left=left, right=right, start=start, size=size, cols=cols):
                        value = inner(left[at(m, m_rows), :], right[:, pl.ds(start, size)])
                        value = value.reshape(2, 2, 2, chunk_rows, size)
                        if side == 0:
                            give[m, :, :, :, :, cols] = value.astype(BF16)
                        else:
                            value = value + from_core[group % 2, m, :, :, :, :, cols].astype(F32)
                            mine_g[group, m, :, :, :, :, cols] = value.astype(BF16)

                if side == 0:
                    core_move(group, part).start()
                else:
                    halving(group, part, 0).start()
        if group == 0:
            pl.semaphore_signal(credit, inc=1, device_id=partner, device_id_type=MESH)

    part_out = 2 * model + hidden

    def sum_move(level):
        device = partner if level == 0 else across(level - 1)
        return remote(vsend.at[level], vrecv.at[level], vsem.at[0, level], vsem.at[1, level], device)

    def sum_next(level):
        sum_move(level).wait()
        value = vsend[level] + vrecv[level]
        if level == BITS:
            sums_sum[...] = value
        else:
            vsend[level + 1] = value
            sum_move(level + 1).start()

    wide, deep = wq.shape[1], wd_half.shape[0]
    pieces = []
    for i, array in enumerate((wq, wk, wv)):
        pieces.append((array, wqkv.at[:, pl.ds(pl.multiple_of(i * model + core * wide, wide), wide)]))
    pieces.append((wo_half, wo.at[at(core, wide), :]))
    pieces.append((wu_half, wu.at[:, at(core, deep)]))
    pieces.append((wd_half, wd.at[at(core, deep), :]))
    heres = [pltpu.make_async_copy(array, place, wlocal.at[i]) for i, (array, place) in enumerate(pieces)]
    for copy in heres:
        copy.start()

    shape = cluster_perm.shape
    positions = lax.broadcasted_iota(jnp.int32, shape, 0) * CLUSTER + lax.broadcasted_iota(jnp.int32, shape, 1)
    positions = positions + seq * rows
    doc_start = jnp.zeros(shape, jnp.int32)
    doc_length = jnp.zeros(shape, jnp.int32)
    start = 0
    for i in range(doc_lengths.shape[0]):
        length = doc_lengths[i]
        inside = positions >= start
        doc_start = jnp.where(inside, start, doc_start)
        doc_length = jnp.where(inside, length, doc_length)
        start = start + (length + CLUSTER - 1) // CLUSTER * CLUSTER
    valid[...] = jnp.where(cluster_perm[...] < doc_length, 1.0, 0.0)
    from_row = doc_start + cluster_perm[...]
    for i in range(shape[0]):
        line = from_row[i : i + 1, :]
        source[:, pl.ds(i * CLUSTER, CLUSTER)] = line
        rel[pl.ds(i * CLUSTER, CLUSTER), :] = jnp.broadcast_to(line - seq * rows, (CLUSTER, CLUSTER)).T
    sources[2] = source[...]
    for i, vector in enumerate((bo_in, g1_in, s1_in, bd_in, g2_in, s2_in)):
        vectors[i] = vector[...].reshape(1, model)
    bo, g1, s1, bd, g2, s2 = (vectors.at[i] for i in range(6))
    at_v = pl.ds(pl.multiple_of(2 * model + core * wide, wide), wide)
    bqkv[:, at(core, wide)] = bq[...].reshape(1, wide)
    bqkv[:, pl.ds(model, model)] = jnp.zeros((1, model), F32)
    bqkv[:, at_v] = bv[...].reshape(1, wide)
    bu[:, at(core, deep)] = bu_half[...].reshape(1, deep)
    pl.semaphore_wait(pltpu.get_barrier_semaphore(), arrivals)

    send_own(0)
    weights = []
    for place in (bqkv.at[:, at(core, wide)], bqkv.at[:, at_v], bu.at[:, at(core, deep)]):
        pieces.append((place, place))
    for i, (array, place) in enumerate(pieces):
        weights.append(remote(array, place, wsend.at[i], wrecv.at[i], partner))
        weights[i].start()
    tinies = []
    for offset in OFFSETS[1:]:
        device, there_ok = others[offset]
        out = remote(source, sources.at[2 - offset], ssend.at[2 - offset], srecv.at[2 - offset], device)
        back = remote(source, sources.at[2 + offset], ssend.at[2 + offset], srecv.at[2 + offset], device)
        pl.when(there_ok)(out.start)
        tinies.append((there_ok, out, back))

    pick(0, [(OWN, 0), (OWN, 1)], fresh=True)
    pick(1, [(OWN, 0), (OWN, 1)], fresh=True)
    first_hop(0, 0)
    first_hop(0, 1)
    second_hop(0, 0)
    pick(0, [(FROM_X, 0), (FROM_Y, 0)])
    first_hop(0, 2)
    second_hop(0, 1)
    first_hop(0, 3)
    second_hop(0, 2)
    pick(0, [(FROM_X, 1), (FROM_Y, 1), (FROM_Z, 0)])
    second_hop(0, 3)
    send_own(1)
    last_hop(0, 0)
    last_hop(0, 1)
    pick(0, [(FROM_Z, 1), (FROM_LAST, 0)])
    last_hop(0, 2)
    last_hop(0, 3)
    pick(0, [(FROM_LAST, 1)])
    begin(deliver(0))
    for copy in heres + weights:
        copy.wait()
    end(deliver(0))

    lanes = lax.broadcasted_iota(jnp.int32, (CLUSTER, 128), 1)
    first_f = jnp.where(lanes < HEAD_DIM, 1.0, 0.0)
    first = first_f.astype(BF16)
    second = (1.0 - first_f).astype(BF16)

    def stacked(pair):
        return jnp.concatenate([pair * first, pair * second], axis=0)

    def beside(tall):
        return jnp.concatenate([tall[:CLUSTER], tall[CLUSTER:]], axis=1)

    @pl.loop(0, 3 * model // tile)
    def _(step):
        cols = at(step, tile)
        qkv[:, cols] = (inner(x[...], wqkv[:, cols]) + bqkv[:, cols]).astype(BF16)

    first_hop(1, 0)

    @pl.loop(0, clusters)
    def _(cluster):
        r = at(cluster, CLUSTER)
        for pair in range(pairs):
            q = qkv[r, pl.ds(pair * 128, 128)]
            k = qkv[r, pl.ds(model + pair * 128, 128)]
            v = qkv[r, pl.ds(2 * model + pair * 128, 128)]
            scores = outer(stacked(q), k) * score_scale
            scores = jnp.where(valid[pl.ds(core * clusters + cluster, 1), :] > 0.5, scores, masked_score)
            top = jnp.max(scores, axis=-1, keepdims=True)
            weight = jnp.exp(scores - top)
            p = weight * (1.0 / jnp.sum(weight, axis=-1, keepdims=True))
            prob[cluster * pairs + pair] = p
            ctx[r, pl.ds(pair * 128, 128)] = inner(beside(p.astype(BF16)), stacked(v)).astype(BF16)

    first_hop(1, 1)

    @pl.loop(0, model // tile)
    def _(step):
        cols = at(step, tile)
        hat1[:, cols] = inner(ctx[...], wo[:, cols]) + x[:, cols].astype(F32) + bo[:, cols]

    @pl.loop(0, half // band)
    def _(step):
        r = at(step, band)
        h = hat1[r, :]
        centered = h - jnp.mean(h, axis=-1, keepdims=True)
        inv = lax.rsqrt(jnp.mean(centered * centered, axis=-1, keepdims=True) + norm_eps)
        hat = centered * inv
        hat1[r, :] = hat
        inv12[r, pl.ds(0, 1)] = inv
        low1[r, :] = (hat * g1[...] + s1[...]).astype(BF16)

    first_hop(1, 2)
    second_hop(1, 0)

    @pl.loop(0, hidden // tile)
    def _(step):
        cols = at(step, tile)
        pre = inner(low1[...], wu[:, cols]) + bu[:, cols]
        cdf = 0.5 * (1.0 + lax.erf(pre * root_half))
        act[:, cols] = (pre * cdf).astype(BF16)
        slope[:, cols] = cdf + pre * jnp.exp(-0.5 * pre * pre) * inv_root_tau

    first_hop(1, 3)
    second_hop(1, 1)

    @pl.loop(0, model // tile)
    def _(step):
        cols = at(step, tile)
        norm = hat1[:, cols] * g1[:, cols] + s1[:, cols]
        work[:, cols] = inner(act[...], wd[:, cols]) + norm + bd[:, cols]

    second_hop(1, 2)

    @pl.loop(0, half // band)
    def _(step):
        r = at(step, band)
        h = work[r, :]
        centered = h - jnp.mean(h, axis=-1, keepdims=True)
        inv = lax.rsqrt(jnp.mean(centered * centered, axis=-1, keepdims=True) + norm_eps)
        hat = centered * inv
        work[r, :] = hat
        inv12[r, pl.ds(1, 1)] = inv
        in_low[r, :] = (hat * g2[...] + s2[...]).astype(BF16)

    begin(collect(2))
    second_hop(1, 3)
    pick(1, [(FROM_X, 0), (FROM_Y, 0), (FROM_X, 1), (FROM_Y, 1)])
    end(collect(2))
    for chunk in range(CHUNKS):
        last_hop(1, chunk)
    send_own(2)
    pick(1, [(FROM_Z, 0), (FROM_Z, 1), (FROM_LAST, 0), (FROM_LAST, 1)])
    begin(deliver(1))
    accs[...] = jnp.zeros_like(accs)
    end(deliver(1))

    @pl.loop(0, half // band)
    def _(step):
        r = at(step, band)
        hat = work[r, :]
        grad = og[r, :].astype(F32)
        accs[4] += fold_rows(grad * hat)
        accs[5] += fold_rows(grad)
        scaled = grad * g2[...]
        back = inv12[r, pl.ds(1, 1)] * (
            scaled
            - jnp.mean(scaled, axis=-1, keepdims=True)
            - hat * jnp.mean(scaled * hat, axis=-1, keepdims=True)
        )
        accs[3] += fold_rows(back)
        work[r, :] = back
        low2[r, :] = back.astype(BF16)

    def flip(source_rows, target=flipped):
        @pl.loop(0, model // 128)
        def _(step):
            target[at(step, 128), :] = source_rows[:, at(step, 128)].T

    def long_columns(part, side):
        start = pl.multiple_of(side * span + part * part_span, part_span)
        return [(flipped, act, start, part_span)]

    first_hop(2, 0)
    flip(low2)
    group_products(0, long_columns, lambda: first_hop(2, 1))
    first_hop(2, 2)
    second_hop(2, 0)

    @pl.loop(0, hidden // tile)
    def _(step):
        cols = at(step, tile)
        back = outer(low2[...], wd[cols, :]) * slope[:, cols]
        back = back.astype(BF16)
        act[:, cols] = back
        vsend[0, :, pl.ds(pl.multiple_of(2 * model + step * tile, tile), tile)] = jnp.sum(
            back.astype(F32), axis=0, keepdims=True
        )

    first_hop(2, 3)
    second_hop(2, 1)
    flip(low1)
    group_products(1, long_columns, lambda: second_hop(2, 2))

    @pl.loop(0, model // tile)
    def _(step):
        cols = at(step, tile)
        work[:, cols] += outer(act[...], wu[cols, :])

    @pl.loop(0, half // band)
    def _(step):
        r = at(step, band)
        grad = work[r, :]
        hat = hat1[r, :]
        accs[1] += fold_rows(grad * hat)
        accs[2] += fold_rows(grad)
        scaled = grad * g1[...]
        back = inv12[r, pl.ds(0, 1)] * (
            scaled
            - jnp.mean(scaled, axis=-1, keepdims=True)
            - hat * jnp.mean(scaled * hat, axis=-1, keepdims=True)
        )
        accs[0] += fold_rows(back)
        work[r, :] = back
        low2[r, :] = back.astype(BF16)

    @pl.loop(0, model // tile)
    def _(step):
        cols = at(step, tile)
        low1[:, cols] = outer(low2[...], wo[cols, :]).astype(BF16)

    def attention_backward(cluster):
        r = at(cluster, CLUSTER)
        for pair in range(pairs):
            at_q = pl.ds(pair * 128, 128)
            at_k = pl.ds(model + pair * 128, 128)
            at_v = pl.ds(2 * model + pair * 128, 128)
            q, k, v = qkv[r, at_q], qkv[r, at_k], qkv[r, at_v]
            p = prob[cluster * pairs + pair]
            dctx = stacked(low1[r, at_q])
            dprob = outer(dctx, v)
            dscore = (p * (dprob - jnp.sum(p * dprob, axis=-1, keepdims=True))).astype(BF16)
            qkv[r, at_q] = (inner(beside(dscore), stacked(k)) * score_scale).astype(BF16)
            qkv[r, at_k] = (under(dscore, stacked(q)) * score_scale).astype(BF16)
            qkv[r, at_v] = under(p.astype(BF16), dctx).astype(BF16)

    second_hop(2, 3)
    advance(0, 0)
    pl.loop(0, clusters // 2)(attention_backward)
    pl.loop(clusters // 2, clusters)(attention_backward)
    advance(0, 1)

    @pl.loop(0, model // tile)
    def _(step):
        cols = at(step, tile)
        in_low[:, cols] = (work[:, cols] + outer(qkv[...], wqkv[cols, :])).astype(BF16)

    begin(collect(3))
    end(collect(3))
    send_own(3)

    for which in range(2):
        @pl.loop(0, model // tile)
        def _(step, which=which):
            value = qkv[:, pl.ds(pl.multiple_of(2 * which * model + step * tile, tile), tile)]
            vsend[0, :, pl.ds(pl.multiple_of(which * model + step * tile, tile), tile)] = jnp.sum(
                value.astype(F32), axis=0, keepdims=True
            )

    for i in range(6):
        vsend[0, :, pl.ds(part_out + i * model, model)] = jnp.sum(accs[i], axis=0, keepdims=True)
    sum_move(0).start()

    flip(low2)
    flip(x, flipped_x)

    def square_columns(part, side):
        def cut(left, right, base, start, size):
            return (left, right, pl.multiple_of(base + side * width + start, 128), size)

        third = width // 3
        if part == 0:
            return [cut(flipped, ctx, 0, 0, 3 * third), cut(flipped_x, qkv, 0, 0, third)]
        if part == 1:
            return [
                cut(flipped_x, qkv, 0, third, 2 * third),
                cut(flipped_x, qkv, model, 0, 2 * third),
            ]
        return [
            cut(flipped_x, qkv, model, 2 * third, third),
            cut(flipped_x, qkv, 2 * model, 0, 3 * third),
        ]

    def hops():
        first_hop(3, 0)

    group_products(2, square_columns, hops)
    first_hop(3, 1)
    advance(1, 0)
    advance(0, 2)
    second_hop(3, 0)
    advance(1, 1)
    first_hop(3, 2)
    second_hop(3, 1)
    advance(0, 3)
    sum_next(0)
    for there_ok, out, back in tinies:

        def finish(out=out, back=back):
            out.wait_send()
            back.wait_recv()

        pl.when(there_ok)(finish)
    for chunk in range(CHUNKS):
        last_hop(2, chunk)
    first_hop(3, 3)
    second_hop(3, 2)
    pick(2, [(OWN, 0), (OWN, 1)], fresh=True)
    sum_next(1)
    second_hop(3, 3)
    advance(2, 0)
    pick(2, [(FROM_X, 0), (FROM_Y, 0), (FROM_X, 1), (FROM_Y, 1)])
    sum_next(2)
    advance(2, 1)
    advance(1, 2)
    pick(2, [(FROM_Z, 0), (FROM_Z, 1), (FROM_LAST, 0), (FROM_LAST, 1)])
    begin(bring_home(2))
    pick(3, [(OWN, 0), (OWN, 1)], fresh=True)
    sum_next(3)
    pick(3, [(FROM_X, 0), (FROM_Y, 0), (FROM_X, 1), (FROM_Y, 1)])
    advance(2, 2)
    advance(1, 3)
    last_hop(3, 0)
    last_hop(3, 1)
    pick(3, [(FROM_Z, 0), (FROM_Z, 1), (FROM_LAST, 0)])
    sum_next(4)
    last_hop(3, 2)
    last_hop(3, 3)
    pick(3, [(FROM_LAST, 1)])
    begin(bring_home(3))
    advance(2, 3)
    for part in range(PARTS):
        core_move(2, part).wait_send()
    for e in range(EXCHANGES):
        all_sent(e)
    end(bring_home(2))
    end(bring_home(3))
    for group in range(GROUPS):
        for part in range(PARTS):
            write_out(group, part).wait()


def whole(mesh, *args):
    tokens, wu_half = args[0], args[8]
    rows, model = tokens.shape
    half, width = rows // 2, model // 2
    hidden = 2 * wu_half.shape[1]
    blocks = mesh.shape["seq"]
    hbm = pl.BlockSpec(memory_space=pl.ANY)
    vmem = pl.BlockSpec(memory_space=pltpu.VMEM)
    smem = pl.BlockSpec(memory_space=pltpu.SMEM)
    dma = pltpu.SemaphoreType.DMA
    chunk = model // blocks
    span = 4 * width
    part_span = span // PARTS
    steps = half // CLUSTER * (model // 128)
    total = 8 * model + hidden
    cube = (2, 2, 2, 2)
    return pl.pallas_call(
        functools.partial(whole_kernel, blocks),
        out_shape=(
            jax.ShapeDtypeStruct((rows, model), BF16),
            jax.ShapeDtypeStruct((rows, model), BF16),
            jax.ShapeDtypeStruct((chunk, GROUPS * span), F32),
            jax.ShapeDtypeStruct((1, total), F32),
            jax.ShapeDtypeStruct((EXCHANGES, 5, rows, width), BF16),
        ),
        in_specs=[hbm, hbm, smem, vmem] + [hbm] * 6 + [vmem] * 9,
        out_specs=(hbm, hbm, hbm, vmem, hbm),
        scratch_shapes=[
            pltpu.VMEM((model, 3 * model), BF16),
            pltpu.VMEM((model, model), BF16),
            pltpu.VMEM((model, hidden), BF16),
            pltpu.VMEM((hidden, model), BF16),
            pltpu.VMEM((1, 3 * model), F32),
            pltpu.VMEM((1, hidden), F32),
            pltpu.VMEM((4, half, width), BF16),
            pltpu.VMEM((2, rows, width), BF16),
            pltpu.VMEM((2, rows, width), BF16),
            pltpu.VMEM((1, rows), jnp.int32),
            pltpu.VMEM((5, 1, rows), jnp.int32),
            pltpu.VMEM((rows, CLUSTER), jnp.int32),
            pltpu.VMEM((rows // CLUSTER, CLUSTER), F32),
            pltpu.VMEM((6, 1, model), F32),
            pltpu.VMEM((half, model), BF16),
            pltpu.VMEM((half, model), BF16),
            pltpu.VMEM((half, 3 * model), BF16),
            pltpu.VMEM((half, model), BF16),
            pltpu.VMEM((steps, 2 * CLUSTER, CLUSTER), F32),
            pltpu.VMEM((half, model), F32),
            pltpu.VMEM((half, 2), F32),
            pltpu.VMEM((half, model), BF16),
            pltpu.VMEM((half, hidden), BF16),
            pltpu.VMEM((half, hidden), F32),
            pltpu.VMEM((half, model), F32),
            pltpu.VMEM((model, half), BF16),
            pltpu.VMEM((model, half), BF16),
            pltpu.VMEM((half, model), BF16),
            pltpu.VMEM((6, 8, model), F32),
            pltpu.VMEM((GROUPS,) + cube + (chunk, span), BF16),
            pltpu.VMEM((2,) + cube + (chunk, span), BF16),
            pltpu.VMEM(cube + (chunk, span), BF16),
            pltpu.VMEM((GROUPS, PARTS, 2, 2, 2, chunk, part_span), BF16),
            pltpu.VMEM((GROUPS, PARTS, 2, 2, chunk, part_span), BF16),
            pltpu.VMEM((GROUPS, PARTS, 2, chunk, part_span), BF16),
            pltpu.VMEM((GROUPS, PARTS, chunk, part_span), BF16),
            pltpu.VMEM((BITS + 1, 1, total), F32),
            pltpu.VMEM((BITS + 1, 1, total), F32),
            dma((9,)),
            dma((9,)),
            dma((9,)),
            dma((EXCHANGES, 5, CHUNKS)),
            dma((EXCHANGES, 5, CHUNKS)),
            dma((5,)),
            dma((5,)),
            dma((4,)),
            dma((EXCHANGES,)),
            dma((EXCHANGES,)),
            dma((EXCHANGES,)),
            dma((2,)),
            dma((2,)),
            dma((2,)),
            dma((GROUPS, PARTS)),
            dma((GROUPS, PARTS)),
            dma((GROUPS, PARTS, BITS)),
            dma((GROUPS, PARTS, BITS)),
            dma((2, BITS + 1)),
            dma((GROUPS, PARTS)),
            pltpu.SemaphoreType.REGULAR,
        ],
        compiler_params=pltpu.CompilerParams(
            collective_id=2, has_side_effects=True, vmem_limit_bytes=64 * MEBI
        ),
    )(*args)[:4]


def body(
    mesh,
    tokens,
    out_grad,
    doc_lengths,
    cluster_perm,
    query_weight,
    query_bias,
    key_weight,
    value_weight,
    value_bias,
    output_weight,
    output_bias,
    first_gain,
    first_shift,
    up_weight,
    up_bias,
    down_weight,
    down_bias,
    second_gain,
    second_shift,
):
    rows, model = tokens.shape
    half = rows // 2
    hidden = 2 * up_weight.shape[1]
    blocks = mesh.shape["seq"]
    seq, core = lax.axis_index("seq"), lax.axis_index("head")
    positions = seq * rows + jnp.arange(rows, dtype=jnp.int32)
    slot_start, slot_length = doc_lookup(doc_lengths, positions)
    source = slot_start + cluster_perm
    valid = (cluster_perm < slot_length).astype(F32).reshape(2, half // CLUSTER, 1, CLUSTER)
    valid = lax.dynamic_index_in_dim(valid, core, 0, keepdims=False)

    def row(v):
        return v.reshape(1, -1)

    rel = (source - seq * rows).reshape(rows, 1)
    chunk = model // blocks
    part_q, part_h = model // 2, hidden // 2
    order = ("q", "k", "v", "o", "up", "down")
    if blocks == 1 << BITS and chunk % 16 == 0 and hidden == 4 * model:
        order = ("down", "up", "o", "q", "k", "v")
        out_home, in_home, grad_sum, sums = whole(
            mesh,
            tokens,
            out_grad,
            doc_lengths,
            cluster_perm.reshape(rows // CLUSTER, CLUSTER),
            query_weight,
            key_weight,
            value_weight,
            output_weight,
            up_weight,
            down_weight,
            query_bias,
            value_bias,
            up_bias,
            output_bias,
            first_gain,
            first_shift,
            down_bias,
            second_gain,
            second_shift,
        )
    else:
        x, og, sources, wqkv, wo, wu, wd, bqkv, bu = entry(
            mesh,
            tokens,
            out_grad,
            rel,
            row(source),
            query_weight,
            key_weight,
            value_weight,
            output_weight,
            up_weight,
            down_weight,
            row(query_bias),
            row(value_bias),
            row(up_bias),
        )
        no_key = (jnp.arange(3 * model) // model != 1)[None, :]
        bqkv = jnp.where(no_key, bqkv, 0.0)
        reduce = chunk % 16 == 0 and blocks >= 4 and blocks & (blocks - 1) == 0
        out_low, in_low, grads, sums = layer(
            chunk if reduce else 48,
            x,
            og,
            valid,
            wqkv,
            wo,
            wu,
            wd,
            bqkv,
            row(output_bias),
            row(first_gain),
            row(first_shift),
            bu,
            row(down_bias),
            row(second_gain),
            row(second_shift),
        )
        if reduce:
            out_home, in_home, grad_sum, sums = leave(mesh, True, out_low, in_low, sources, grads, sums)
        else:
            out_home, in_home = leave(mesh, False, out_low, in_low, sources, None, None)
            sums = lax.psum(sums, ("seq", "head"))
            grads = grads.reshape(2, model, -1)
            grads = lax.psum_scatter(grads.astype(F32), "head", scatter_dimension=0, tiled=True)[0]
            grad_sum = lax.psum_scatter(grads, "seq", scatter_dimension=0, tiled=True)
    grad_of, place = {}, 0
    for name in order:
        size = part_h if name in ("up", "down") else part_q
        grad_of[name] = grad_sum[:, place : place + size]
        place += size
    sums = sums[0]

    def mine(start, size):
        return lax.dynamic_slice(sums, (start + core * size,), (size,))

    def block(index):
        return lax.dynamic_slice(sums, (2 * model + hidden + index * model + seq * chunk,), (chunk,))

    return (
        out_home.astype(F32),
        in_home.astype(F32),
        grad_of["q"],
        mine(0, part_q),
        grad_of["k"],
        grad_of["v"],
        mine(model, part_q),
        grad_of["o"].T,
        block(0),
        block(1),
        block(2),
        grad_of["up"],
        mine(2 * model, part_h),
        grad_of["down"].T,
        block(3),
        block(4),
        block(5),
    )


def solution(mesh):
    placed = (
        P("seq", None),
        P("seq", None),
        P(),
        P("seq"),
        P(None, "head"),
        P("head"),
        P(None, "head"),
        P(None, "head"),
        P("head"),
        P("head", None),
        P(),
        P(),
        P(),
        P(None, "head"),
        P("head"),
        P("head", None),
        P(),
        P(),
        P(),
    )
    return jax.shard_map(
        functools.partial(body, mesh),
        mesh=mesh,
        in_specs=placed,
        out_specs=(
            P("seq", None),
            P("seq", None),
            P("seq", "head"),
            P("head"),
            P("seq", "head"),
            P("seq", "head"),
            P("head"),
            P("head", "seq"),
            P("seq"),
            P("seq"),
            P("seq"),
            P("seq", "head"),
            P("head"),
            P("head", "seq"),
            P("seq"),
            P("seq"),
            P("seq"),
        ),
        check_vma=False,
    )
```
